256 devices in a mesh: seq: 32 (over z, y), head: 8 (over x, core).
Axes of the slice: x: 4, y: 4, z: 8, core: 2. Of those that a mesh axis runs over, the one named last changes fastest.
Arguments:
- cluster_id: int32 [32768], P(('seq', 'head')), may hold values from 0 to 255, as said below
- queries: bfloat16 [32768, 4096], P('seq', 'head'), may hold values from -6 to 6
- key_vectors: bfloat16 [32768, 4096], P('seq', 'head'), may hold values from -6 to 6
- value_vectors: bfloat16 [32768, 4096], P('seq', 'head'), may hold values from -6 to 6
- grad_output: bfloat16 [32768, 4096], P('seq', 'head'), may hold values from -6 to 6
Outputs:
- grad_query: bfloat16 [32768, 4096], P('seq', 'head')
- grad_key: bfloat16 [32768, 4096], P('seq', 'head')
- grad_value: bfloat16 [32768, 4096], P('seq', 'head')
The draws below stay inside these ranges and needn't reach their ends.
Inputs may be any that keep to these rules, and one draw needn't show every extreme that they name: `cluster_id`: of the 1024 tokens of one index of seq, at most 48 have sorted positions in the block of 1024 sorted positions of any one index of seq, and some pair reaches 48 in every draw. The clusters of each block of 8 consecutive ids hold 1024 tokens together.
All inputs are finite; a program needn't handle non-finite values.
Results may differ from the reference program's by a relative error of at most 0.0093.
Values may be sent and summed in bfloat16 or wider, within the bound.
A program may use at most 128 MiB of HBM per device.

```python
import math
import jax
import jax.numpy as jnp
from jax import lax

HEADS = 32
HD = 128
CLUSTERS = 256
SPAN = 512
TOK_DEV = 1024
TOKENS = 32768
FEAT = 4096
N_SEQ = 32


def draw_cluster_id(key, part):
    key = jax.random.fold_in(key, 11)
    subkeys = jax.random.split(key, 6)
    seq_count = N_SEQ
    capacity = TOK_DEV * 3 // (2 * seq_count)
    base_count = (TOK_DEV - capacity) // (seq_count - 1)
    leftover = TOK_DEV - capacity - (seq_count - 1) * base_count
    spread = min(capacity - base_count - 1, base_count)
    indices = jnp.arange(seq_count - 1, dtype=jnp.int32)
    others = base_count + (indices < leftover).astype(jnp.int32)
    jitter = jax.random.randint(subkeys[0], (seq_count - 1,), 0, spread + 1)
    others = others + jitter - jnp.roll(jitter, 1)
    weights = jnp.concatenate([jnp.array([capacity], jnp.int32), others.astype(jnp.int32)])
    weights = jax.random.permutation(subkeys[1], weights)
    sigma = jax.random.permutation(subkeys[2], seq_count)
    tau = jax.random.permutation(subkeys[3], seq_count)
    pair_counts = weights[(sigma[None, :] - tau[:, None]) % seq_count]
    ends = jnp.cumsum(pair_counts, axis=1)
    slots = jnp.arange(TOK_DEV, dtype=jnp.int32)
    owner_label = jnp.sum((slots[None, :, None] >= ends[:, None, :]).astype(jnp.int32), axis=-1)
    per_owner = CLUSTERS // seq_count
    clusters = owner_label * per_owner + jax.random.randint(subkeys[4], (seq_count, TOK_DEV), 0, per_owner)
    row_keys = jax.random.split(subkeys[5], seq_count)
    clusters = jax.vmap(jax.random.permutation)(row_keys, clusters)
    return clusters.reshape(-1).astype(jnp.int32)


def draw_queries(key, part):
    key = jax.random.fold_in(key, 21)
    return jnp.clip(jax.random.normal(key, (TOKENS, FEAT), jnp.float32), -6.0, 6.0).astype(jnp.bfloat16)


def draw_key_vectors(key, part):
    key = jax.random.fold_in(key, 22)
    return jnp.clip(jax.random.normal(key, (TOKENS, FEAT), jnp.float32), -6.0, 6.0).astype(jnp.bfloat16)


def shard_levels(own_key, extent, cuts, low, high):
    def one(dim, blocks):
        heights = jax.random.uniform(jax.random.fold_in(jax.random.fold_in(own_key, 6), dim), (blocks,), jnp.float32, low / len(cuts), high / len(cuts))
        return jnp.repeat(jnp.exp(heights), extent[dim] // blocks).reshape((-1,) + (1,) * (len(extent) - dim - 1))

    loudness = one(*cuts[0])
    for cut in cuts[1:]:
        loudness = loudness * one(*cut)
    return loudness


def normal_values(own_key, shape, scale, limit, shards=(), held_as=jnp.bfloat16):
    loudness = shard_levels(own_key, shape, shards, -0.22, 0.18) if shards else 1.0
    result = jax.random.normal(own_key, shape, jnp.float32) * scale * loudness
    return jnp.minimum(jnp.maximum(result, -limit), limit).astype(held_as)


def setup_inputs(seed: int = 0) -> dict:
    arg_keys = jax.random.split(jax.random.key(seed), 6)
    return {
        "cluster_id": draw_cluster_id(jax.random.fold_in(arg_keys[5], 71), 0),
        "queries": draw_queries(jax.random.fold_in(arg_keys[5], 71), 0),
        "key_vectors": draw_key_vectors(jax.random.fold_in(arg_keys[5], 71), 0),
        "value_vectors": normal_values(arg_keys[3], (TOKENS, FEAT), 1.0, 6.0, ((0, 32), (1, 8))),
        "grad_output": normal_values(arg_keys[4], (TOKENS, FEAT), 1.0, 6.0, ((0, 32), (1, 8))),
    }


def span_grads(query_rows, key_rows, value_rows, cotangent, has_previous):
    factor = 1.0 / math.sqrt(query_rows.shape[-1])
    raw_scores = jnp.dot(query_rows, key_rows.T, preferred_element_type=jnp.float32) * factor
    columns = jnp.arange(key_rows.shape[0])
    keep = (columns >= query_rows.shape[0]) | has_previous
    raw_scores = jnp.where(keep[None, :], raw_scores, -jnp.inf)
    top_score = lax.optimization_barrier(jnp.max(raw_scores, axis=-1, keepdims=True))
    expo = jnp.exp(raw_scores - top_score)
    probs = expo / lax.optimization_barrier(jnp.sum(expo, axis=-1, keepdims=True))
    probs_rounded = probs.astype(jnp.bfloat16)
    value_part = jnp.dot(probs_rounded.T, cotangent, preferred_element_type=jnp.float32)
    grad_probs = jnp.dot(cotangent, value_rows.T, preferred_element_type=jnp.float32)
    delta = lax.optimization_barrier(jnp.sum(probs * grad_probs, axis=-1, keepdims=True))
    grad_scores = (probs * (grad_probs - delta) * factor).astype(jnp.bfloat16)
    query_part = jnp.dot(grad_scores, key_rows, preferred_element_type=jnp.float32)
    key_part = jnp.dot(grad_scores.T, query_rows, preferred_element_type=jnp.float32)
    return (query_part, key_part, value_part)

def reference(cluster_id, queries, key_vectors, value_vectors, grad_output):
    sorting = jnp.argsort(cluster_id, stable=True).astype(jnp.int32)
    span_count = TOKENS // SPAN

    def to_spans(matrix):
        return matrix[sorting].reshape(span_count, SPAN, HEADS, HD).transpose(0, 2, 1, 3)
    query_spans = to_spans(queries)
    key_spans = to_spans(key_vectors)
    value_spans = to_spans(value_vectors)
    grad_spans = to_spans(grad_output)
    key_before = jnp.concatenate([jnp.zeros_like(key_spans[:1]), key_spans[:-1]], axis=0)
    value_before = jnp.concatenate([jnp.zeros_like(value_spans[:1]), value_spans[:-1]], axis=0)
    key_window = jnp.concatenate([key_before, key_spans], axis=2)
    value_window = jnp.concatenate([value_before, value_spans], axis=2)
    has_previous = jnp.arange(span_count) > 0

    def per_span(item):
        query_rows, key_rows, value_rows, cotangent, flag = item
        return jax.vmap(span_grads, in_axes=(0, 0, 0, 0, None))(query_rows, key_rows, value_rows, cotangent, flag)
    query_part, key_part, value_part = lax.map(per_span, (query_spans, key_window, value_window, grad_spans, has_previous))

    def combine(term):
        leading = term[:, :, :SPAN]
        own_rows = term[:, :, SPAN:]
        return own_rows + jnp.concatenate([leading[1:], jnp.zeros_like(leading[:1])], axis=0)

    def restore(term):
        flat = term.transpose(0, 2, 1, 3).reshape(TOKENS, FEAT).astype(jnp.bfloat16)
        return jnp.zeros((TOKENS, FEAT), jnp.bfloat16).at[sorting].set(flat)
    return (restore(query_part), restore(combine(key_part)), restore(combine(value_part)))
```

```python
import functools
import math

import jax
import jax.numpy as jnp
from jax import lax
from jax.experimental import pallas as pl
from jax.experimental.pallas import tpu as pltpu
from jax.sharding import PartitionSpec as P

MESH = pl.DeviceIdType.MESH
HD = 128
SPAN = 512
ROWS = 1024
SEQ = 32
HEAD = 8
NY = 4
NZ = 8
HEADS = 4
CAP = 48
SLOTS = SEQ * CAP
QT = 256
FACTOR = 1.0 / math.sqrt(HD)
LOG2E = 1.4426950408889634
F32 = jnp.float32
BF16 = jnp.bfloat16
I32 = jnp.int32


def iota(shape, dim):
    return lax.broadcasted_iota(I32, shape, dim)


def onehot(mask):
    return jnp.where(mask, 1.0, 0.0).astype(BF16)


def mm(a, b):
    return jnp.dot(a, b, preferred_element_type=F32)


def mm_nt(a, b):
    return lax.dot_general(a, b, (((1,), (1,)), ((), ())), preferred_element_type=F32)


def aligned(value, size):
    return pl.multiple_of(value, size)


def kernel(
    ids_ref, q_ref, k_ref, v_ref, g_ref, dq_ref, dk_ref, dv_ref,
    ids_buf, xin, send_f, recv_f, meta_s, meta_r, rows, tail, lead_s, lead_r,
    grads, send_r, recv_r, outs, acc_k, acc_v, flat, send_row, send_col, pos_row, pos_col,
    in_sem, out_sem, ids_ss, ids_rs, meta_ss, meta_rs, fwd_ss, fwd_rs, ret_ss, ret_rs,
    tail_ss, tail_rs, lead_ss, lead_rs,
):
    me = lax.axis_index("seq")
    head = lax.axis_index("head")
    zi = me // NY
    yi = lax.rem(me, NY)

    def block_at(device, j):
        return (device // NY) * NY + lax.rem(lax.rem(device, NY) + NY - j, NY)

    def device_of(block, j):
        return (block // NY) * NY + lax.rem(lax.rem(block, NY) + j, NY)

    def peer(k):
        return lax.rem(me + k, SEQ)

    def remote(src, dst, ss, rs, seq, hd):
        return pltpu.make_async_remote_copy(
            src_ref=src, dst_ref=dst, send_sem=ss, recv_sem=rs,
            device_id=(seq, hd), device_id_type=MESH,
        )

    def wait_bytes(ref, sem):
        pltpu.make_async_copy(ref, ref, sem).wait()

    def in_copy(j, t):
        src = (q_ref, k_ref, v_ref, g_ref)[t]
        return pltpu.make_async_copy(
            src.at[:, pl.ds(aligned(j * HD, HD), HD)],
            xin.at[j, :, pl.ds(t * HD, HD)],
            in_sem.at[j, t],
        )

    def out_copy(j, t):
        dst = (dq_ref, dk_ref, dv_ref)[t]
        return pltpu.make_async_copy(
            outs.at[j, :, pl.ds(t * HD, HD)],
            dst.at[:, pl.ds(aligned(j * HD, HD), HD)],
            out_sem.at[j, t],
        )

    barrier = pltpu.get_barrier_semaphore()

    @pl.loop(1, SEQ)
    def _(k):
        pl.semaphore_signal(barrier, inc=1, device_id=(peer(k), head), device_id_type=MESH)

    @pl.loop(1, HEAD)
    def _(k):
        pl.semaphore_signal(
            barrier, inc=1, device_id=(me, lax.rem(head + k, HEAD)), device_id_type=MESH
        )

    @pl.loop(0, HEADS)
    def _(j):
        for t in range(4):
            in_copy(j, t).start()

    ids_buf[head] = ids_ref[...]
    pl.semaphore_wait(barrier, SEQ - 1 + HEAD - 1)

    @pl.loop(1, HEAD)
    def _(k):
        remote(
            ids_buf.at[head], ids_buf.at[head], ids_ss, ids_rs, me, lax.rem(head + k, HEAD)
        ).start()

    lane = iota((128, SLOTS), 1)
    source_of = lax.shift_right_logical(lane * 1366, 16)
    flat[...] = onehot(lane - source_of * CAP == iota((128, SLOTS), 0))
    upper = onehot(iota((128, 128), 0) < iota((128, 128), 1))
    wait_bytes(ids_buf.at[pl.ds(0, HEAD - 1)], ids_rs)

    run = jnp.zeros((SEQ, 1), F32)
    meta = jnp.zeros((SEQ, 128), F32)
    for c in range(ROWS // 128):
        idc = ids_buf[c]
        owner = lax.shift_right_logical(idc, 3)
        cluster = (idc & 7).astype(F32) + 1.0
        mine = jnp.where(iota((SEQ, 128), 0) == owner, 1.0, 0.0)
        before = mm(mine.astype(BF16), upper) + run
        run = run + jnp.sum(mine, axis=1, keepdims=True)
        slot = jnp.sum(mine * before, axis=0, keepdims=True).astype(I32)
        index = owner * CAP + slot
        send_row[:, c * 128 : (c + 1) * 128] = jnp.broadcast_to(index, (8, 128))
        send_col[c * 128 : (c + 1) * 128, :] = (
            jnp.broadcast_to(index, (128, 128)).astype(F32).T.astype(I32)
        )
        meta = meta + mm_nt((mine * cluster).astype(BF16), onehot(iota((128, 128), 0) == slot))
    for b in range(SEQ):
        meta_s[b % NY, b // NY] = meta[b : b + 1, :]

    @pl.loop(1, SEQ)
    def _(k):
        device = peer(k)
        remote(
            meta_s.at[:, device // NY], meta_r.at[:, me], meta_ss, meta_rs, device, head
        ).start()

    for b in range(NY):
        meta_r[b, me] = meta_s[b, zi]

    def pack_forward(j):
        for t in range(4):
            in_copy(j, t).wait()

        @pl.loop(0, SLOTS // 256)
        def _(t):
            r0 = aligned(t * 256, 256)
            choose = onehot(send_row[0:1, :] == iota((256, ROWS), 0) + r0)
            send_f[j, pl.ds(r0, 256), :] = mm(choose, xin[j]).astype(BF16)

        @pl.loop(1, SEQ)
        def _(k):
            device = peer(k)
            start = aligned(block_at(device, j) * CAP, CAP)
            remote(
                send_f.at[j, pl.ds(start, CAP)],
                recv_f.at[j, pl.ds(aligned(me * CAP, CAP), CAP)],
                fwd_ss.at[j], fwd_rs.at[j], device, head,
            ).start()

        own = aligned(block_at(me, j) * CAP, CAP)
        recv_f[j, pl.ds(aligned(me * CAP, CAP), CAP), :] = send_f[j, pl.ds(own, CAP), :]

    @pl.loop(0, 2)
    def _(j):
        pack_forward(j)

    wait_bytes(meta_r.at[:, pl.ds(0, SEQ - 1)], meta_rs)

    def positions(j):
        m = meta_r[lax.rem(yi + NY - j, NY)].reshape(SEQ, 128)
        hot = jnp.concatenate([jnp.where(m == c + 1.0, 1.0, 0.0) for c in range(8)], axis=0)
        within = mm(hot.astype(BF16), upper)
        total = jnp.broadcast_to(jnp.sum(hot, axis=1, keepdims=True), (8 * SEQ, 128))
        lower = onehot(iota((8 * SEQ, 8 * SEQ), 1) < iota((8 * SEQ, 8 * SEQ), 0))
        placed = hot * (mm(lower, total.astype(BF16)) + within)
        pos = jnp.where(m > 0.5, 0.0, -1.0)
        for c in range(8):
            pos = pos + placed[c * SEQ : (c + 1) * SEQ, :]
        high = jnp.floor(pos * (1.0 / 32.0))
        low = pos - high * 32.0
        parts = mm(jnp.concatenate([high, low], axis=0).astype(BF16), flat[...])
        spread = parts[:SEQ] * 32.0 + parts[SEQ:]
        mine = iota((SEQ, SLOTS), 0) == lax.shift_right_logical(iota((SEQ, SLOTS), 1) * 1366, 16)
        row = jnp.sum(jnp.where(mine, spread, 0.0), axis=0, keepdims=True)
        pos_row[...] = jnp.broadcast_to(row, (8, SLOTS)).astype(I32)
        for c in range(SLOTS // 128):
            piece = row[:, c * 128 : (c + 1) * 128]
            pos_col[c * 128 : (c + 1) * 128, :] = (
                jnp.broadcast_to(piece, (128, 128)).T.astype(I32)
            )

    def column_hot(column, count):
        return jnp.concatenate(
            [onehot(column == iota((256, 128), 1) + 128 * c) for c in range(count)], axis=1
        )

    def attend(j, span):
        base = span * SPAN
        if span == 1:
            keys = rows[j, :, HD : 2 * HD]
            values = rows[j, :, 2 * HD : 3 * HD]
        else:
            keys = jnp.concatenate([tail[j, :, :HD], rows[j, :SPAN, HD : 2 * HD]], axis=0)
            values = jnp.concatenate([tail[j, :, HD:], rows[j, :SPAN, 2 * HD : 3 * HD]], axis=0)
        first = block_at(me, j) == 0
        part_k = part_v = None
        for t in range(SPAN // QT):
            at = base + t * QT
            query = rows[j, at : at + QT, 0:HD]
            cot = rows[j, at : at + QT, 3 * HD : 4 * HD]
            scores = mm_nt(keys, query)
            if span == 0:
                gone = jnp.logical_and(iota((2 * SPAN, QT), 0) < SPAN, first)
                scores = jnp.where(gone, -jnp.inf, scores)
            top = jnp.max(scores, axis=0, keepdims=True)
            expo = jnp.exp2((scores - top) * (FACTOR * LOG2E))
            probs = expo * (1.0 / jnp.sum(expo, axis=0, keepdims=True))
            grad_probs = mm_nt(values, cot)
            delta = jnp.sum(probs * grad_probs, axis=0, keepdims=True)
            ds = (probs * (grad_probs - delta) * FACTOR).astype(BF16)
            pv = mm(probs.astype(BF16), cot)
            pk = mm(ds, query)
            part_k = pk if part_k is None else part_k + pk
            part_v = pv if part_v is None else part_v + pv
            dq = lax.dot_general(
                keys, ds, (((0,), (0,)), ((), ())), preferred_element_type=F32
            )
            grads[at : at + QT, 0:HD] = dq.T.astype(BF16)
        return part_k, part_v

    @pl.loop(0, HEADS)
    def _(j):
        positions(j)
        wait_bytes(recv_f.at[j, pl.ds(0, SLOTS - CAP)], fwd_rs.at[j])

        @pl.loop(0, ROWS // 256)
        def _(t):
            r0 = aligned(t * 256, 256)
            choose = onehot(pos_row[0:1, :] == iota((256, SLOTS), 0) + r0)
            rows[j, pl.ds(r0, 256), :] = mm(choose, recv_f[j]).astype(BF16)

        block = block_at(me, j)
        after = device_of(lax.rem(block + 1, SEQ), j)
        prior = device_of(lax.rem(block + SEQ - 1, SEQ), j)
        send_tail = remote(
            rows.at[j, pl.ds(SPAN, SPAN), pl.ds(HD, 2 * HD)], tail.at[j],
            tail_ss.at[j], tail_rs.at[j], after, head,
        )
        send_tail.start()

        @pl.when(j < HEADS - 2)
        def _():
            pack_forward(j + 2)

        part_k, part_v = attend(j, 1)
        acc_k[...] = part_k
        acc_v[...] = part_v
        send_tail.wait_recv()
        part_k, part_v = attend(j, 0)
        lead_s[j, :, :HD] = part_k[:SPAN].astype(BF16)
        lead_s[j, :, HD:] = part_v[:SPAN].astype(BF16)
        send_lead = remote(
            lead_s.at[j], lead_r.at[j], lead_ss.at[j], lead_rs.at[j], prior, head
        )
        send_lead.start()
        grads[:SPAN, HD : 2 * HD] = (acc_k[:SPAN] + part_k[SPAN:]).astype(BF16)
        grads[:SPAN, 2 * HD :] = (acc_v[:SPAN] + part_v[SPAN:]).astype(BF16)
        send_lead.wait_recv()
        grads[SPAN:, HD : 2 * HD] = (acc_k[SPAN:] + lead_r[j, :, :HD].astype(F32)).astype(BF16)
        grads[SPAN:, 2 * HD :] = (acc_v[SPAN:] + lead_r[j, :, HD:].astype(F32)).astype(BF16)

        @pl.loop(0, SLOTS // 256)
        def _(t):
            r0 = aligned(t * 256, 256)
            choose = column_hot(pos_col[pl.ds(r0, 256), :], ROWS // 128)
            send_r[j, pl.ds(r0, 256), :] = mm(choose, grads[...]).astype(BF16)

        own = aligned(block * CAP, CAP)

        @pl.loop(1, SEQ)
        def _(k):
            device = peer(k)
            remote(
                send_r.at[j, pl.ds(aligned(device * CAP, CAP), CAP)],
                recv_r.at[j, pl.ds(own, CAP)],
                ret_ss.at[j], ret_rs.at[j], device, head,
            ).start()

        recv_r[j, pl.ds(own, CAP), :] = send_r[j, pl.ds(aligned(me * CAP, CAP), CAP), :]

    @pl.loop(0, HEADS)
    def _(j):
        wait_bytes(recv_r.at[j, pl.ds(0, SLOTS - CAP)], ret_rs.at[j])

        @pl.loop(0, ROWS // 256)
        def _(t):
            r0 = aligned(t * 256, 256)
            choose = column_hot(send_col[pl.ds(r0, 256), :], SLOTS // 128)
            outs[j, pl.ds(r0, 256), :] = mm(choose, recv_r[j]).astype(BF16)

        for t in range(3):
            out_copy(j, t).start()

    wait_bytes(ids_buf.at[pl.ds(0, HEAD - 1)], ids_ss)
    wait_bytes(meta_r.at[:, pl.ds(0, SEQ - 1)], meta_ss)

    @pl.loop(0, HEADS)
    def _(j):
        wait_bytes(send_f.at[j, pl.ds(0, SLOTS - CAP)], fwd_ss.at[j])
        wait_bytes(send_r.at[j, pl.ds(0, SLOTS - CAP)], ret_ss.at[j])
        wait_bytes(tail.at[j], tail_ss.at[j])
        wait_bytes(lead_s.at[j], lead_ss.at[j])
        for t in range(3):
            out_copy(j, t).wait()


def local(cluster_id, queries, key_vectors, value_vectors, grad_output):
    hbm = pl.BlockSpec(memory_space=pl.ANY)
    dma = pltpu.SemaphoreType.DMA
    grad = jax.ShapeDtypeStruct((ROWS, HEADS * HD), BF16)
    return pl.pallas_call(
        kernel,
        out_shape=(grad, grad, grad),
        in_specs=[pl.BlockSpec(memory_space=pltpu.VMEM), hbm, hbm, hbm, hbm],
        out_specs=(hbm, hbm, hbm),
        scratch_shapes=[
            pltpu.VMEM((HEAD, 1, 128), I32),
            pltpu.VMEM((HEADS, ROWS, 4 * HD), BF16),
            pltpu.VMEM((HEADS, SLOTS, 4 * HD), BF16),
            pltpu.VMEM((HEADS, SLOTS, 4 * HD), BF16),
            pltpu.VMEM((NY, NZ, 1, 128), F32),
            pltpu.VMEM((NY, SEQ, 1, 128), F32),
            pltpu.VMEM((HEADS, ROWS, 4 * HD), BF16),
            pltpu.VMEM((HEADS, SPAN, 2 * HD), BF16),
            pltpu.VMEM((HEADS, SPAN, 2 * HD), BF16),
            pltpu.VMEM((HEADS, SPAN, 2 * HD), BF16),
            pltpu.VMEM((ROWS, 3 * HD), BF16),
            pltpu.VMEM((HEADS, SLOTS, 3 * HD), BF16),
            pltpu.VMEM((HEADS, SLOTS, 3 * HD), BF16),
            pltpu.VMEM((HEADS, ROWS, 3 * HD), BF16),
            pltpu.VMEM((ROWS, HD), F32),
            pltpu.VMEM((ROWS, HD), F32),
            pltpu.VMEM((128, SLOTS), BF16),
            pltpu.VMEM((8, ROWS), I32),
            pltpu.VMEM((ROWS, 128), I32),
            pltpu.VMEM((8, SLOTS), I32),
            pltpu.VMEM((SLOTS, 128), I32),
            dma((HEADS, 4)),
            dma((HEADS, 3)),
            dma, dma, dma, dma,
            dma((HEADS,)), dma((HEADS,)), dma((HEADS,)), dma((HEADS,)),
            dma((HEADS,)), dma((HEADS,)), dma((HEADS,)), dma((HEADS,)),
        ],
        compiler_params=pltpu.CompilerParams(
            collective_id=0, has_side_effects=True, vmem_limit_bytes=60 * 1024 * 1024
        ),
    )(cluster_id.reshape(1, 128), queries, key_vectors, value_vectors, grad_output)


def solution(mesh):
    placed = (P(("seq", "head")),) + (P("seq", "head"),) * 4
    return jax.shard_map(
        local,
        mesh=mesh,
        in_specs=placed,
        out_specs=(P("seq", "head"),) * 3,
        check_vma=False,
    )
```

```python
import functools
import math

import jax
import jax.numpy as jnp
from jax import lax
from jax.experimental import pallas as pl
from jax.experimental.pallas import tpu as pltpu
from jax.sharding import PartitionSpec as P

MESH = pl.DeviceIdType.MESH
HD = 128
SPAN = 512
ROWS = 1024
SEQ = 32
HEAD = 8
NY = 4
NZ = 8
HEADS = 4
CAP = 32
DIRECT = SEQ * CAP
SIDE = 64
CROSS = 32
EXTRA = NY * SIDE
SLOTS = DIRECT + EXTRA
WIDE = 48
WIDE_SLOTS = SEQ * WIDE
QT = 256
FACTOR = 1.0 / math.sqrt(HD)
LOG2E = 1.4426950408889634
F32 = jnp.float32
BF16 = jnp.bfloat16
I32 = jnp.int32


def iota(shape, dim):
    return lax.broadcasted_iota(I32, shape, dim)


def onehot(mask):
    return jnp.where(mask, 1.0, 0.0).astype(BF16)


def mm(a, b):
    return jnp.dot(a, b, preferred_element_type=F32)


def mm_nt(a, b):
    return lax.dot_general(a, b, (((1,), (1,)), ((), ())), preferred_element_type=F32)


def aligned(value, size):
    return pl.multiple_of(value, size)


def column_hot(column, count):
    return jnp.concatenate(
        [onehot(column == iota((256, 128), 1) + 128 * c) for c in range(count)], axis=1
    )

def attend(rows, tail, grads, j, span, first):
    base = span * SPAN
    if span == 1:
        keys = rows[j, :, HD : 2 * HD]
        values = rows[j, :, 2 * HD : 3 * HD]
    else:
        keys = jnp.concatenate([tail[j, :, :HD], rows[j, :SPAN, HD : 2 * HD]], axis=0)
        values = jnp.concatenate([tail[j, :, HD:], rows[j, :SPAN, 2 * HD : 3 * HD]], axis=0)
    part_k = part_v = None
    for t in range(SPAN // QT):
        at = base + t * QT
        query = rows[j, at : at + QT, 0:HD]
        cot = rows[j, at : at + QT, 3 * HD : 4 * HD]
        scores = mm_nt(keys, query)
        if span == 0:
            gone = jnp.logical_and(iota((2 * SPAN, QT), 0) < SPAN, first)
            scores = jnp.where(gone, -jnp.inf, scores)
        top = jnp.max(scores, axis=0, keepdims=True)
        expo = jnp.exp2((scores - top) * (FACTOR * LOG2E))
        probs = expo * (1.0 / jnp.sum(expo, axis=0, keepdims=True))
        grad_probs = mm_nt(values, cot)
        delta = jnp.sum(probs * grad_probs, axis=0, keepdims=True)
        ds = (probs * (grad_probs - delta) * FACTOR).astype(BF16)
        pv = mm(probs.astype(BF16), cot)
        pk = mm(ds, query)
        part_k = pk if part_k is None else part_k + pk
        part_v = pv if part_v is None else part_v + pv
        dq = lax.dot_general(
            keys, ds, (((0,), (0,)), ((), ())), preferred_element_type=F32
        )
        grads[j, at : at + QT, 0:HD] = dq.T.astype(BF16)
    return part_k, part_v

def kernel(
    ids_ref, q_ref, k_ref, v_ref, g_ref, dq_ref, dk_ref, dv_ref, flag_ref,
    ids_buf, xin, send_f, recv_f, meta_s, meta_r, cnt_s, cnt_r, flag_s, flag_r, rows, tail,
    lead_s, lead_r, grads, send_r, recv_r, acc_k, acc_v, flat, send_row, send_col, pos_row,
    pos_col, spots, mb, mbt, mc, mct, a_r, b_s, b_r, c_s, cr_r, br_s, br_r, ar_s,
    in_sem, out_sem, ids_ss, ids_rs, meta_ss, meta_rs, cnt_ss, cnt_rs, flag_ss, flag_rs,
    fwd_ss, fwd_rs, ret_ss, ret_rs, tail_ss, tail_rs, lead_ss, lead_rs,
    a_ss, a_rs, b_ss, b_rs, c_ss, c_rs, cr_ss, cr_rs, br_ss, br_rs, ar_ss, ar_rs,
):
    me = lax.axis_index("seq")
    head = lax.axis_index("head")
    zi = me // NY
    yi = lax.rem(me, NY)

    def block_at(device, j):
        return (device // NY) * NY + lax.rem(lax.rem(device, NY) + NY - j, NY)

    def device_of(block, j):
        return (block // NY) * NY + lax.rem(lax.rem(block, NY) + j, NY)

    def peer(k):
        return lax.rem(me + k, SEQ)

    def remote(src, dst, ss, rs, seq, hd):
        return pltpu.make_async_remote_copy(
            src_ref=src, dst_ref=dst, send_sem=ss, recv_sem=rs,
            device_id=(seq, hd), device_id_type=MESH,
        )

    def wait_bytes(ref, sem):
        pltpu.make_async_copy(ref, ref, sem).wait()

    def in_copy(j, t):
        src = (q_ref, k_ref, v_ref, g_ref)[t]
        return pltpu.make_async_copy(
            src.at[:, pl.ds(aligned(j * HD, HD), HD)],
            xin.at[j, :, pl.ds(t * HD, HD)],
            in_sem.at[j, t],
        )

    def out_copy(j, t):
        dst = (dq_ref, dk_ref, dv_ref)[t]
        return pltpu.make_async_copy(
            xin.at[j, :, pl.ds(t * HD, HD)],
            dst.at[:, pl.ds(aligned(j * HD, HD), HD)],
            out_sem.at[j, t],
        )

    barrier = pltpu.get_barrier_semaphore()

    @pl.loop(1, SEQ)
    def _(k):
        pl.semaphore_signal(barrier, inc=1, device_id=(peer(k), head), device_id_type=MESH)

    @pl.loop(1, HEAD)
    def _(k):
        pl.semaphore_signal(
            barrier, inc=1, device_id=(me, lax.rem(head + k, HEAD)), device_id_type=MESH
        )

    @pl.loop(0, HEADS)
    def _(j):
        for t in range(4):
            in_copy(j, t).start()

    ids_buf[head] = ids_ref[...]
    pl.semaphore_wait(barrier, SEQ - 1 + HEAD - 1)

    @pl.loop(1, HEAD)
    def _(k):
        remote(
            ids_buf.at[head], ids_buf.at[head], ids_ss, ids_rs, me, lax.rem(head + k, HEAD)
        ).start()

    def slot_of(shape):
        col = iota(shape, 1)
        near = col < DIRECT
        past = col - DIRECT
        return (
            jnp.where(near, lax.shift_right_logical(col, 5), lax.shift_right_logical(past, 4)),
            jnp.where(near, col & 31, CAP + (past & 15)),
        )

    flat[...] = onehot(slot_of((128, DIRECT + 512))[1] == iota((128, DIRECT + 512), 0))
    upper = onehot(iota((128, 128), 0) < iota((128, 128), 1))
    sub = iota((SEQ, SEQ), 0)
    lan = iota((SEQ, SEQ), 1)
    below = onehot(lan < sub)
    below_z = onehot(
        jnp.logical_and(
            lan < sub, lax.shift_right_logical(lan, 2) == lax.shift_right_logical(sub, 2)
        )
    )
    row32 = iota((SEQ, 128), 0)
    row8 = iota((NZ, 128), 0)
    y_of = row32 & 3

    def quarter(value):
        return lax.shift_right_logical(value, 2)

    wait_bytes(ids_buf.at[pl.ds(0, HEAD - 1)], ids_rs)

    run = jnp.zeros((SEQ, 1), F32)
    meta = jnp.zeros((SEQ, 128), F32)
    owners, slots = [], []
    for c in range(ROWS // 128):
        idc = ids_buf[c]
        owner = lax.shift_right_logical(idc, 3)
        cluster = (idc & 7).astype(F32) + 1.0
        mine = jnp.where(row32 == owner, 1.0, 0.0)
        before = mm(mine.astype(BF16), upper) + run
        run = run + jnp.sum(mine, axis=1, keepdims=True)
        slot = jnp.sum(mine * before, axis=0, keepdims=True).astype(I32)
        meta = meta + mm_nt((mine * cluster).astype(BF16), onehot(iota((128, 128), 0) == slot))
        owners.append(owner)
        slots.append(slot)
    for b in range(SEQ):
        meta_s[b % NY, b // NY] = meta[b : b + 1, :]

    past = jnp.maximum(jnp.broadcast_to(run, (SEQ, 128)) - float(CAP), 0.0)
    base_f = mm(below_z, past.astype(BF16))
    plane = onehot(quarter(iota((NZ, SEQ), 1)) == iota((NZ, SEQ), 0))
    cnt_s[...] = mm(plane, past.astype(BF16))
    cnt_r[yi] = cnt_s[...]

    @pl.loop(1, SEQ)
    def _(k):
        device = peer(k)
        remote(
            meta_s.at[:, device // NY], meta_r.at[:, me], meta_ss, meta_rs, device, head
        ).start()

    @pl.loop(1, NY)
    def _(k):
        device = zi * NY + lax.rem(yi + k, NY)
        remote(cnt_s, cnt_r.at[yi], cnt_ss, cnt_rs, device, head).start()

    for b in range(NY):
        meta_r[b, me] = meta_s[b, zi]

    mine_e = cnt_s[...].astype(I32)
    offs = []
    for yy in range(NY):
        count = quarter(mine_e - ((yy - yi - row8 + 16) & 3) + 3).astype(F32)
        off = jnp.zeros((SEQ, 128), F32)
        for z in range(NZ - 1):
            off = off + jnp.where(quarter(row32) > z, count[z : z + 1, :], 0.0)
        offs.append(off)
    for c in range(ROWS // 128):
        owner, slot = owners[c], slots[c]
        mine = row32 == owner

        def pick(table):
            return jnp.sum(jnp.where(mine, table, 0.0), axis=0, keepdims=True).astype(I32)

        e = pick(base_f) + slot - CAP
        way = (e + yi + quarter(owner) + 64) & 3
        far = DIRECT + way * SIDE + quarter(e + 64) - 16
        for yy in range(NY):
            far = far + jnp.where(way == yy, pick(offs[yy]), 0)
        index = jnp.where(slot < CAP, owner * CAP + slot, far)
        send_row[:, c * 128 : (c + 1) * 128] = jnp.broadcast_to(index, (8, 128))
        send_col[c * 128 : (c + 1) * 128, :] = (
            jnp.broadcast_to(index, (128, 128)).astype(F32).T.astype(I32)
        )

    def pack_tile(j, r0):
        choose = onehot(send_row[0:1, :] == iota((256, ROWS), 0) + r0)
        send_f[j, pl.ds(r0, 256), :] = mm(choose, xin[j]).astype(BF16)

    def y_peer(k):
        return lax.rem(yi + k, NY)

    def z_peer(k):
        return lax.rem(zi + k, NZ)

    def at_side(y):
        return pl.ds(aligned(y * SIDE, SIDE), SIDE)

    def at_cross(z):
        return pl.ds(aligned(z * CROSS, CROSS), CROSS)

    def at_extra(y):
        return pl.ds(aligned(DIRECT + y * SIDE, SIDE), SIDE)

    def stage_a(j):
        for t in range(4):
            in_copy(j, t).wait()
        pack_tile(j, DIRECT)

        @pl.loop(1, NY)
        def _(k):
            y = y_peer(k)
            remote(
                send_f.at[j, at_extra(y)], a_r.at[j, at_side(yi)], a_ss.at[j], a_rs.at[j],
                zi * NY + y, head,
            ).start()

        a_r[j, at_side(yi), :] = send_f[j, at_extra(yi), :]

    def stage_b(j):
        wait_bytes(a_r.at[j, pl.ds(0, EXTRA - SIDE)], a_rs.at[j])
        b_s[j] = mm(mb[...], a_r[j]).astype(BF16)

        @pl.loop(1, NZ)
        def _(k):
            z = z_peer(k)
            remote(
                b_s.at[j, at_cross(z)], b_r.at[j, at_cross(zi)], b_ss.at[j], b_rs.at[j],
                z * NY + yi, head,
            ).start()

        b_r[j, at_cross(zi), :] = b_s[j, at_cross(zi), :]

    def stage_c(j):
        wait_bytes(b_r.at[j, pl.ds(0, EXTRA - CROSS)], b_rs.at[j])
        c_s[j] = mm(mc[...], b_r[j]).astype(BF16)

        @pl.loop(1, NY)
        def _(k):
            y = y_peer(k)
            remote(
                c_s.at[j, at_side(lax.rem(y + NY - j, NY))], recv_f.at[j, at_extra(yi)],
                c_ss.at[j], c_rs.at[j], zi * NY + y, head,
            ).start()

        recv_f[j, at_extra(yi), :] = c_s[j, at_side(lax.rem(yi + NY - j, NY)), :]

    def pack_forward(j):
        @pl.loop(0, DIRECT // 256)
        def _(t):
            pack_tile(j, aligned(t * 256, 256))

        @pl.loop(1, SEQ)
        def _(k):
            device = peer(k)
            start = aligned(block_at(device, j) * CAP, CAP)
            remote(
                send_f.at[j, pl.ds(start, CAP)],
                recv_f.at[j, pl.ds(aligned(me * CAP, CAP), CAP)],
                fwd_ss.at[j], fwd_rs.at[j], device, head,
            ).start()

        own = aligned(block_at(me, j) * CAP, CAP)
        recv_f[j, pl.ds(aligned(me * CAP, CAP), CAP), :] = send_f[j, pl.ds(own, CAP), :]

    @pl.loop(0, HEADS)
    def _(j):
        stage_a(j)

    pack_forward(0)
    wait_bytes(cnt_r.at[pl.ds(0, NY - 1)], cnt_rs)

    bad = jnp.zeros((1, 128), F32)
    starts_a, starts_b, counts = [], [], []
    filled = jnp.zeros((NZ, 128), I32)
    for y in range(NY):
        for yy in range(NY):
            share = quarter(cnt_r[y].astype(I32) - ((yy - y - row8 + 16) & 3) + 3)
            total = jnp.sum(share.astype(F32), axis=0, keepdims=True)
            bad = jnp.maximum(bad, total - float(SIDE))
        share = quarter(cnt_r[y].astype(I32) - ((yi - y - row8 + 16) & 3) + 3)
        start = jnp.zeros((NZ, 128), I32)
        for z in range(NZ - 1):
            start = start + jnp.where(row8 > z, share[z : z + 1, :], 0)
        starts_a.append(start)
        starts_b.append(filled)
        counts.append(share)
        filled = filled + share
    for yy in range(NY):
        total = jnp.zeros((NZ, 128), I32)
        for y in range(NY):
            total = total + quarter(cnt_r[y].astype(I32) - ((yy - y - row8 + 16) & 3) + 3)
        bad = jnp.maximum(
            bad, jnp.max(total.astype(F32), axis=0, keepdims=True) - float(CROSS)
        )

    def by_group(tables):
        group = lax.shift_right_logical(iota((NZ, EXTRA), 1), 6)
        result = jnp.zeros((NZ, EXTRA), I32)
        for y in range(NY):
            result = jnp.where(group == y, jnp.concatenate([tables[y]] * 2, axis=1), result)
        return result

    wide_a, wide_b, wide_c = by_group(starts_a), by_group(starts_b), by_group(counts)
    for z in range(NZ):
        step = iota((CROSS, EXTRA), 0) - wide_b[z : z + 1, :]
        place = (iota((CROSS, EXTRA), 1) & (SIDE - 1)) - wide_a[z : z + 1, :]
        hit = jnp.logical_and(
            jnp.logical_and(step >= 0, step < wide_c[z : z + 1, :]), step == place
        )
        mb[z * CROSS : (z + 1) * CROSS, :] = onehot(hit)
    mbt[...] = mb[...].astype(F32).T.astype(BF16)

    @pl.loop(0, HEADS)
    def _(j):
        stage_b(j)

    pack_forward(1)
    wait_bytes(meta_r.at[:, pl.ds(0, SEQ - 1)], meta_rs)

    bases = [jnp.zeros((SEQ, 128), I32)]
    for b in range(NY):
        held = jnp.where(meta_r[b].reshape(SEQ, 128) > 0.5, 1.0, 0.0)
        held = jnp.maximum(jnp.sum(held, axis=1, keepdims=True) - float(CAP), 0.0)
        bases.append(bases[b] + jnp.broadcast_to(held, (SEQ, 128)).astype(I32))
    firsts = []
    for yy in range(NY):
        residue = (yy - y_of - zi + 16) & 3
        firsts.append([quarter(base - residue + 3) for base in bases])
    lengths = [[f[b + 1] - f[b] for b in range(NY)] for f in firsts]
    stacked = jnp.concatenate([v.astype(F32) for f in lengths for v in f], axis=1)
    before_c = mm(below, stacked.astype(BF16))
    landing = []
    for yy in range(NY):
        landing.append([])
        for b in range(NY):
            at = (yy * NY + b) * 128
            part = before_c[:, at : at + 128].astype(I32)
            landing[yy].append(part)
            total = (part + lengths[yy][b])[SEQ - 1 : SEQ, :].astype(F32)
            bad = jnp.maximum(bad, total - float(SIDE))
    lane = iota((SEQ, 128), 1)
    for b in range(NY):
        e = bases[b] + lane - CAP
        way = (e + y_of + zi + 64) & 3
        spot = jnp.zeros((SEQ, 128), I32)
        for yy in range(NY):
            here = yy * SIDE + landing[yy][b] + quarter(e + 64) - 16 - firsts[yy][b]
            spot = jnp.where(way == yy, here, spot)
        used = jnp.logical_and(meta_r[b].reshape(SEQ, 128) > 0.5, lane >= CAP)
        spots[b] = jnp.where(used, spot.astype(F32), -1.0)

    def chosen(tables):
        result = tables[0]
        for yy in range(1, NY):
            result = jnp.where(yi == yy, tables[yy], result)
        return result

    my_total = chosen([f[NY] for f in firsts])
    my_start = mm(below_z, my_total.astype(F32).astype(BF16))
    col = iota((SEQ, EXTRA), 1)
    for b in range(NY):
        landing_b = chosen([landing[yy][b] for yy in range(NY)]).astype(F32)
        length_b = chosen([lengths[yy][b] for yy in range(NY)]).astype(F32)
        source_b = my_start + chosen([firsts[yy][b] for yy in range(NY)]).astype(F32)
        found = jnp.zeros((SIDE, EXTRA), F32)
        for y in range(NY):
            match = iota((SEQ, EXTRA), 0) == lax.shift_right_logical(col, 5) * NY + y

            def across(table):
                twice = jnp.concatenate([table, table], axis=1)
                return jnp.sum(jnp.where(match, twice, 0.0), axis=0, keepdims=True).astype(I32)

            step = iota((SIDE, EXTRA), 0) - across(landing_b)
            place = (iota((SIDE, EXTRA), 1) & (CROSS - 1)) - across(source_b)
            hit = jnp.logical_and(
                jnp.logical_and(step >= 0, step < across(length_b)), step == place
            )
            found = found + jnp.where(hit, 1.0, 0.0)
        mc[b * SIDE : (b + 1) * SIDE, :] = found.astype(BF16)
    mct[...] = mc[...].astype(F32).T.astype(BF16)

    flag_s[...] = jnp.broadcast_to(jnp.where(bad > 0.5, 1.0, 0.0), (8, 128))
    flag_r[zi] = flag_s[...]

    @pl.loop(1, NZ)
    def _(k):
        remote(
            flag_s, flag_r.at[zi], flag_ss, flag_rs, z_peer(k) * NY + yi, head
        ).start()

    @pl.loop(0, HEADS)
    def _(j):
        stage_c(j)

    def positions(j):
        block = lax.rem(yi + NY - j, NY)
        m = meta_r[block].reshape(SEQ, 128)
        hot = jnp.concatenate([jnp.where(m == c + 1.0, 1.0, 0.0) for c in range(8)], axis=0)
        within = mm(hot.astype(BF16), upper)
        total = jnp.broadcast_to(jnp.sum(hot, axis=1, keepdims=True), (8 * SEQ, 128))
        lower = onehot(iota((8 * SEQ, 8 * SEQ), 1) < iota((8 * SEQ, 8 * SEQ), 0))
        placed = hot * (mm(lower, total.astype(BF16)) + within)
        pos = jnp.where(m > 0.5, 0.0, -1.0)
        for c in range(8):
            pos = pos + placed[c * SEQ : (c + 1) * SEQ, :]

        def halves(value):
            high = jnp.floor(value * (1.0 / 32.0))
            return [high, value - high * 32.0]

        parts = mm(
            jnp.concatenate(halves(pos) + halves(spots[block]), axis=0).astype(BF16), flat[...]
        )
        mine = iota((SEQ, DIRECT + 512), 0) == slot_of((SEQ, DIRECT + 512))[0]
        spread = jnp.where(mine, parts[:SEQ] * 32.0 + parts[SEQ : 2 * SEQ], 0.0)
        line = jnp.sum(spread, axis=0, keepdims=True)
        spread = jnp.where(mine, parts[2 * SEQ : 3 * SEQ] * 32.0 + parts[3 * SEQ :], 0.0)
        target = jnp.sum(spread, axis=0, keepdims=True)[:, DIRECT:].astype(I32)
        high, low = halves(line[:, DIRECT:] + 1.0)
        pair = jnp.concatenate(
            [jnp.broadcast_to(high, (8, 512)), jnp.broadcast_to(low, (8, 512))], axis=0
        )
        found = mm_nt(pair.astype(BF16), onehot(iota((EXTRA, 512), 0) == target))
        extra = found[0:1, :] * 32.0 + found[8:9, :] - 1.0
        row = jnp.concatenate([line[:, :DIRECT], extra], axis=1)
        pos_row[j] = jnp.broadcast_to(row, (8, SLOTS)).astype(I32)
        for c in range(SLOTS // 128):
            piece = row[:, c * 128 : (c + 1) * 128]
            pos_col[j, c * 128 : (c + 1) * 128, :] = (
                jnp.broadcast_to(piece, (128, 128)).T.astype(I32)
            )

    def tail_copy(j):
        after = device_of(lax.rem(block_at(me, j) + 1, SEQ), j)
        return remote(
            rows.at[j, pl.ds(SPAN, SPAN), pl.ds(HD, 2 * HD)], tail.at[j],
            tail_ss.at[j], tail_rs.at[j], after, head,
        )

    def lead_copy(j):
        prior = device_of(lax.rem(block_at(me, j) + SEQ - 1, SEQ), j)
        return remote(lead_s.at[j], lead_r.at[j], lead_ss.at[j], lead_rs.at[j], prior, head)

    def open_chunk(j):
        positions(j)
        wait_bytes(recv_f.at[j, pl.ds(0, DIRECT - CAP)], fwd_rs.at[j])
        wait_bytes(recv_f.at[j, pl.ds(0, EXTRA - SIDE)], c_rs.at[j])

        @pl.loop(0, ROWS // 256)
        def _(t):
            r0 = aligned(t * 256, 256)
            choose = onehot(pos_row[j, 0:1, :] == iota((256, SLOTS), 0) + r0)
            rows[j, pl.ds(r0, 256), :] = mm(choose, recv_f[j]).astype(BF16)

        tail_copy(j).start()

    def last_span(j):
        part_k, part_v = attend(rows, tail, grads, j, 1, block_at(me, j) == 0)
        acc_k[j] = part_k
        acc_v[j] = part_v

    def first_span(j):
        tail_copy(j).wait_recv()
        part_k, part_v = attend(rows, tail, grads, j, 0, block_at(me, j) == 0)
        lead_s[j, :, :HD] = part_k[:SPAN].astype(BF16)
        lead_s[j, :, HD:] = part_v[:SPAN].astype(BF16)
        lead_copy(j).start()
        grads[j, :SPAN, HD : 2 * HD] = (acc_k[j, :SPAN] + part_k[SPAN:]).astype(BF16)
        grads[j, :SPAN, 2 * HD :] = (acc_v[j, :SPAN] + part_v[SPAN:]).astype(BF16)

    def close_chunk(j):
        lead_copy(j).wait_recv()
        grads[j, SPAN:, HD : 2 * HD] = (
            acc_k[j, SPAN:] + lead_r[j, :, :HD].astype(F32)
        ).astype(BF16)
        grads[j, SPAN:, 2 * HD :] = (
            acc_v[j, SPAN:] + lead_r[j, :, HD:].astype(F32)
        ).astype(BF16)

        def pack_back(r0):
            choose = column_hot(pos_col[j, pl.ds(r0, 256), :], ROWS // 128)
            send_r[j, pl.ds(r0, 256), :] = mm(choose, grads[j]).astype(BF16)

        pack_back(DIRECT)
        own_y = lax.rem(yi + NY - j, NY)

        @pl.loop(1, NY)
        def _(k):
            y = y_peer(k)
            remote(
                send_r.at[j, at_extra(y)], cr_r.at[j, at_side(own_y)], cr_ss.at[j],
                cr_rs.at[j], zi * NY + y, head,
            ).start()

        cr_r[j, at_side(own_y), :] = send_r[j, at_extra(yi), :]

        @pl.loop(0, DIRECT // 256)
        def _(t):
            pack_back(aligned(t * 256, 256))

        own = aligned(block_at(me, j) * CAP, CAP)

        @pl.loop(1, SEQ)
        def _(k):
            device = peer(k)
            remote(
                send_r.at[j, pl.ds(aligned(device * CAP, CAP), CAP)],
                recv_r.at[j, pl.ds(own, CAP)],
                ret_ss.at[j], ret_rs.at[j], device, head,
            ).start()

        recv_r[j, pl.ds(own, CAP), :] = send_r[j, pl.ds(aligned(me * CAP, CAP), CAP), :]

    def back_b(j):
        wait_bytes(cr_r.at[j, pl.ds(0, EXTRA - SIDE)], cr_rs.at[j])
        br_s[j] = mm(mct[...], cr_r[j]).astype(BF16)

        @pl.loop(1, NZ)
        def _(k):
            z = z_peer(k)
            remote(
                br_s.at[j, at_cross(z)], br_r.at[j, at_cross(zi)], br_ss.at[j], br_rs.at[j],
                z * NY + yi, head,
            ).start()

        br_r[j, at_cross(zi), :] = br_s[j, at_cross(zi), :]

    def back_a(j):
        wait_bytes(br_r.at[j, pl.ds(0, EXTRA - CROSS)], br_rs.at[j])
        ar_s[j] = mm(mbt[...], br_r[j]).astype(BF16)

        @pl.loop(1, NY)
        def _(k):
            y = y_peer(k)
            remote(
                ar_s.at[j, at_side(y)], recv_r.at[j, at_extra(yi)], ar_ss.at[j], ar_rs.at[j],
                zi * NY + y, head,
            ).start()

        recv_r[j, at_extra(yi), :] = ar_s[j, at_side(yi), :]

    @pl.loop(0, HEADS + 4)
    def _(i):
        @pl.when(i < HEADS - 2)
        def _():
            pack_forward(i + 2)

        @pl.when(i < HEADS)
        def _():
            open_chunk(i)

        @pl.when(jnp.logical_and(i >= 1, i <= HEADS))
        def _():
            first_span(i - 1)

        @pl.when(i < HEADS)
        def _():
            last_span(i)

        @pl.when(jnp.logical_and(i >= 2, i < HEADS + 2))
        def _():
            close_chunk(i - 2)

        @pl.when(jnp.logical_and(i >= 3, i < HEADS + 3))
        def _():
            back_b(i - 3)

        @pl.when(i >= 4)
        def _():
            back_a(i - 4)

    @pl.loop(0, HEADS)
    def _(j):
        wait_bytes(recv_r.at[j, pl.ds(0, DIRECT - CAP)], ret_rs.at[j])
        wait_bytes(recv_r.at[j, pl.ds(0, EXTRA - SIDE)], ar_rs.at[j])

        @pl.loop(0, ROWS // 256)
        def _(t):
            r0 = aligned(t * 256, 256)
            choose = column_hot(send_col[pl.ds(r0, 256), :], SLOTS // 128)
            xin[j, pl.ds(r0, 256), : 3 * HD] = mm(choose, recv_r[j]).astype(BF16)

        for t in range(3):
            out_copy(j, t).start()

    wait_bytes(flag_r.at[pl.ds(0, NZ - 1)], flag_rs)
    flag_ref[...] = jnp.max(flag_r[...], axis=0)
    wait_bytes(ids_buf.at[pl.ds(0, HEAD - 1)], ids_ss)
    wait_bytes(meta_r.at[:, pl.ds(0, SEQ - 1)], meta_ss)
    wait_bytes(cnt_r.at[pl.ds(0, NY - 1)], cnt_ss)
    wait_bytes(flag_r.at[pl.ds(0, NZ - 1)], flag_ss)

    @pl.loop(0, HEADS)
    def _(j):
        wait_bytes(send_f.at[j, pl.ds(0, DIRECT - CAP)], fwd_ss.at[j])
        wait_bytes(send_r.at[j, pl.ds(0, DIRECT - CAP)], ret_ss.at[j])
        wait_bytes(a_r.at[j, pl.ds(0, EXTRA - SIDE)], a_ss.at[j])
        wait_bytes(b_r.at[j, pl.ds(0, EXTRA - CROSS)], b_ss.at[j])
        wait_bytes(c_s.at[j, pl.ds(0, EXTRA - SIDE)], c_ss.at[j])
        wait_bytes(cr_r.at[j, pl.ds(0, EXTRA - SIDE)], cr_ss.at[j])
        wait_bytes(br_r.at[j, pl.ds(0, EXTRA - CROSS)], br_ss.at[j])
        wait_bytes(ar_s.at[j, pl.ds(0, EXTRA - SIDE)], ar_ss.at[j])
        wait_bytes(tail.at[j], tail_ss.at[j])
        wait_bytes(lead_s.at[j], lead_ss.at[j])
        for t in range(3):
            out_copy(j, t).wait()


def wide_kernel(
    ids_ref, q_ref, k_ref, v_ref, g_ref, dq_ref, dk_ref, dv_ref,
    ids_buf, xin, send_f, recv_f, meta_s, meta_r, rows, tail, lead_s, lead_r,
    grads, send_r, recv_r, outs, acc_k, acc_v, flat, send_row, send_col, pos_row, pos_col,
    in_sem, out_sem, ids_ss, ids_rs, meta_ss, meta_rs, fwd_ss, fwd_rs, ret_ss, ret_rs,
    tail_ss, tail_rs, lead_ss, lead_rs,
):
    me = lax.axis_index("seq")
    head = lax.axis_index("head")
    zi = me // NY
    yi = lax.rem(me, NY)

    def block_at(device, j):
        return (device // NY) * NY + lax.rem(lax.rem(device, NY) + NY - j, NY)

    def device_of(block, j):
        return (block // NY) * NY + lax.rem(lax.rem(block, NY) + j, NY)

    def peer(k):
        return lax.rem(me + k, SEQ)

    def remote(src, dst, ss, rs, seq, hd):
        return pltpu.make_async_remote_copy(
            src_ref=src, dst_ref=dst, send_sem=ss, recv_sem=rs,
            device_id=(seq, hd), device_id_type=MESH,
        )

    def wait_bytes(ref, sem):
        pltpu.make_async_copy(ref, ref, sem).wait()

    def in_copy(j, t):
        src = (q_ref, k_ref, v_ref, g_ref)[t]
        return pltpu.make_async_copy(
            src.at[:, pl.ds(aligned(j * HD, HD), HD)],
            xin.at[j, :, pl.ds(t * HD, HD)],
            in_sem.at[j, t],
        )

    def out_copy(j, t):
        dst = (dq_ref, dk_ref, dv_ref)[t]
        return pltpu.make_async_copy(
            outs.at[j, :, pl.ds(t * HD, HD)],
            dst.at[:, pl.ds(aligned(j * HD, HD), HD)],
            out_sem.at[j, t],
        )

    barrier = pltpu.get_barrier_semaphore()

    @pl.loop(1, SEQ)
    def _(k):
        pl.semaphore_signal(barrier, inc=1, device_id=(peer(k), head), device_id_type=MESH)

    @pl.loop(1, HEAD)
    def _(k):
        pl.semaphore_signal(
            barrier, inc=1, device_id=(me, lax.rem(head + k, HEAD)), device_id_type=MESH
        )

    @pl.loop(0, HEADS)
    def _(j):
        for t in range(4):
            in_copy(j, t).start()

    ids_buf[head] = ids_ref[...]
    pl.semaphore_wait(barrier, SEQ - 1 + HEAD - 1)

    @pl.loop(1, HEAD)
    def _(k):
        remote(
            ids_buf.at[head], ids_buf.at[head], ids_ss, ids_rs, me, lax.rem(head + k, HEAD)
        ).start()

    lane = iota((128, WIDE_SLOTS), 1)
    source_of = lax.shift_right_logical(lane * 1366, 16)
    flat[...] = onehot(lane - source_of * WIDE == iota((128, WIDE_SLOTS), 0))
    upper = onehot(iota((128, 128), 0) < iota((128, 128), 1))
    wait_bytes(ids_buf.at[pl.ds(0, HEAD - 1)], ids_rs)

    run = jnp.zeros((SEQ, 1), F32)
    meta = jnp.zeros((SEQ, 128), F32)
    for c in range(ROWS // 128):
        idc = ids_buf[c]
        owner = lax.shift_right_logical(idc, 3)
        cluster = (idc & 7).astype(F32) + 1.0
        mine = jnp.where(iota((SEQ, 128), 0) == owner, 1.0, 0.0)
        before = mm(mine.astype(BF16), upper) + run
        run = run + jnp.sum(mine, axis=1, keepdims=True)
        slot = jnp.sum(mine * before, axis=0, keepdims=True).astype(I32)
        index = owner * WIDE + slot
        send_row[:, c * 128 : (c + 1) * 128] = jnp.broadcast_to(index, (8, 128))
        send_col[c * 128 : (c + 1) * 128, :] = (
            jnp.broadcast_to(index, (128, 128)).astype(F32).T.astype(I32)
        )
        meta = meta + mm_nt((mine * cluster).astype(BF16), onehot(iota((128, 128), 0) == slot))
    for b in range(SEQ):
        meta_s[b % NY, b // NY] = meta[b : b + 1, :]

    @pl.loop(1, SEQ)
    def _(k):
        device = peer(k)
        remote(
            meta_s.at[:, device // NY], meta_r.at[:, me], meta_ss, meta_rs, device, head
        ).start()

    for b in range(NY):
        meta_r[b, me] = meta_s[b, zi]

    def pack_forward(j):
        for t in range(4):
            in_copy(j, t).wait()

        @pl.loop(0, WIDE_SLOTS // 256)
        def _(t):
            r0 = aligned(t * 256, 256)
            choose = onehot(send_row[0:1, :] == iota((256, ROWS), 0) + r0)
            send_f[j, pl.ds(r0, 256), :] = mm(choose, xin[j]).astype(BF16)

        @pl.loop(1, SEQ)
        def _(k):
            device = peer(k)
            start = aligned(block_at(device, j) * WIDE, WIDE)
            remote(
                send_f.at[j, pl.ds(start, WIDE)],
                recv_f.at[j, pl.ds(aligned(me * WIDE, WIDE), WIDE)],
                fwd_ss.at[j], fwd_rs.at[j], device, head,
            ).start()

        own = aligned(block_at(me, j) * WIDE, WIDE)
        recv_f[j, pl.ds(aligned(me * WIDE, WIDE), WIDE), :] = send_f[j, pl.ds(own, WIDE), :]

    @pl.loop(0, 2)
    def _(j):
        pack_forward(j)

    wait_bytes(meta_r.at[:, pl.ds(0, SEQ - 1)], meta_rs)

    def positions(j):
        m = meta_r[lax.rem(yi + NY - j, NY)].reshape(SEQ, 128)
        hot = jnp.concatenate([jnp.where(m == c + 1.0, 1.0, 0.0) for c in range(8)], axis=0)
        within = mm(hot.astype(BF16), upper)
        total = jnp.broadcast_to(jnp.sum(hot, axis=1, keepdims=True), (8 * SEQ, 128))
        lower = onehot(iota((8 * SEQ, 8 * SEQ), 1) < iota((8 * SEQ, 8 * SEQ), 0))
        placed = hot * (mm(lower, total.astype(BF16)) + within)
        pos = jnp.where(m > 0.5, 0.0, -1.0)
        for c in range(8):
            pos = pos + placed[c * SEQ : (c + 1) * SEQ, :]
        high = jnp.floor(pos * (1.0 / 32.0))
        low = pos - high * 32.0
        parts = mm(jnp.concatenate([high, low], axis=0).astype(BF16), flat[...])
        spread = parts[:SEQ] * 32.0 + parts[SEQ:]
        mine = iota((SEQ, WIDE_SLOTS), 0) == lax.shift_right_logical(iota((SEQ, WIDE_SLOTS), 1) * 1366, 16)
        row = jnp.sum(jnp.where(mine, spread, 0.0), axis=0, keepdims=True)
        pos_row[j] = jnp.broadcast_to(row, (8, WIDE_SLOTS)).astype(I32)
        for c in range(WIDE_SLOTS // 128):
            piece = row[:, c * 128 : (c + 1) * 128]
            pos_col[j, c * 128 : (c + 1) * 128, :] = (
                jnp.broadcast_to(piece, (128, 128)).T.astype(I32)
            )

    def tail_copy(j):
        after = device_of(lax.rem(block_at(me, j) + 1, SEQ), j)
        return remote(
            rows.at[j, pl.ds(SPAN, SPAN), pl.ds(HD, 2 * HD)], tail.at[j],
            tail_ss.at[j], tail_rs.at[j], after, head,
        )

    def lead_copy(j):
        prior = device_of(lax.rem(block_at(me, j) + SEQ - 1, SEQ), j)
        return remote(lead_s.at[j], lead_r.at[j], lead_ss.at[j], lead_rs.at[j], prior, head)

    def open_chunk(j):
        positions(j)
        wait_bytes(recv_f.at[j, pl.ds(0, WIDE_SLOTS - WIDE)], fwd_rs.at[j])

        @pl.loop(0, ROWS // 256)
        def _(t):
            r0 = aligned(t * 256, 256)
            choose = onehot(pos_row[j, 0:1, :] == iota((256, WIDE_SLOTS), 0) + r0)
            rows[j, pl.ds(r0, 256), :] = mm(choose, recv_f[j]).astype(BF16)

        tail_copy(j).start()

    def last_span(j):
        part_k, part_v = attend(rows, tail, grads, j, 1, block_at(me, j) == 0)
        acc_k[j] = part_k
        acc_v[j] = part_v

    def first_span(j):
        tail_copy(j).wait_recv()
        part_k, part_v = attend(rows, tail, grads, j, 0, block_at(me, j) == 0)
        lead_s[j, :, :HD] = part_k[:SPAN].astype(BF16)
        lead_s[j, :, HD:] = part_v[:SPAN].astype(BF16)
        lead_copy(j).start()
        grads[j, :SPAN, HD : 2 * HD] = (acc_k[j, :SPAN] + part_k[SPAN:]).astype(BF16)
        grads[j, :SPAN, 2 * HD :] = (acc_v[j, :SPAN] + part_v[SPAN:]).astype(BF16)

    def close_chunk(j):
        lead_copy(j).wait_recv()
        grads[j, SPAN:, HD : 2 * HD] = (
            acc_k[j, SPAN:] + lead_r[j, :, :HD].astype(F32)
        ).astype(BF16)
        grads[j, SPAN:, 2 * HD :] = (
            acc_v[j, SPAN:] + lead_r[j, :, HD:].astype(F32)
        ).astype(BF16)

        @pl.loop(0, WIDE_SLOTS // 256)
        def _(t):
            r0 = aligned(t * 256, 256)
            choose = column_hot(pos_col[j, pl.ds(r0, 256), :], ROWS // 128)
            send_r[j, pl.ds(r0, 256), :] = mm(choose, grads[j]).astype(BF16)

        own = aligned(block_at(me, j) * WIDE, WIDE)

        @pl.loop(1, SEQ)
        def _(k):
            device = peer(k)
            remote(
                send_r.at[j, pl.ds(aligned(device * WIDE, WIDE), WIDE)],
                recv_r.at[j, pl.ds(own, WIDE)],
                ret_ss.at[j], ret_rs.at[j], device, head,
            ).start()

        recv_r[j, pl.ds(own, WIDE), :] = send_r[j, pl.ds(aligned(me * WIDE, WIDE), WIDE), :]

    @pl.loop(0, HEADS + 2)
    def _(i):
        @pl.when(i < HEADS)
        def _():
            open_chunk(i)

        @pl.when(i < HEADS - 2)
        def _():
            pack_forward(i + 2)

        @pl.when(jnp.logical_and(i >= 1, i <= HEADS))
        def _():
            first_span(i - 1)

        @pl.when(i < HEADS)
        def _():
            last_span(i)

        @pl.when(i >= 2)
        def _():
            close_chunk(i - 2)

    @pl.loop(0, HEADS)
    def _(j):
        wait_bytes(recv_r.at[j, pl.ds(0, WIDE_SLOTS - WIDE)], ret_rs.at[j])

        @pl.loop(0, ROWS // 256)
        def _(t):
            r0 = aligned(t * 256, 256)
            choose = column_hot(send_col[pl.ds(r0, 256), :], WIDE_SLOTS // 128)
            outs[j, pl.ds(r0, 256), :] = mm(choose, recv_r[j]).astype(BF16)

        for t in range(3):
            out_copy(j, t).start()

    wait_bytes(ids_buf.at[pl.ds(0, HEAD - 1)], ids_ss)
    wait_bytes(meta_r.at[:, pl.ds(0, SEQ - 1)], meta_ss)

    @pl.loop(0, HEADS)
    def _(j):
        wait_bytes(send_f.at[j, pl.ds(0, WIDE_SLOTS - WIDE)], fwd_ss.at[j])
        wait_bytes(send_r.at[j, pl.ds(0, WIDE_SLOTS - WIDE)], ret_ss.at[j])
        wait_bytes(tail.at[j], tail_ss.at[j])
        wait_bytes(lead_s.at[j], lead_ss.at[j])
        for t in range(3):
            out_copy(j, t).wait()


def call_kernel(args):
    hbm = pl.BlockSpec(memory_space=pl.ANY)
    near = pl.BlockSpec(memory_space=pltpu.VMEM)
    dma = pltpu.SemaphoreType.DMA
    grad = jax.ShapeDtypeStruct((ROWS, HEADS * HD), BF16)
    step = pltpu.VMEM((HEADS, EXTRA, 4 * HD), BF16)
    back = pltpu.VMEM((HEADS, EXTRA, 3 * HD), BF16)
    square = pltpu.VMEM((EXTRA, EXTRA), BF16)
    return pl.pallas_call(
        kernel,
        out_shape=(grad, grad, grad, jax.ShapeDtypeStruct((8, 128), F32)),
        in_specs=[near, hbm, hbm, hbm, hbm],
        out_specs=(hbm, hbm, hbm, near),
        scratch_shapes=[
            pltpu.VMEM((HEAD, 1, 128), I32),
            pltpu.VMEM((HEADS, ROWS, 4 * HD), BF16),
            pltpu.VMEM((HEADS, SLOTS, 4 * HD), BF16),
            pltpu.VMEM((HEADS, SLOTS, 4 * HD), BF16),
            pltpu.VMEM((NY, NZ, 1, 128), F32),
            pltpu.VMEM((NY, SEQ, 1, 128), F32),
            pltpu.VMEM((NZ, 128), F32),
            pltpu.VMEM((NY, NZ, 128), F32),
            pltpu.VMEM((8, 128), F32),
            pltpu.VMEM((NZ, 8, 128), F32),
            pltpu.VMEM((HEADS, ROWS, 4 * HD), BF16),
            pltpu.VMEM((HEADS, SPAN, 2 * HD), BF16),
            pltpu.VMEM((HEADS, SPAN, 2 * HD), BF16),
            pltpu.VMEM((HEADS, SPAN, 2 * HD), BF16),
            pltpu.VMEM((HEADS, ROWS, 3 * HD), BF16),
            pltpu.VMEM((HEADS, SLOTS, 3 * HD), BF16),
            pltpu.VMEM((HEADS, SLOTS, 3 * HD), BF16),
            pltpu.VMEM((HEADS, ROWS, HD), F32),
            pltpu.VMEM((HEADS, ROWS, HD), F32),
            pltpu.VMEM((128, DIRECT + 512), BF16),
            pltpu.VMEM((8, ROWS), I32),
            pltpu.VMEM((ROWS, 128), I32),
            pltpu.VMEM((HEADS, 8, SLOTS), I32),
            pltpu.VMEM((HEADS, SLOTS, 128), I32),
            pltpu.VMEM((NY, SEQ, 128), F32),
            square, square, square, square,
            step, step, step, step, back, back, back, back,
            dma((HEADS, 4)),
            dma((HEADS, 3)),
        ]
        + [dma] * 8
        + [dma((HEADS,))] * 20,
        compiler_params=pltpu.CompilerParams(
            collective_id=0, has_side_effects=True, vmem_limit_bytes=60 * 1024 * 1024
        ),
    )(*args)


def call_wide(args):
    hbm = pl.BlockSpec(memory_space=pl.ANY)
    dma = pltpu.SemaphoreType.DMA
    grad = jax.ShapeDtypeStruct((ROWS, HEADS * HD), BF16)
    return pl.pallas_call(
        wide_kernel,
        out_shape=(grad, grad, grad),
        in_specs=[pl.BlockSpec(memory_space=pltpu.VMEM), hbm, hbm, hbm, hbm],
        out_specs=(hbm, hbm, hbm),
        scratch_shapes=[
            pltpu.VMEM((HEAD, 1, 128), I32),
            pltpu.VMEM((HEADS, ROWS, 4 * HD), BF16),
            pltpu.VMEM((HEADS, WIDE_SLOTS, 4 * HD), BF16),
            pltpu.VMEM((HEADS, WIDE_SLOTS, 4 * HD), BF16),
            pltpu.VMEM((NY, NZ, 1, 128), F32),
            pltpu.VMEM((NY, SEQ, 1, 128), F32),
            pltpu.VMEM((HEADS, ROWS, 4 * HD), BF16),
            pltpu.VMEM((HEADS, SPAN, 2 * HD), BF16),
            pltpu.VMEM((HEADS, SPAN, 2 * HD), BF16),
            pltpu.VMEM((HEADS, SPAN, 2 * HD), BF16),
            pltpu.VMEM((HEADS, ROWS, 3 * HD), BF16),
            pltpu.VMEM((HEADS, WIDE_SLOTS, 3 * HD), BF16),
            pltpu.VMEM((HEADS, WIDE_SLOTS, 3 * HD), BF16),
            pltpu.VMEM((HEADS, ROWS, 3 * HD), BF16),
            pltpu.VMEM((HEADS, ROWS, HD), F32),
            pltpu.VMEM((HEADS, ROWS, HD), F32),
            pltpu.VMEM((128, WIDE_SLOTS), BF16),
            pltpu.VMEM((8, ROWS), I32),
            pltpu.VMEM((ROWS, 128), I32),
            pltpu.VMEM((HEADS, 8, WIDE_SLOTS), I32),
            pltpu.VMEM((HEADS, WIDE_SLOTS, 128), I32),
            dma((HEADS, 4)),
            dma((HEADS, 3)),
            dma, dma, dma, dma,
            dma((HEADS,)), dma((HEADS,)), dma((HEADS,)), dma((HEADS,)),
            dma((HEADS,)), dma((HEADS,)), dma((HEADS,)), dma((HEADS,)),
        ],
        compiler_params=pltpu.CompilerParams(
            collective_id=1, has_side_effects=True, vmem_limit_bytes=60 * 1024 * 1024
        ),
    )(*args)


def local(cluster_id, queries, key_vectors, value_vectors, grad_output):
    args = (cluster_id.reshape(1, 128), queries, key_vectors, value_vectors, grad_output)
    dq, dk, dv, flag = call_kernel(args)
    return lax.cond(
        flag[0, 0] > 0.5, lambda given, done: call_wide(given), lambda given, done: done,
        args, (dq, dk, dv),
    )


def solution(mesh):
    placed = (P(("seq", "head")),) + (P("seq", "head"),) * 4
    return jax.shard_map(
        local,
        mesh=mesh,
        in_specs=placed,
        out_specs=(P("seq", "head"),) * 3,
        check_vma=False,
    )
```

```python
import functools
import math

import jax
import jax.numpy as jnp
from jax import lax
from jax.experimental import pallas as pl
from jax.experimental.pallas import tpu as pltpu
from jax.sharding import PartitionSpec as P

MESH = pl.DeviceIdType.MESH
HD = 128
SPAN = 512
ROWS = 1024
SEQ = 32
HEAD = 8
NY = 4
NZ = 8
HEADS = 4
CAP = 32
DIRECT = SEQ * CAP
SIDE = 64
CROSS = 32
EXTRA = NY * SIDE
SLOTS = DIRECT + EXTRA
WIDE = 48
WIDE_SLOTS = SEQ * WIDE
QT = 256
FACTOR = 1.0 / math.sqrt(HD)
LOG2E = 1.4426950408889634
F32 = jnp.float32
BF16 = jnp.bfloat16
I32 = jnp.int32


def iota(shape, dim):
    return lax.broadcasted_iota(I32, shape, dim)


def onehot(mask):
    return jnp.where(mask, 1.0, 0.0).astype(BF16)


def mm(a, b):
    return jnp.dot(a, b, preferred_element_type=F32)


def mm_nt(a, b):
    return lax.dot_general(a, b, (((1,), (1,)), ((), ())), preferred_element_type=F32)


def aligned(value, size):
    return pl.multiple_of(value, size)


def column_hot(column, count):
    return jnp.concatenate(
        [onehot(column == iota((256, 128), 1) + 128 * c) for c in range(count)], axis=1
    )

def attend(rows, tail, grads, j, span, first):
    base = span * SPAN
    if span == 1:
        keys = rows[j, :, HD : 2 * HD]
        values = rows[j, :, 2 * HD : 3 * HD]
    else:
        keys = jnp.concatenate([tail[j, :, :HD], rows[j, :SPAN, HD : 2 * HD]], axis=0)
        values = jnp.concatenate([tail[j, :, HD:], rows[j, :SPAN, 2 * HD : 3 * HD]], axis=0)
    part_k = part_v = None
    for t in range(SPAN // QT):
        at = base + t * QT
        query = rows[j, at : at + QT, 0:HD]
        cot = rows[j, at : at + QT, 3 * HD : 4 * HD]
        scores = mm_nt(keys, query)
        if span == 0:
            gone = jnp.logical_and(iota((2 * SPAN, QT), 0) < SPAN, first)
            scores = jnp.where(gone, -jnp.inf, scores)
        top = jnp.max(scores, axis=0, keepdims=True)
        expo = jnp.exp2((scores - top) * (FACTOR * LOG2E))
        probs = expo * (1.0 / jnp.sum(expo, axis=0, keepdims=True))
        grad_probs = mm_nt(values, cot)
        delta = jnp.sum(probs * grad_probs, axis=0, keepdims=True)
        ds = (probs * (grad_probs - delta) * FACTOR).astype(BF16)
        pv = mm(probs.astype(BF16), cot)
        pk = mm(ds, query)
        part_k = pk if part_k is None else part_k + pk
        part_v = pv if part_v is None else part_v + pv
        dq = lax.dot_general(
            keys, ds, (((0,), (0,)), ((), ())), preferred_element_type=F32
        )
        grads[j, at : at + QT, 0:HD] = dq.T.astype(BF16)
    return part_k, part_v

def kernel(
    ids_ref, q_ref, k_ref, v_ref, g_ref, dq_ref, dk_ref, dv_ref, flag_ref,
    ids_buf, xin, send_f, recv_f, meta_s, meta_r, cnt_s, cnt_r, flag_s, flag_r, rows, tail,
    lead_s, lead_r, grads, send_r, recv_r, acc_k, acc_v, flat, send_row, send_col, pos_row,
    pos_col, spots, mb, mbt, mc, mct, a_r, b_s, b_r, c_s, cr_r, br_s, br_r, ar_s,
    in_sem, out_sem, ids_ss, ids_rs, meta_ss, meta_rs, cnt_ss, cnt_rs, flag_ss, flag_rs,
    fwd_ss, fwd_rs, ret_ss, ret_rs, tail_ss, tail_rs, lead_ss, lead_rs,
    a_ss, a_rs, b_ss, b_rs, c_ss, c_rs, cr_ss, cr_rs, br_ss, br_rs, ar_ss, ar_rs,
):
    me = lax.axis_index("seq")
    head = lax.axis_index("head")
    zi = me // NY
    yi = lax.rem(me, NY)

    def block_at(device, j):
        return (device // NY) * NY + lax.rem(lax.rem(device, NY) + NY - j, NY)

    def device_of(block, j):
        return (block // NY) * NY + lax.rem(lax.rem(block, NY) + j, NY)

    def peer(k):
        return lax.rem(me + k, SEQ)

    def remote(src, dst, ss, rs, seq, hd):
        return pltpu.make_async_remote_copy(
            src_ref=src, dst_ref=dst, send_sem=ss, recv_sem=rs,
            device_id=(seq, hd), device_id_type=MESH,
        )

    def wait_bytes(ref, sem):
        pltpu.make_async_copy(ref, ref, sem).wait()

    def in_copy(j, t):
        src = (q_ref, k_ref, v_ref, g_ref)[t]
        return pltpu.make_async_copy(
            src.at[:, pl.ds(aligned(j * HD, HD), HD)],
            xin.at[j, :, pl.ds(t * HD, HD)],
            in_sem.at[j, t],
        )

    def out_copy(j, t):
        dst = (dq_ref, dk_ref, dv_ref)[t]
        return pltpu.make_async_copy(
            xin.at[j, :, pl.ds(t * HD, HD)],
            dst.at[:, pl.ds(aligned(j * HD, HD), HD)],
            out_sem.at[j, t],
        )

    barrier = pltpu.get_barrier_semaphore()

    @pl.loop(1, SEQ)
    def _(k):
        pl.semaphore_signal(barrier, inc=1, device_id=(peer(k), head), device_id_type=MESH)

    @pl.loop(1, HEAD)
    def _(k):
        pl.semaphore_signal(
            barrier, inc=1, device_id=(me, lax.rem(head + k, HEAD)), device_id_type=MESH
        )

    @pl.loop(0, HEADS)
    def _(j):
        for t in range(4):
            in_copy(j, t).start()

    ids_buf[head] = ids_ref[...]
    pl.semaphore_wait(barrier, SEQ - 1 + HEAD - 1)

    @pl.loop(1, HEAD)
    def _(k):
        remote(
            ids_buf.at[head], ids_buf.at[head], ids_ss, ids_rs, me, lax.rem(head + k, HEAD)
        ).start()

    def slot_of(shape):
        col = iota(shape, 1)
        near = col < DIRECT
        past = col - DIRECT
        return (
            jnp.where(near, lax.shift_right_logical(col, 5), lax.shift_right_logical(past, 4)),
            jnp.where(near, col & 31, CAP + (past & 15)),
        )

    flat[...] = onehot(slot_of((128, DIRECT + 512))[1] == iota((128, DIRECT + 512), 0))
    upper = onehot(iota((128, 128), 0) < iota((128, 128), 1))
    sub = iota((SEQ, SEQ), 0)
    lan = iota((SEQ, SEQ), 1)
    below = onehot(lan < sub)
    below_z = onehot(
        jnp.logical_and(
            lan < sub, lax.shift_right_logical(lan, 2) == lax.shift_right_logical(sub, 2)
        )
    )
    row32 = iota((SEQ, 128), 0)
    row8 = iota((NZ, 128), 0)
    y_of = row32 & 3

    def quarter(value):
        return lax.shift_right_logical(value, 2)

    wait_bytes(ids_buf.at[pl.ds(0, HEAD - 1)], ids_rs)

    run = jnp.zeros((SEQ, 1), F32)
    owners, slots = [], []
    for c in range(ROWS // 128):
        owner = lax.shift_right_logical(ids_buf[c], 3)
        mine = jnp.where(row32 == owner, 1.0, 0.0)
        before = mm(mine.astype(BF16), upper) + run
        run = run + jnp.sum(mine, axis=1, keepdims=True)
        owners.append(owner)
        slots.append(jnp.sum(mine * before, axis=0, keepdims=True).astype(I32))

    past = jnp.maximum(jnp.broadcast_to(run, (SEQ, 128)) - float(CAP), 0.0)
    base_f = mm(below_z, past.astype(BF16))
    plane = onehot(quarter(iota((NZ, SEQ), 1)) == iota((NZ, SEQ), 0))
    cnt_s[...] = mm(plane, past.astype(BF16))
    cnt_r[yi] = cnt_s[...]

    @pl.loop(1, NY)
    def _(k):
        device = zi * NY + lax.rem(yi + k, NY)
        remote(cnt_s, cnt_r.at[yi], cnt_ss, cnt_rs, device, head).start()

    mine_e = cnt_s[...].astype(I32)
    offs = []
    for yy in range(NY):
        count = quarter(mine_e - ((yy - yi - row8 + 16) & 3) + 3).astype(F32)
        off = jnp.zeros((SEQ, 128), F32)
        for z in range(NZ - 1):
            off = off + jnp.where(quarter(row32) > z, count[z : z + 1, :], 0.0)
        offs.append(off)
    for c in range(ROWS // 128):
        owner, slot = owners[c], slots[c]
        mine = row32 == owner

        def pick(table):
            return jnp.sum(jnp.where(mine, table, 0.0), axis=0, keepdims=True).astype(I32)

        e = pick(base_f) + slot - CAP
        way = (e + yi + quarter(owner) + 64) & 3
        far = DIRECT + way * SIDE + quarter(e + 64) - 16
        for yy in range(NY):
            far = far + jnp.where(way == yy, pick(offs[yy]), 0)
        index = jnp.where(slot < CAP, owner * CAP + slot, far)
        send_row[:, c * 128 : (c + 1) * 128] = jnp.broadcast_to(index, (8, 128))

    def pack_tile(j, r0):
        choose = onehot(send_row[0:1, :] == iota((256, ROWS), 0) + r0)
        send_f[j, pl.ds(r0, 256), :] = mm(choose, xin[j]).astype(BF16)

    def y_peer(k):
        return lax.rem(yi + k, NY)

    def z_peer(k):
        return lax.rem(zi + k, NZ)

    def at_side(y):
        return pl.ds(aligned(y * SIDE, SIDE), SIDE)

    def at_cross(z):
        return pl.ds(aligned(z * CROSS, CROSS), CROSS)

    def at_extra(y):
        return pl.ds(aligned(DIRECT + y * SIDE, SIDE), SIDE)

    def stage_a(j):
        for t in range(4):
            in_copy(j, t).wait()
        pack_tile(j, DIRECT)

        @pl.loop(1, NY)
        def _(k):
            y = y_peer(k)
            remote(
                send_f.at[j, at_extra(y)], a_r.at[j, at_side(yi)], a_ss.at[j], a_rs.at[j],
                zi * NY + y, head,
            ).start()

        a_r[j, at_side(yi), :] = send_f[j, at_extra(yi), :]

    def stage_b(j):
        wait_bytes(a_r.at[j, pl.ds(0, EXTRA - SIDE)], a_rs.at[j])
        b_s[j] = mm(mb[...], a_r[j]).astype(BF16)

        @pl.loop(1, NZ)
        def _(k):
            z = z_peer(k)
            remote(
                b_s.at[j, at_cross(z)], b_r.at[j, at_cross(zi)], b_ss.at[j], b_rs.at[j],
                z * NY + yi, head,
            ).start()

        b_r[j, at_cross(zi), :] = b_s[j, at_cross(zi), :]

    def stage_c(j):
        wait_bytes(b_r.at[j, pl.ds(0, EXTRA - CROSS)], b_rs.at[j])
        c_s[j] = mm(mc[...], b_r[j]).astype(BF16)

        @pl.loop(1, NY)
        def _(k):
            y = y_peer(k)
            remote(
                c_s.at[j, at_side(lax.rem(y + NY - j, NY))], recv_f.at[j, at_extra(yi)],
                c_ss.at[j], c_rs.at[j], zi * NY + y, head,
            ).start()

        recv_f[j, at_extra(yi), :] = c_s[j, at_side(lax.rem(yi + NY - j, NY)), :]

    def pack_forward(j):
        @pl.loop(0, DIRECT // 256)
        def _(t):
            tile = lax.rem(zi // 2 + t, DIRECT // 256)
            pack_tile(j, aligned(tile * 256, 256))

            @pl.loop(0, 256 // CAP)
            def _(k):
                block = tile * (256 // CAP) + lax.rem(me + k, 256 // CAP)
                device = device_of(block, j)
                source = aligned(block * CAP, CAP)

                @pl.when(device != me)
                def _():
                    remote(
                        send_f.at[j, pl.ds(source, CAP)],
                        recv_f.at[j, pl.ds(aligned(me * CAP, CAP), CAP)],
                        fwd_ss.at[j], fwd_rs.at[j], device, head,
                    ).start()

        own = aligned(block_at(me, j) * CAP, CAP)
        recv_f[j, pl.ds(aligned(me * CAP, CAP), CAP), :] = send_f[j, pl.ds(own, CAP), :]

    stage_a(0)
    pack_forward(0)

    @pl.loop(1, HEADS)
    def _(j):
        stage_a(j)

    meta = jnp.zeros((SEQ, 128), F32)
    for c in range(ROWS // 128):
        cluster = (ids_buf[c] & 7).astype(F32) + 1.0
        mine = jnp.where(row32 == owners[c], cluster, 0.0)
        meta = meta + mm_nt(mine.astype(BF16), onehot(iota((128, 128), 0) == slots[c]))
    for b in range(SEQ):
        meta_s[b % NY, b // NY] = meta[b : b + 1, :]

    @pl.loop(1, SEQ)
    def _(k):
        device = peer(k)
        remote(
            meta_s.at[:, device // NY], meta_r.at[:, me], meta_ss, meta_rs, device, head
        ).start()

    for b in range(NY):
        meta_r[b, me] = meta_s[b, zi]
    wait_bytes(cnt_r.at[pl.ds(0, NY - 1)], cnt_rs)

    bad = jnp.zeros((1, 128), F32)
    starts_a, starts_b, counts = [], [], []
    filled = jnp.zeros((NZ, 128), I32)
    for y in range(NY):
        for yy in range(NY):
            share = quarter(cnt_r[y].astype(I32) - ((yy - y - row8 + 16) & 3) + 3)
            total = jnp.sum(share.astype(F32), axis=0, keepdims=True)
            bad = jnp.maximum(bad, total - float(SIDE))
        share = quarter(cnt_r[y].astype(I32) - ((yi - y - row8 + 16) & 3) + 3)
        start = jnp.zeros((NZ, 128), I32)
        for z in range(NZ - 1):
            start = start + jnp.where(row8 > z, share[z : z + 1, :], 0)
        starts_a.append(start)
        starts_b.append(filled)
        counts.append(share)
        filled = filled + share
    for yy in range(NY):
        total = jnp.zeros((NZ, 128), I32)
        for y in range(NY):
            total = total + quarter(cnt_r[y].astype(I32) - ((yy - y - row8 + 16) & 3) + 3)
        bad = jnp.maximum(
            bad, jnp.max(total.astype(F32), axis=0, keepdims=True) - float(CROSS)
        )

    def by_group(tables):
        group = lax.shift_right_logical(iota((NZ, EXTRA), 1), 6)
        result = jnp.zeros((NZ, EXTRA), I32)
        for y in range(NY):
            result = jnp.where(group == y, jnp.concatenate([tables[y]] * 2, axis=1), result)
        return result

    wide_a, wide_b, wide_c = by_group(starts_a), by_group(starts_b), by_group(counts)
    for z in range(NZ):
        step = iota((CROSS, EXTRA), 0) - wide_b[z : z + 1, :]
        place = (iota((CROSS, EXTRA), 1) & (SIDE - 1)) - wide_a[z : z + 1, :]
        hit = jnp.logical_and(
            jnp.logical_and(step >= 0, step < wide_c[z : z + 1, :]), step == place
        )
        mb[z * CROSS : (z + 1) * CROSS, :] = onehot(hit)
    mbt[...] = mb[...].astype(F32).T.astype(BF16)

    stage_b(0)
    pack_forward(1)

    @pl.loop(1, HEADS)
    def _(j):
        stage_b(j)

    for c in range(ROWS // 128):
        send_col[c * 128 : (c + 1) * 128, :] = (
            jnp.broadcast_to(send_row[0:1, c * 128 : (c + 1) * 128], (128, 128))
            .astype(F32).T.astype(I32)
        )
    wait_bytes(meta_r.at[:, pl.ds(0, SEQ - 1)], meta_rs)

    bases = [jnp.zeros((SEQ, 128), I32)]
    for b in range(NY):
        held = jnp.where(meta_r[b].reshape(SEQ, 128) > 0.5, 1.0, 0.0)
        held = jnp.maximum(jnp.sum(held, axis=1, keepdims=True) - float(CAP), 0.0)
        bases.append(bases[b] + jnp.broadcast_to(held, (SEQ, 128)).astype(I32))
    firsts = []
    for yy in range(NY):
        residue = (yy - y_of - zi + 16) & 3
        firsts.append([quarter(base - residue + 3) for base in bases])
    lengths = [[f[b + 1] - f[b] for b in range(NY)] for f in firsts]
    stacked = jnp.concatenate([v.astype(F32) for f in lengths for v in f], axis=1)
    before_c = mm(below, stacked.astype(BF16))
    landing = []
    for yy in range(NY):
        landing.append([])
        for b in range(NY):
            at = (yy * NY + b) * 128
            part = before_c[:, at : at + 128].astype(I32)
            landing[yy].append(part)
            total = (part + lengths[yy][b])[SEQ - 1 : SEQ, :].astype(F32)
            bad = jnp.maximum(bad, total - float(SIDE))
    lane = iota((SEQ, 128), 1)
    for b in range(NY):
        e = bases[b] + lane - CAP
        way = (e + y_of + zi + 64) & 3
        spot = jnp.zeros((SEQ, 128), I32)
        for yy in range(NY):
            here = yy * SIDE + landing[yy][b] + quarter(e + 64) - 16 - firsts[yy][b]
            spot = jnp.where(way == yy, here, spot)
        used = jnp.logical_and(meta_r[b].reshape(SEQ, 128) > 0.5, lane >= CAP)
        spots[b] = jnp.where(used, spot.astype(F32), -1.0)

    def chosen(tables):
        result = tables[0]
        for yy in range(1, NY):
            result = jnp.where(yi == yy, tables[yy], result)
        return result

    my_total = chosen([f[NY] for f in firsts])
    my_start = mm(below_z, my_total.astype(F32).astype(BF16))
    col = iota((SEQ, EXTRA), 1)
    for b in range(NY):
        landing_b = chosen([landing[yy][b] for yy in range(NY)]).astype(F32)
        length_b = chosen([lengths[yy][b] for yy in range(NY)]).astype(F32)
        source_b = my_start + chosen([firsts[yy][b] for yy in range(NY)]).astype(F32)
        found = jnp.zeros((SIDE, EXTRA), F32)
        for y in range(NY):
            match = iota((SEQ, EXTRA), 0) == lax.shift_right_logical(col, 5) * NY + y

            def across(table):
                twice = jnp.concatenate([table, table], axis=1)
                return jnp.sum(jnp.where(match, twice, 0.0), axis=0, keepdims=True).astype(I32)

            step = iota((SIDE, EXTRA), 0) - across(landing_b)
            place = (iota((SIDE, EXTRA), 1) & (CROSS - 1)) - across(source_b)
            hit = jnp.logical_and(
                jnp.logical_and(step >= 0, step < across(length_b)), step == place
            )
            found = found + jnp.where(hit, 1.0, 0.0)
        mc[b * SIDE : (b + 1) * SIDE, :] = found.astype(BF16)
    mct[...] = mc[...].astype(F32).T.astype(BF16)

    flag_s[...] = jnp.broadcast_to(jnp.where(bad > 0.5, 1.0, 0.0), (8, 128))
    flag_r[zi] = flag_s[...]

    @pl.loop(1, NZ)
    def _(k):
        remote(
            flag_s, flag_r.at[zi], flag_ss, flag_rs, z_peer(k) * NY + yi, head
        ).start()

    stage_c(0)

    def positions(j):
        block = lax.rem(yi + NY - j, NY)
        m = meta_r[block].reshape(SEQ, 128)
        hot = jnp.concatenate([jnp.where(m == c + 1.0, 1.0, 0.0) for c in range(8)], axis=0)
        within = mm(hot.astype(BF16), upper)
        total = jnp.broadcast_to(jnp.sum(hot, axis=1, keepdims=True), (8 * SEQ, 128))
        lower = onehot(iota((8 * SEQ, 8 * SEQ), 1) < iota((8 * SEQ, 8 * SEQ), 0))
        placed = hot * (mm(lower, total.astype(BF16)) + within)
        pos = jnp.where(m > 0.5, 0.0, -1.0)
        for c in range(8):
            pos = pos + placed[c * SEQ : (c + 1) * SEQ, :]

        def halves(value):
            high = jnp.floor(value * (1.0 / 32.0))
            return [high, value - high * 32.0]

        parts = mm(
            jnp.concatenate(halves(pos) + halves(spots[block]), axis=0).astype(BF16), flat[...]
        )
        mine = iota((SEQ, DIRECT + 512), 0) == slot_of((SEQ, DIRECT + 512))[0]
        spread = jnp.where(mine, parts[:SEQ] * 32.0 + parts[SEQ : 2 * SEQ], 0.0)
        line = jnp.sum(spread, axis=0, keepdims=True)
        spread = jnp.where(mine, parts[2 * SEQ : 3 * SEQ] * 32.0 + parts[3 * SEQ :], 0.0)
        target = jnp.sum(spread, axis=0, keepdims=True)[:, DIRECT:].astype(I32)
        high, low = halves(line[:, DIRECT:] + 1.0)
        pair = jnp.concatenate(
            [jnp.broadcast_to(high, (8, 512)), jnp.broadcast_to(low, (8, 512))], axis=0
        )
        found = mm_nt(pair.astype(BF16), onehot(iota((EXTRA, 512), 0) == target))
        extra = found[0:1, :] * 32.0 + found[8:9, :] - 1.0
        row = jnp.concatenate([line[:, :DIRECT], extra], axis=1)
        pos_row[j] = jnp.broadcast_to(row, (8, SLOTS)).astype(I32)
        for c in range(SLOTS // 128):
            piece = row[:, c * 128 : (c + 1) * 128]
            pos_col[j, c * 128 : (c + 1) * 128, :] = (
                jnp.broadcast_to(piece, (128, 128)).T.astype(I32)
            )

    def tail_copy(j):
        after = device_of(lax.rem(block_at(me, j) + 1, SEQ), j)
        return remote(
            rows.at[j, pl.ds(SPAN, SPAN), pl.ds(HD, 2 * HD)], tail.at[j],
            tail_ss.at[j], tail_rs.at[j], after, head,
        )

    def lead_copy(j):
        prior = device_of(lax.rem(block_at(me, j) + SEQ - 1, SEQ), j)
        return remote(lead_s.at[j], lead_r.at[j], lead_ss.at[j], lead_rs.at[j], prior, head)

    def open_chunk(j):
        positions(j)
        wait_bytes(recv_f.at[j, pl.ds(0, DIRECT - CAP)], fwd_rs.at[j])
        wait_bytes(recv_f.at[j, pl.ds(0, EXTRA - SIDE)], c_rs.at[j])

        @pl.loop(0, ROWS // 256)
        def _(t):
            r0 = aligned(t * 256, 256)
            choose = onehot(pos_row[j, 0:1, :] == iota((256, SLOTS), 0) + r0)
            rows[j, pl.ds(r0, 256), :] = mm(choose, recv_f[j]).astype(BF16)

        tail_copy(j).start()

    def last_span(j):
        part_k, part_v = attend(rows, tail, grads, j, 1, block_at(me, j) == 0)
        acc_k[j] = part_k
        acc_v[j] = part_v

    def first_span(j):
        tail_copy(j).wait_recv()
        part_k, part_v = attend(rows, tail, grads, j, 0, block_at(me, j) == 0)
        lead_s[j, :, :HD] = part_k[:SPAN].astype(BF16)
        lead_s[j, :, HD:] = part_v[:SPAN].astype(BF16)
        lead_copy(j).start()
        grads[j, :SPAN, HD : 2 * HD] = (acc_k[j, :SPAN] + part_k[SPAN:]).astype(BF16)
        grads[j, :SPAN, 2 * HD :] = (acc_v[j, :SPAN] + part_v[SPAN:]).astype(BF16)

    def close_chunk(j):
        lead_copy(j).wait_recv()
        grads[j, SPAN:, HD : 2 * HD] = (
            acc_k[j, SPAN:] + lead_r[j, :, :HD].astype(F32)
        ).astype(BF16)
        grads[j, SPAN:, 2 * HD :] = (
            acc_v[j, SPAN:] + lead_r[j, :, HD:].astype(F32)
        ).astype(BF16)

        def pack_back(r0):
            choose = column_hot(pos_col[j, pl.ds(r0, 256), :], ROWS // 128)
            send_r[j, pl.ds(r0, 256), :] = mm(choose, grads[j]).astype(BF16)

        pack_back(DIRECT)
        own_y = lax.rem(yi + NY - j, NY)

        @pl.loop(1, NY)
        def _(k):
            y = y_peer(k)
            remote(
                send_r.at[j, at_extra(y)], cr_r.at[j, at_side(own_y)], cr_ss.at[j],
                cr_rs.at[j], zi * NY + y, head,
            ).start()

        cr_r[j, at_side(own_y), :] = send_r[j, at_extra(yi), :]

        @pl.loop(0, DIRECT // 256)
        def _(t):
            pack_back(aligned(t * 256, 256))

        own = aligned(block_at(me, j) * CAP, CAP)

        @pl.loop(1, SEQ)
        def _(k):
            device = peer(k)
            remote(
                send_r.at[j, pl.ds(aligned(device * CAP, CAP), CAP)],
                recv_r.at[j, pl.ds(own, CAP)],
                ret_ss.at[j], ret_rs.at[j], device, head,
            ).start()

        recv_r[j, pl.ds(own, CAP), :] = send_r[j, pl.ds(aligned(me * CAP, CAP), CAP), :]

    def back_b(j):
        wait_bytes(cr_r.at[j, pl.ds(0, EXTRA - SIDE)], cr_rs.at[j])
        br_s[j] = mm(mct[...], cr_r[j]).astype(BF16)

        @pl.loop(1, NZ)
        def _(k):
            z = z_peer(k)
            remote(
                br_s.at[j, at_cross(z)], br_r.at[j, at_cross(zi)], br_ss.at[j], br_rs.at[j],
                z * NY + yi, head,
            ).start()

        br_r[j, at_cross(zi), :] = br_s[j, at_cross(zi), :]

    def back_a(j):
        wait_bytes(br_r.at[j, pl.ds(0, EXTRA - CROSS)], br_rs.at[j])
        ar_s[j] = mm(mbt[...], br_r[j]).astype(BF16)

        @pl.loop(1, NY)
        def _(k):
            y = y_peer(k)
            remote(
                ar_s.at[j, at_side(y)], recv_r.at[j, at_extra(yi)], ar_ss.at[j], ar_rs.at[j],
                zi * NY + y, head,
            ).start()

        recv_r[j, at_extra(yi), :] = ar_s[j, at_side(yi), :]

    @pl.loop(0, HEADS + 4)
    def _(i):
        @pl.when(i < HEADS)
        def _():
            open_chunk(i)

        @pl.when(jnp.logical_and(i >= 1, i <= HEADS))
        def _():
            first_span(i - 1)

        @pl.when(i < 1)
        def _():
            stage_c(1)

        @pl.when(i < HEADS - 2)
        def _():
            pack_forward(i + 2)
            stage_c(i + 2)

        @pl.when(i < HEADS)
        def _():
            last_span(i)

        @pl.when(jnp.logical_and(i >= 2, i < HEADS + 2))
        def _():
            close_chunk(i - 2)

        @pl.when(jnp.logical_and(i >= 3, i < HEADS + 3))
        def _():
            back_b(i - 3)

        @pl.when(i >= 4)
        def _():
            back_a(i - 4)

    @pl.loop(0, HEADS)
    def _(j):
        wait_bytes(recv_r.at[j, pl.ds(0, DIRECT - CAP)], ret_rs.at[j])
        wait_bytes(recv_r.at[j, pl.ds(0, EXTRA - SIDE)], ar_rs.at[j])

        @pl.loop(0, ROWS // 256)
        def _(t):
            r0 = aligned(t * 256, 256)
            choose = column_hot(send_col[pl.ds(r0, 256), :], SLOTS // 128)
            xin[j, pl.ds(r0, 256), : 3 * HD] = mm(choose, recv_r[j]).astype(BF16)

        for t in range(3):
            out_copy(j, t).start()

    wait_bytes(flag_r.at[pl.ds(0, NZ - 1)], flag_rs)
    flag_ref[0, 0] = jnp.max(flag_r[...])
    wait_bytes(ids_buf.at[pl.ds(0, HEAD - 1)], ids_ss)
    wait_bytes(meta_r.at[:, pl.ds(0, SEQ - 1)], meta_ss)
    wait_bytes(cnt_r.at[pl.ds(0, NY - 1)], cnt_ss)
    wait_bytes(flag_r.at[pl.ds(0, NZ - 1)], flag_ss)

    @pl.loop(0, HEADS)
    def _(j):
        wait_bytes(send_f.at[j, pl.ds(0, DIRECT - CAP)], fwd_ss.at[j])
        wait_bytes(send_r.at[j, pl.ds(0, DIRECT - CAP)], ret_ss.at[j])
        wait_bytes(a_r.at[j, pl.ds(0, EXTRA - SIDE)], a_ss.at[j])
        wait_bytes(b_r.at[j, pl.ds(0, EXTRA - CROSS)], b_ss.at[j])
        wait_bytes(c_s.at[j, pl.ds(0, EXTRA - SIDE)], c_ss.at[j])
        wait_bytes(cr_r.at[j, pl.ds(0, EXTRA - SIDE)], cr_ss.at[j])
        wait_bytes(br_r.at[j, pl.ds(0, EXTRA - CROSS)], br_ss.at[j])
        wait_bytes(ar_s.at[j, pl.ds(0, EXTRA - SIDE)], ar_ss.at[j])
        wait_bytes(tail.at[j], tail_ss.at[j])
        wait_bytes(lead_s.at[j], lead_ss.at[j])
        for t in range(3):
            out_copy(j, t).wait()


def wide_kernel(
    ids_ref, q_ref, k_ref, v_ref, g_ref, dq_ref, dk_ref, dv_ref,
    ids_buf, xin, send_f, recv_f, meta_s, meta_r, rows, tail, lead_s, lead_r,
    grads, send_r, recv_r, outs, acc_k, acc_v, flat, send_row, send_col, pos_row, pos_col,
    in_sem, out_sem, ids_ss, ids_rs, meta_ss, meta_rs, fwd_ss, fwd_rs, ret_ss, ret_rs,
    tail_ss, tail_rs, lead_ss, lead_rs,
):
    me = lax.axis_index("seq")
    head = lax.axis_index("head")
    zi = me // NY
    yi = lax.rem(me, NY)

    def block_at(device, j):
        return (device // NY) * NY + lax.rem(lax.rem(device, NY) + NY - j, NY)

    def device_of(block, j):
        return (block // NY) * NY + lax.rem(lax.rem(block, NY) + j, NY)

    def peer(k):
        return lax.rem(me + k, SEQ)

    def remote(src, dst, ss, rs, seq, hd):
        return pltpu.make_async_remote_copy(
            src_ref=src, dst_ref=dst, send_sem=ss, recv_sem=rs,
            device_id=(seq, hd), device_id_type=MESH,
        )

    def wait_bytes(ref, sem):
        pltpu.make_async_copy(ref, ref, sem).wait()

    def in_copy(j, t):
        src = (q_ref, k_ref, v_ref, g_ref)[t]
        return pltpu.make_async_copy(
            src.at[:, pl.ds(aligned(j * HD, HD), HD)],
            xin.at[j, :, pl.ds(t * HD, HD)],
            in_sem.at[j, t],
        )

    def out_copy(j, t):
        dst = (dq_ref, dk_ref, dv_ref)[t]
        return pltpu.make_async_copy(
            outs.at[j, :, pl.ds(t * HD, HD)],
            dst.at[:, pl.ds(aligned(j * HD, HD), HD)],
            out_sem.at[j, t],
        )

    barrier = pltpu.get_barrier_semaphore()

    @pl.loop(1, SEQ)
    def _(k):
        pl.semaphore_signal(barrier, inc=1, device_id=(peer(k), head), device_id_type=MESH)

    @pl.loop(1, HEAD)
    def _(k):
        pl.semaphore_signal(
            barrier, inc=1, device_id=(me, lax.rem(head + k, HEAD)), device_id_type=MESH
        )

    @pl.loop(0, HEADS)
    def _(j):
        for t in range(4):
            in_copy(j, t).start()

    ids_buf[head] = ids_ref[...]
    pl.semaphore_wait(barrier, SEQ - 1 + HEAD - 1)

    @pl.loop(1, HEAD)
    def _(k):
        remote(
            ids_buf.at[head], ids_buf.at[head], ids_ss, ids_rs, me, lax.rem(head + k, HEAD)
        ).start()

    lane = iota((128, WIDE_SLOTS), 1)
    source_of = lax.shift_right_logical(lane * 1366, 16)
    flat[...] = onehot(lane - source_of * WIDE == iota((128, WIDE_SLOTS), 0))
    upper = onehot(iota((128, 128), 0) < iota((128, 128), 1))
    wait_bytes(ids_buf.at[pl.ds(0, HEAD - 1)], ids_rs)

    run = jnp.zeros((SEQ, 1), F32)
    meta = jnp.zeros((SEQ, 128), F32)
    for c in range(ROWS // 128):
        idc = ids_buf[c]
        owner = lax.shift_right_logical(idc, 3)
        cluster = (idc & 7).astype(F32) + 1.0
        mine = jnp.where(iota((SEQ, 128), 0) == owner, 1.0, 0.0)
        before = mm(mine.astype(BF16), upper) + run
        run = run + jnp.sum(mine, axis=1, keepdims=True)
        slot = jnp.sum(mine * before, axis=0, keepdims=True).astype(I32)
        index = owner * WIDE + slot
        send_row[:, c * 128 : (c + 1) * 128] = jnp.broadcast_to(index, (8, 128))
        send_col[c * 128 : (c + 1) * 128, :] = (
            jnp.broadcast_to(index, (128, 128)).astype(F32).T.astype(I32)
        )
        meta = meta + mm_nt((mine * cluster).astype(BF16), onehot(iota((128, 128), 0) == slot))
    for b in range(SEQ):
        meta_s[b % NY, b // NY] = meta[b : b + 1, :]

    @pl.loop(1, SEQ)
    def _(k):
        device = peer(k)
        remote(
            meta_s.at[:, device // NY], meta_r.at[:, me], meta_ss, meta_rs, device, head
        ).start()

    for b in range(NY):
        meta_r[b, me] = meta_s[b, zi]

    def pack_forward(j):
        for t in range(4):
            in_copy(j, t).wait()

        @pl.loop(0, WIDE_SLOTS // 256)
        def _(t):
            r0 = aligned(t * 256, 256)
            choose = onehot(send_row[0:1, :] == iota((256, ROWS), 0) + r0)
            send_f[j, pl.ds(r0, 256), :] = mm(choose, xin[j]).astype(BF16)

        @pl.loop(1, SEQ)
        def _(k):
            device = peer(k)
            start = aligned(block_at(device, j) * WIDE, WIDE)
            remote(
                send_f.at[j, pl.ds(start, WIDE)],
                recv_f.at[j, pl.ds(aligned(me * WIDE, WIDE), WIDE)],
                fwd_ss.at[j], fwd_rs.at[j], device, head,
            ).start()

        own = aligned(block_at(me, j) * WIDE, WIDE)
        recv_f[j, pl.ds(aligned(me * WIDE, WIDE), WIDE), :] = send_f[j, pl.ds(own, WIDE), :]

    @pl.loop(0, 2)
    def _(j):
        pack_forward(j)

    wait_bytes(meta_r.at[:, pl.ds(0, SEQ - 1)], meta_rs)

    def positions(j):
        m = meta_r[lax.rem(yi + NY - j, NY)].reshape(SEQ, 128)
        hot = jnp.concatenate([jnp.where(m == c + 1.0, 1.0, 0.0) for c in range(8)], axis=0)
        within = mm(hot.astype(BF16), upper)
        total = jnp.broadcast_to(jnp.sum(hot, axis=1, keepdims=True), (8 * SEQ, 128))
        lower = onehot(iota((8 * SEQ, 8 * SEQ), 1) < iota((8 * SEQ, 8 * SEQ), 0))
        placed = hot * (mm(lower, total.astype(BF16)) + within)
        pos = jnp.where(m > 0.5, 0.0, -1.0)
        for c in range(8):
            pos = pos + placed[c * SEQ : (c + 1) * SEQ, :]
        high = jnp.floor(pos * (1.0 / 32.0))
        low = pos - high * 32.0
        parts = mm(jnp.concatenate([high, low], axis=0).astype(BF16), flat[...])
        spread = parts[:SEQ] * 32.0 + parts[SEQ:]
        mine = iota((SEQ, WIDE_SLOTS), 0) == lax.shift_right_logical(iota((SEQ, WIDE_SLOTS), 1) * 1366, 16)
        row = jnp.sum(jnp.where(mine, spread, 0.0), axis=0, keepdims=True)
        pos_row[j] = jnp.broadcast_to(row, (8, WIDE_SLOTS)).astype(I32)
        for c in range(WIDE_SLOTS // 128):
            piece = row[:, c * 128 : (c + 1) * 128]
            pos_col[j, c * 128 : (c + 1) * 128, :] = (
                jnp.broadcast_to(piece, (128, 128)).T.astype(I32)
            )

    def tail_copy(j):
        after = device_of(lax.rem(block_at(me, j) + 1, SEQ), j)
        return remote(
            rows.at[j, pl.ds(SPAN, SPAN), pl.ds(HD, 2 * HD)], tail.at[j],
            tail_ss.at[j], tail_rs.at[j], after, head,
        )

    def lead_copy(j):
        prior = device_of(lax.rem(block_at(me, j) + SEQ - 1, SEQ), j)
        return remote(lead_s.at[j], lead_r.at[j], lead_ss.at[j], lead_rs.at[j], prior, head)

    def open_chunk(j):
        positions(j)
        wait_bytes(recv_f.at[j, pl.ds(0, WIDE_SLOTS - WIDE)], fwd_rs.at[j])

        @pl.loop(0, ROWS // 256)
        def _(t):
            r0 = aligned(t * 256, 256)
            choose = onehot(pos_row[j, 0:1, :] == iota((256, WIDE_SLOTS), 0) + r0)
            rows[j, pl.ds(r0, 256), :] = mm(choose, recv_f[j]).astype(BF16)

        tail_copy(j).start()

    def last_span(j):
        part_k, part_v = attend(rows, tail, grads, j, 1, block_at(me, j) == 0)
        acc_k[j] = part_k
        acc_v[j] = part_v

    def first_span(j):
        tail_copy(j).wait_recv()
        part_k, part_v = attend(rows, tail, grads, j, 0, block_at(me, j) == 0)
        lead_s[j, :, :HD] = part_k[:SPAN].astype(BF16)
        lead_s[j, :, HD:] = part_v[:SPAN].astype(BF16)
        lead_copy(j).start()
        grads[j, :SPAN, HD : 2 * HD] = (acc_k[j, :SPAN] + part_k[SPAN:]).astype(BF16)
        grads[j, :SPAN, 2 * HD :] = (acc_v[j, :SPAN] + part_v[SPAN:]).astype(BF16)

    def close_chunk(j):
        lead_copy(j).wait_recv()
        grads[j, SPAN:, HD : 2 * HD] = (
            acc_k[j, SPAN:] + lead_r[j, :, :HD].astype(F32)
        ).astype(BF16)
        grads[j, SPAN:, 2 * HD :] = (
            acc_v[j, SPAN:] + lead_r[j, :, HD:].astype(F32)
        ).astype(BF16)

        @pl.loop(0, WIDE_SLOTS // 256)
        def _(t):
            r0 = aligned(t * 256, 256)
            choose = column_hot(pos_col[j, pl.ds(r0, 256), :], ROWS // 128)
            send_r[j, pl.ds(r0, 256), :] = mm(choose, grads[j]).astype(BF16)

        own = aligned(block_at(me, j) * WIDE, WIDE)

        @pl.loop(1, SEQ)
        def _(k):
            device = peer(k)
            remote(
                send_r.at[j, pl.ds(aligned(device * WIDE, WIDE), WIDE)],
                recv_r.at[j, pl.ds(own, WIDE)],
                ret_ss.at[j], ret_rs.at[j], device, head,
            ).start()

        recv_r[j, pl.ds(own, WIDE), :] = send_r[j, pl.ds(aligned(me * WIDE, WIDE), WIDE), :]

    @pl.loop(0, HEADS + 2)
    def _(i):
        @pl.when(i < HEADS)
        def _():
            open_chunk(i)

        @pl.when(i < HEADS - 2)
        def _():
            pack_forward(i + 2)

        @pl.when(jnp.logical_and(i >= 1, i <= HEADS))
        def _():
            first_span(i - 1)

        @pl.when(i < HEADS)
        def _():
            last_span(i)

        @pl.when(i >= 2)
        def _():
            close_chunk(i - 2)

    @pl.loop(0, HEADS)
    def _(j):
        wait_bytes(recv_r.at[j, pl.ds(0, WIDE_SLOTS - WIDE)], ret_rs.at[j])

        @pl.loop(0, ROWS // 256)
        def _(t):
            r0 = aligned(t * 256, 256)
            choose = column_hot(send_col[pl.ds(r0, 256), :], WIDE_SLOTS // 128)
            outs[j, pl.ds(r0, 256), :] = mm(choose, recv_r[j]).astype(BF16)

        for t in range(3):
            out_copy(j, t).start()

    wait_bytes(ids_buf.at[pl.ds(0, HEAD - 1)], ids_ss)
    wait_bytes(meta_r.at[:, pl.ds(0, SEQ - 1)], meta_ss)

    @pl.loop(0, HEADS)
    def _(j):
        wait_bytes(send_f.at[j, pl.ds(0, WIDE_SLOTS - WIDE)], fwd_ss.at[j])
        wait_bytes(send_r.at[j, pl.ds(0, WIDE_SLOTS - WIDE)], ret_ss.at[j])
        wait_bytes(tail.at[j], tail_ss.at[j])
        wait_bytes(lead_s.at[j], lead_ss.at[j])
        for t in range(3):
            out_copy(j, t).wait()


def call_kernel(args):
    hbm = pl.BlockSpec(memory_space=pl.ANY)
    near = pl.BlockSpec(memory_space=pltpu.VMEM)
    dma = pltpu.SemaphoreType.DMA
    grad = jax.ShapeDtypeStruct((ROWS, HEADS * HD), BF16)
    step = pltpu.VMEM((HEADS, EXTRA, 4 * HD), BF16)
    back = pltpu.VMEM((HEADS, EXTRA, 3 * HD), BF16)
    square = pltpu.VMEM((EXTRA, EXTRA), BF16)
    return pl.pallas_call(
        kernel,
        out_shape=(grad, grad, grad, jax.ShapeDtypeStruct((1, 1), F32)),
        in_specs=[near, hbm, hbm, hbm, hbm],
        out_specs=(hbm, hbm, hbm, pl.BlockSpec(memory_space=pltpu.SMEM)),
        scratch_shapes=[
            pltpu.VMEM((HEAD, 1, 128), I32),
            pltpu.VMEM((HEADS, ROWS, 4 * HD), BF16),
            pltpu.VMEM((HEADS, SLOTS, 4 * HD), BF16),
            pltpu.VMEM((HEADS, SLOTS, 4 * HD), BF16),
            pltpu.VMEM((NY, NZ, 1, 128), F32),
            pltpu.VMEM((NY, SEQ, 1, 128), F32),
            pltpu.VMEM((NZ, 128), F32),
            pltpu.VMEM((NY, NZ, 128), F32),
            pltpu.VMEM((8, 128), F32),
            pltpu.VMEM((NZ, 8, 128), F32),
            pltpu.VMEM((HEADS, ROWS, 4 * HD), BF16),
            pltpu.VMEM((HEADS, SPAN, 2 * HD), BF16),
            pltpu.VMEM((HEADS, SPAN, 2 * HD), BF16),
            pltpu.VMEM((HEADS, SPAN, 2 * HD), BF16),
            pltpu.VMEM((HEADS, ROWS, 3 * HD), BF16),
            pltpu.VMEM((HEADS, SLOTS, 3 * HD), BF16),
            pltpu.VMEM((HEADS, SLOTS, 3 * HD), BF16),
            pltpu.VMEM((HEADS, ROWS, HD), F32),
            pltpu.VMEM((HEADS, ROWS, HD), F32),
            pltpu.VMEM((128, DIRECT + 512), BF16),
            pltpu.VMEM((8, ROWS), I32),
            pltpu.VMEM((ROWS, 128), I32),
            pltpu.VMEM((HEADS, 8, SLOTS), I32),
            pltpu.VMEM((HEADS, SLOTS, 128), I32),
            pltpu.VMEM((NY, SEQ, 128), F32),
            square, square, square, square,
            step, step, step, step, back, back, back, back,
            dma((HEADS, 4)),
            dma((HEADS, 3)),
        ]
        + [dma] * 8
        + [dma((HEADS,))] * 20,
        compiler_params=pltpu.CompilerParams(
            collective_id=0, has_side_effects=True, vmem_limit_bytes=60 * 1024 * 1024
        ),
    )(*args)


def call_wide(args):
    hbm = pl.BlockSpec(memory_space=pl.ANY)
    dma = pltpu.SemaphoreType.DMA
    grad = jax.ShapeDtypeStruct((ROWS, HEADS * HD), BF16)
    return pl.pallas_call(
        wide_kernel,
        out_shape=(grad, grad, grad),
        in_specs=[pl.BlockSpec(memory_space=pltpu.VMEM), hbm, hbm, hbm, hbm],
        out_specs=(hbm, hbm, hbm),
        scratch_shapes=[
            pltpu.VMEM((HEAD, 1, 128), I32),
            pltpu.VMEM((HEADS, ROWS, 4 * HD), BF16),
            pltpu.VMEM((HEADS, WIDE_SLOTS, 4 * HD), BF16),
            pltpu.VMEM((HEADS, WIDE_SLOTS, 4 * HD), BF16),
            pltpu.VMEM((NY, NZ, 1, 128), F32),
            pltpu.VMEM((NY, SEQ, 1, 128), F32),
            pltpu.VMEM((HEADS, ROWS, 4 * HD), BF16),
            pltpu.VMEM((HEADS, SPAN, 2 * HD), BF16),
            pltpu.VMEM((HEADS, SPAN, 2 * HD), BF16),
            pltpu.VMEM((HEADS, SPAN, 2 * HD), BF16),
            pltpu.VMEM((HEADS, ROWS, 3 * HD), BF16),
            pltpu.VMEM((HEADS, WIDE_SLOTS, 3 * HD), BF16),
            pltpu.VMEM((HEADS, WIDE_SLOTS, 3 * HD), BF16),
            pltpu.VMEM((HEADS, ROWS, 3 * HD), BF16),
            pltpu.VMEM((HEADS, ROWS, HD), F32),
            pltpu.VMEM((HEADS, ROWS, HD), F32),
            pltpu.VMEM((128, WIDE_SLOTS), BF16),
            pltpu.VMEM((8, ROWS), I32),
            pltpu.VMEM((ROWS, 128), I32),
            pltpu.VMEM((HEADS, 8, WIDE_SLOTS), I32),
            pltpu.VMEM((HEADS, WIDE_SLOTS, 128), I32),
            dma((HEADS, 4)),
            dma((HEADS, 3)),
            dma, dma, dma, dma,
            dma((HEADS,)), dma((HEADS,)), dma((HEADS,)), dma((HEADS,)),
            dma((HEADS,)), dma((HEADS,)), dma((HEADS,)), dma((HEADS,)),
        ],
        compiler_params=pltpu.CompilerParams(
            collective_id=1, has_side_effects=True, vmem_limit_bytes=60 * 1024 * 1024
        ),
    )(*args)


def hand_over(*refs):
    held, in_sem, out_sem = refs[6:]
    pieces = [(t, p) for p in range(4) for t in range(3)]

    def move(t, p, inward):
        part = pl.ds(p * (ROWS // 4), ROWS // 4)
        if inward:
            return pltpu.make_async_copy(refs[t].at[part], held.at[t, part], in_sem.at[t, p])
        return pltpu.make_async_copy(held.at[t, part], refs[t + 3].at[part], out_sem.at[t, p])

    for t, p in pieces:
        move(t, p, True).start()
    for t, p in pieces:
        move(t, p, True).wait()
        move(t, p, False).start()
    for t, p in pieces:
        move(t, p, False).wait()


def call_hand_over(grads):
    hbm = pl.BlockSpec(memory_space=pl.ANY)
    grad = jax.ShapeDtypeStruct((ROWS, HEADS * HD), BF16)
    return pl.pallas_call(
        hand_over, out_shape=(grad, grad, grad), in_specs=[hbm] * 3, out_specs=(hbm, hbm, hbm),
        scratch_shapes=[
            pltpu.VMEM((3, ROWS, HEADS * HD), BF16),
            pltpu.SemaphoreType.DMA((3, 4)),
            pltpu.SemaphoreType.DMA((3, 4)),
        ],
    )(*grads)


def local(cluster_id, queries, key_vectors, value_vectors, grad_output):
    args = (cluster_id.reshape(1, 128), queries, key_vectors, value_vectors, grad_output)
    dq, dk, dv, flag = call_kernel(args)
    grads = lax.cond(
        flag[0, 0] > 0.5, lambda given, done: call_wide(given), lambda given, done: done,
        args, (dq, dk, dv),
    )
    return call_hand_over(grads)


def solution(mesh):
    placed = (P(("seq", "head")),) + (P("seq", "head"),) * 4
    return jax.shard_map(
        local,
        mesh=mesh,
        in_specs=placed,
        out_specs=(P("seq", "head"),) * 3,
        check_vma=False,
    )
```

```python
import functools
import math

import jax
import jax.numpy as jnp
from jax import lax
from jax.experimental import pallas as pl
from jax.experimental.pallas import tpu as pltpu
from jax.sharding import PartitionSpec as P

MESH = pl.DeviceIdType.MESH
HD = 128
SPAN = 512
ROWS = 1024
SEQ = 32
HEAD = 8
NY = 4
NZ = 8
HEADS = 4
CAP = 32
DIRECT = SEQ * CAP
SIDE = 64
CROSS = 32
EXTRA = NY * SIDE
SLOTS = DIRECT + EXTRA
WIDE = 48
WIDE_SLOTS = SEQ * WIDE
QT = 256
FACTOR = 1.0 / math.sqrt(HD)
LOG2E = 1.4426950408889634
F32 = jnp.float32
BF16 = jnp.bfloat16
I32 = jnp.int32


def iota(shape, dim):
    return lax.broadcasted_iota(I32, shape, dim)


def onehot(mask):
    return jnp.where(mask, 1.0, 0.0).astype(BF16)


def mm(a, b):
    return jnp.dot(a, b, preferred_element_type=F32)


def mm_nt(a, b):
    return lax.dot_general(a, b, (((1,), (1,)), ((), ())), preferred_element_type=F32)


def aligned(value, size):
    return pl.multiple_of(value, size)


def column_hot(column, count):
    return jnp.concatenate(
        [onehot(column == iota((256, 128), 1) + 128 * c) for c in range(count)], axis=1
    )

def attend(rows, tail, grads, j, span, first):
    base = span * SPAN
    if span == 1:
        keys = rows[j, :, HD : 2 * HD]
        values = rows[j, :, 2 * HD : 3 * HD]
    else:
        keys = jnp.concatenate([tail[j, :, :HD], rows[j, :SPAN, HD : 2 * HD]], axis=0)
        values = jnp.concatenate([tail[j, :, HD:], rows[j, :SPAN, 2 * HD : 3 * HD]], axis=0)
    part_k = part_v = None
    for t in range(SPAN // QT):
        at = base + t * QT
        query = rows[j, at : at + QT, 0:HD]
        cot = rows[j, at : at + QT, 3 * HD : 4 * HD]
        scores = mm_nt(keys, query)
        if span == 0:
            gone = jnp.logical_and(iota((2 * SPAN, QT), 0) < SPAN, first)
            scores = jnp.where(gone, -jnp.inf, scores)
        top = jnp.max(scores, axis=0, keepdims=True)
        expo = jnp.exp2((scores - top) * (FACTOR * LOG2E))
        probs = expo * (1.0 / jnp.sum(expo, axis=0, keepdims=True))
        grad_probs = mm_nt(values, cot)
        delta = jnp.sum(probs * grad_probs, axis=0, keepdims=True)
        ds = (probs * (grad_probs - delta) * FACTOR).astype(BF16)
        pv = mm(probs.astype(BF16), cot)
        pk = mm(ds, query)
        part_k = pk if part_k is None else part_k + pk
        part_v = pv if part_v is None else part_v + pv
        dq = lax.dot_general(
            keys, ds, (((0,), (0,)), ((), ())), preferred_element_type=F32
        )
        grads[j, at : at + QT, 0:HD] = dq.T.astype(BF16)
    return part_k, part_v

def kernel(
    ids_ref, q_ref, k_ref, v_ref, g_ref, dq_ref, dk_ref, dv_ref, flag_ref,
    ids_buf, xin, send_f, recv_f, meta_s, meta_r, cnt_s, cnt_r, flag_s, flag_r, rows, tail,
    lead_s, lead_r, grads, send_r, recv_r, acc_k, acc_v, flat, send_row, send_col, pos_row,
    pos_col, spots, mb, mbt, mc, mct, a_r, b_s, b_r, c_s, cr_r, br_s, br_r, ar_s,
    in_sem, out_sem, ids_ss, ids_rs, meta_ss, meta_rs, cnt_ss, cnt_rs, flag_ss, flag_rs,
    fwd_ss, fwd_rs, ret_ss, ret_rs, tail_ss, tail_rs, lead_ss, lead_rs,
    a_ss, a_rs, b_ss, b_rs, c_ss, c_rs, cr_ss, cr_rs, br_ss, br_rs, ar_ss, ar_rs,
):
    me = lax.axis_index("seq")
    head = lax.axis_index("head")
    zi = me // NY
    yi = lax.rem(me, NY)

    def block_at(device, j):
        return (device // NY) * NY + lax.rem(lax.rem(device, NY) + NY - j, NY)

    def device_of(block, j):
        return (block // NY) * NY + lax.rem(lax.rem(block, NY) + j, NY)

    def peer(k):
        return lax.rem(me + k, SEQ)

    def remote(src, dst, ss, rs, seq, hd):
        return pltpu.make_async_remote_copy(
            src_ref=src, dst_ref=dst, send_sem=ss, recv_sem=rs,
            device_id=(seq, hd), device_id_type=MESH,
        )

    def wait_bytes(ref, sem):
        pltpu.make_async_copy(ref, ref, sem).wait()

    def in_copy(j, t):
        src = (q_ref, k_ref, v_ref, g_ref)[t]
        return pltpu.make_async_copy(
            src.at[:, pl.ds(aligned(j * HD, HD), HD)],
            xin.at[j, :, pl.ds(t * HD, HD)],
            in_sem.at[j, t],
        )

    def out_copy(j, t):
        dst = (dq_ref, dk_ref, dv_ref)[t]
        return pltpu.make_async_copy(
            xin.at[j, :, pl.ds(t * HD, HD)],
            dst.at[:, pl.ds(aligned(j * HD, HD), HD)],
            out_sem.at[j, t],
        )

    barrier = pltpu.get_barrier_semaphore()

    @pl.loop(1, SEQ)
    def _(k):
        pl.semaphore_signal(barrier, inc=1, device_id=(peer(k), head), device_id_type=MESH)

    @pl.loop(1, HEAD)
    def _(k):
        pl.semaphore_signal(
            barrier, inc=1, device_id=(me, lax.rem(head + k, HEAD)), device_id_type=MESH
        )

    @pl.loop(0, HEADS)
    def _(j):
        for t in range(4):
            in_copy(j, t).start()

    ids_buf[head] = ids_ref[...]
    pl.semaphore_wait(barrier, SEQ - 1 + HEAD - 1)

    @pl.loop(1, HEAD)
    def _(k):
        remote(
            ids_buf.at[head], ids_buf.at[head], ids_ss, ids_rs, me, lax.rem(head + k, HEAD)
        ).start()

    def slot_of(shape):
        col = iota(shape, 1)
        near = col < DIRECT
        past = col - DIRECT
        return (
            jnp.where(near, lax.shift_right_logical(col, 5), lax.shift_right_logical(past, 4)),
            jnp.where(near, col & 31, CAP + (past & 15)),
        )

    flat[...] = onehot(slot_of((128, DIRECT + 512))[1] == iota((128, DIRECT + 512), 0))
    upper = onehot(iota((128, 128), 0) < iota((128, 128), 1))
    sub = iota((SEQ, SEQ), 0)
    lan = iota((SEQ, SEQ), 1)
    below = onehot(lan < sub)
    below_z = onehot(
        jnp.logical_and(
            lan < sub, lax.shift_right_logical(lan, 2) == lax.shift_right_logical(sub, 2)
        )
    )
    row32 = iota((SEQ, 128), 0)
    row8 = iota((NZ, 128), 0)
    y_of = row32 & 3

    def quarter(value):
        return lax.shift_right_logical(value, 2)

    wait_bytes(ids_buf.at[pl.ds(0, HEAD - 1)], ids_rs)

    run = jnp.zeros((SEQ, 1), F32)
    owners, slots = [], []
    for c in range(ROWS // 128):
        owner = lax.shift_right_logical(ids_buf[c], 3)
        mine = jnp.where(row32 == owner, 1.0, 0.0)
        before = mm(mine.astype(BF16), upper) + run
        run = run + jnp.sum(mine, axis=1, keepdims=True)
        owners.append(owner)
        slots.append(jnp.sum(mine * before, axis=0, keepdims=True).astype(I32))

    past = jnp.maximum(jnp.broadcast_to(run, (SEQ, 128)) - float(CAP), 0.0)
    base_f = mm(below_z, past.astype(BF16))
    plane = onehot(quarter(iota((NZ, SEQ), 1)) == iota((NZ, SEQ), 0))
    cnt_s[...] = mm(plane, past.astype(BF16))
    cnt_r[yi] = cnt_s[...]

    @pl.loop(1, NY)
    def _(k):
        device = zi * NY + lax.rem(yi + k, NY)
        remote(cnt_s, cnt_r.at[yi], cnt_ss, cnt_rs, device, head).start()

    mine_e = cnt_s[...].astype(I32)
    offs = []
    for yy in range(NY):
        count = quarter(mine_e - ((yy - yi - row8 + 16) & 3) + 3).astype(F32)
        off = jnp.zeros((SEQ, 128), F32)
        for z in range(NZ - 1):
            off = off + jnp.where(quarter(row32) > z, count[z : z + 1, :], 0.0)
        offs.append(off)
    for c in range(ROWS // 128):
        owner, slot = owners[c], slots[c]
        mine = row32 == owner

        def pick(table):
            return jnp.sum(jnp.where(mine, table, 0.0), axis=0, keepdims=True).astype(I32)

        e = pick(base_f) + slot - CAP
        way = (e + yi + quarter(owner) + 64) & 3
        far = DIRECT + way * SIDE + quarter(e + 64) - 16
        for yy in range(NY):
            far = far + jnp.where(way == yy, pick(offs[yy]), 0)
        index = jnp.where(slot < CAP, owner * CAP + slot, far)
        send_row[:, c * 128 : (c + 1) * 128] = jnp.broadcast_to(index, (8, 128))

    def pack_tile(j, r0):
        choose = onehot(send_row[0:1, :] == iota((256, ROWS), 0) + r0)
        send_f[j, pl.ds(r0, 256), :] = mm(choose, xin[j]).astype(BF16)

    def y_peer(k):
        return lax.rem(yi + k, NY)

    def z_peer(k):
        return lax.rem(zi + k, NZ)

    def at_side(y):
        return pl.ds(aligned(y * SIDE, SIDE), SIDE)

    def at_cross(z):
        return pl.ds(aligned(z * CROSS, CROSS), CROSS)

    def at_extra(y):
        return pl.ds(aligned(DIRECT + y * SIDE, SIDE), SIDE)

    def stage_a(j):
        for t in range(4):
            in_copy(j, t).wait()
        pack_tile(j, DIRECT)

        @pl.loop(1, NY)
        def _(k):
            y = y_peer(k)
            remote(
                send_f.at[j, at_extra(y)], a_r.at[j, at_side(yi)], a_ss.at[j], a_rs.at[j],
                zi * NY + y, head,
            ).start()

        a_r[j, at_side(yi), :] = send_f[j, at_extra(yi), :]

    def stage_b(j):
        wait_bytes(a_r.at[j, pl.ds(0, EXTRA - SIDE)], a_rs.at[j])
        b_s[j] = mm(mb[...], a_r[j]).astype(BF16)

        @pl.loop(1, NZ)
        def _(k):
            z = z_peer(k)
            remote(
                b_s.at[j, at_cross(z)], b_r.at[j, at_cross(zi)], b_ss.at[j], b_rs.at[j],
                z * NY + yi, head,
            ).start()

        b_r[j, at_cross(zi), :] = b_s[j, at_cross(zi), :]

    def stage_c(j):
        wait_bytes(b_r.at[j, pl.ds(0, EXTRA - CROSS)], b_rs.at[j])
        c_s[j] = mm(mc[...], b_r[j]).astype(BF16)

        @pl.loop(1, NY)
        def _(k):
            y = y_peer(k)
            remote(
                c_s.at[j, at_side(lax.rem(y + NY - j, NY))], recv_f.at[j, at_extra(yi)],
                c_ss.at[j], c_rs.at[j], zi * NY + y, head,
            ).start()

        recv_f[j, at_extra(yi), :] = c_s[j, at_side(lax.rem(yi + NY - j, NY)), :]

    def pack_forward(j):
        @pl.loop(0, DIRECT // 256)
        def _(t):
            tile = lax.rem(zi // 2 + t, DIRECT // 256)
            pack_tile(j, aligned(tile * 256, 256))

            @pl.loop(0, 256 // CAP)
            def _(k):
                block = tile * (256 // CAP) + lax.rem(me + k, 256 // CAP)
                device = device_of(block, j)
                source = aligned(block * CAP, CAP)

                @pl.when(device != me)
                def _():
                    remote(
                        send_f.at[j, pl.ds(source, CAP)],
                        recv_f.at[j, pl.ds(aligned(me * CAP, CAP), CAP)],
                        fwd_ss.at[j], fwd_rs.at[j], device, head,
                    ).start()

        own = aligned(block_at(me, j) * CAP, CAP)
        recv_f[j, pl.ds(aligned(me * CAP, CAP), CAP), :] = send_f[j, pl.ds(own, CAP), :]

    stage_a(0)
    pack_forward(0)

    @pl.loop(1, HEADS)
    def _(j):
        stage_a(j)

    meta = jnp.zeros((SEQ, 128), F32)
    for c in range(ROWS // 128):
        cluster = (ids_buf[c] & 7).astype(F32) + 1.0
        mine = jnp.where(row32 == owners[c], cluster, 0.0)
        meta = meta + mm_nt(mine.astype(BF16), onehot(iota((128, 128), 0) == slots[c]))
    for b in range(SEQ):
        meta_s[b % NY, b // NY] = meta[b : b + 1, :]

    @pl.loop(1, SEQ)
    def _(k):
        device = peer(k)
        remote(
            meta_s.at[:, device // NY], meta_r.at[:, me], meta_ss, meta_rs, device, head
        ).start()

    for b in range(NY):
        meta_r[b, me] = meta_s[b, zi]
    wait_bytes(cnt_r.at[pl.ds(0, NY - 1)], cnt_rs)

    bad = jnp.zeros((1, 128), F32)
    starts_a, starts_b, counts = [], [], []
    filled = jnp.zeros((NZ, 128), I32)
    for y in range(NY):
        for yy in range(NY):
            share = quarter(cnt_r[y].astype(I32) - ((yy - y - row8 + 16) & 3) + 3)
            total = jnp.sum(share.astype(F32), axis=0, keepdims=True)
            bad = jnp.maximum(bad, total - float(SIDE))
        share = quarter(cnt_r[y].astype(I32) - ((yi - y - row8 + 16) & 3) + 3)
        start = jnp.zeros((NZ, 128), I32)
        for z in range(NZ - 1):
            start = start + jnp.where(row8 > z, share[z : z + 1, :], 0)
        starts_a.append(start)
        starts_b.append(filled)
        counts.append(share)
        filled = filled + share
    for yy in range(NY):
        total = jnp.zeros((NZ, 128), I32)
        for y in range(NY):
            total = total + quarter(cnt_r[y].astype(I32) - ((yy - y - row8 + 16) & 3) + 3)
        bad = jnp.maximum(
            bad, jnp.max(total.astype(F32), axis=0, keepdims=True) - float(CROSS)
        )

    def by_group(tables):
        group = lax.shift_right_logical(iota((NZ, EXTRA), 1), 6)
        result = jnp.zeros((NZ, EXTRA), I32)
        for y in range(NY):
            result = jnp.where(group == y, jnp.concatenate([tables[y]] * 2, axis=1), result)
        return result

    wide_a, wide_b, wide_c = by_group(starts_a), by_group(starts_b), by_group(counts)
    for z in range(NZ):
        step = iota((CROSS, EXTRA), 0) - wide_b[z : z + 1, :]
        place = (iota((CROSS, EXTRA), 1) & (SIDE - 1)) - wide_a[z : z + 1, :]
        hit = jnp.logical_and(
            jnp.logical_and(step >= 0, step < wide_c[z : z + 1, :]), step == place
        )
        mb[z * CROSS : (z + 1) * CROSS, :] = onehot(hit)
    mbt[...] = mb[...].astype(F32).T.astype(BF16)

    stage_b(0)
    pack_forward(1)

    @pl.loop(1, HEADS)
    def _(j):
        stage_b(j)

    for c in range(ROWS // 128):
        send_col[c * 128 : (c + 1) * 128, :] = (
            jnp.broadcast_to(send_row[0:1, c * 128 : (c + 1) * 128], (128, 128))
            .astype(F32).T.astype(I32)
        )
    wait_bytes(meta_r.at[:, pl.ds(0, SEQ - 1)], meta_rs)

    bases = [jnp.zeros((SEQ, 128), I32)]
    for b in range(NY):
        held = jnp.where(meta_r[b].reshape(SEQ, 128) > 0.5, 1.0, 0.0)
        held = jnp.maximum(jnp.sum(held, axis=1, keepdims=True) - float(CAP), 0.0)
        bases.append(bases[b] + jnp.broadcast_to(held, (SEQ, 128)).astype(I32))
    firsts = []
    for yy in range(NY):
        residue = (yy - y_of - zi + 16) & 3
        firsts.append([quarter(base - residue + 3) for base in bases])
    lengths = [[f[b + 1] - f[b] for b in range(NY)] for f in firsts]
    stacked = jnp.concatenate([v.astype(F32) for f in lengths for v in f], axis=1)
    before_c = mm(below, stacked.astype(BF16))
    landing = []
    for yy in range(NY):
        landing.append([])
        for b in range(NY):
            at = (yy * NY + b) * 128
            part = before_c[:, at : at + 128].astype(I32)
            landing[yy].append(part)
            total = (part + lengths[yy][b])[SEQ - 1 : SEQ, :].astype(F32)
            bad = jnp.maximum(bad, total - float(SIDE))
    lane = iota((SEQ, 128), 1)
    for b in range(NY):
        e = bases[b] + lane - CAP
        way = (e + y_of + zi + 64) & 3
        spot = jnp.zeros((SEQ, 128), I32)
        for yy in range(NY):
            here = yy * SIDE + landing[yy][b] + quarter(e + 64) - 16 - firsts[yy][b]
            spot = jnp.where(way == yy, here, spot)
        used = jnp.logical_and(meta_r[b].reshape(SEQ, 128) > 0.5, lane >= CAP)
        spots[b] = jnp.where(used, spot.astype(F32), -1.0)

    def chosen(tables):
        result = tables[0]
        for yy in range(1, NY):
            result = jnp.where(yi == yy, tables[yy], result)
        return result

    my_total = chosen([f[NY] for f in firsts])
    my_start = mm(below_z, my_total.astype(F32).astype(BF16))
    col = iota((SEQ, EXTRA), 1)
    for b in range(NY):
        landing_b = chosen([landing[yy][b] for yy in range(NY)]).astype(F32)
        length_b = chosen([lengths[yy][b] for yy in range(NY)]).astype(F32)
        source_b = my_start + chosen([firsts[yy][b] for yy in range(NY)]).astype(F32)
        found = jnp.zeros((SIDE, EXTRA), F32)
        for y in range(NY):
            match = iota((SEQ, EXTRA), 0) == lax.shift_right_logical(col, 5) * NY + y

            def across(table):
                twice = jnp.concatenate([table, table], axis=1)
                return jnp.sum(jnp.where(match, twice, 0.0), axis=0, keepdims=True).astype(I32)

            step = iota((SIDE, EXTRA), 0) - across(landing_b)
            place = (iota((SIDE, EXTRA), 1) & (CROSS - 1)) - across(source_b)
            hit = jnp.logical_and(
                jnp.logical_and(step >= 0, step < across(length_b)), step == place
            )
            found = found + jnp.where(hit, 1.0, 0.0)
        mc[b * SIDE : (b + 1) * SIDE, :] = found.astype(BF16)
    mct[...] = mc[...].astype(F32).T.astype(BF16)

    flag_s[...] = jnp.broadcast_to(jnp.where(bad > 0.5, 1.0, 0.0), (8, 128))
    flag_r[zi] = flag_s[...]

    @pl.loop(1, NZ)
    def _(k):
        remote(
            flag_s, flag_r.at[zi], flag_ss, flag_rs, z_peer(k) * NY + yi, head
        ).start()

    stage_c(0)

    def positions(j):
        block = lax.rem(yi + NY - j, NY)
        m = meta_r[block].reshape(SEQ, 128)
        hot = jnp.concatenate([jnp.where(m == c + 1.0, 1.0, 0.0) for c in range(8)], axis=0)
        within = mm(hot.astype(BF16), upper)
        total = jnp.broadcast_to(jnp.sum(hot, axis=1, keepdims=True), (8 * SEQ, 128))
        lower = onehot(iota((8 * SEQ, 8 * SEQ), 1) < iota((8 * SEQ, 8 * SEQ), 0))
        placed = hot * (mm(lower, total.astype(BF16)) + within)
        pos = jnp.where(m > 0.5, 0.0, -1.0)
        for c in range(8):
            pos = pos + placed[c * SEQ : (c + 1) * SEQ, :]

        def halves(value):
            high = jnp.floor(value * (1.0 / 32.0))
            return [high, value - high * 32.0]

        parts = mm(
            jnp.concatenate(halves(pos) + halves(spots[block]), axis=0).astype(BF16), flat[...]
        )
        mine = iota((SEQ, DIRECT + 512), 0) == slot_of((SEQ, DIRECT + 512))[0]
        spread = jnp.where(mine, parts[:SEQ] * 32.0 + parts[SEQ : 2 * SEQ], 0.0)
        line = jnp.sum(spread, axis=0, keepdims=True)
        spread = jnp.where(mine, parts[2 * SEQ : 3 * SEQ] * 32.0 + parts[3 * SEQ :], 0.0)
        target = jnp.sum(spread, axis=0, keepdims=True)[:, DIRECT:].astype(I32)
        high, low = halves(line[:, DIRECT:] + 1.0)
        pair = jnp.concatenate(
            [jnp.broadcast_to(high, (8, 512)), jnp.broadcast_to(low, (8, 512))], axis=0
        )
        found = mm_nt(pair.astype(BF16), onehot(iota((EXTRA, 512), 0) == target))
        extra = found[0:1, :] * 32.0 + found[8:9, :] - 1.0
        row = jnp.concatenate([line[:, :DIRECT], extra], axis=1)
        pos_row[j] = jnp.broadcast_to(row, (8, SLOTS)).astype(I32)
        for c in range(SLOTS // 128):
            piece = row[:, c * 128 : (c + 1) * 128]
            pos_col[j, c * 128 : (c + 1) * 128, :] = (
                jnp.broadcast_to(piece, (128, 128)).T.astype(I32)
            )

    def tail_copy(j):
        after = device_of(lax.rem(block_at(me, j) + 1, SEQ), j)
        return remote(
            rows.at[j, pl.ds(SPAN, SPAN), pl.ds(HD, 2 * HD)], tail.at[j],
            tail_ss.at[j], tail_rs.at[j], after, head,
        )

    def lead_copy(j):
        prior = device_of(lax.rem(block_at(me, j) + SEQ - 1, SEQ), j)
        return remote(lead_s.at[j], lead_r.at[j], lead_ss.at[j], lead_rs.at[j], prior, head)

    def open_chunk(j):
        positions(j)
        wait_bytes(recv_f.at[j, pl.ds(0, DIRECT - CAP)], fwd_rs.at[j])
        wait_bytes(recv_f.at[j, pl.ds(0, EXTRA - SIDE)], c_rs.at[j])

        @pl.loop(0, ROWS // 256)
        def _(t):
            r0 = aligned(t * 256, 256)
            choose = onehot(pos_row[j, 0:1, :] == iota((256, SLOTS), 0) + r0)
            rows[j, pl.ds(r0, 256), :] = mm(choose, recv_f[j]).astype(BF16)

        tail_copy(j).start()

    def last_span(j):
        part_k, part_v = attend(rows, tail, grads, j, 1, block_at(me, j) == 0)
        acc_k[j] = part_k
        acc_v[j] = part_v

    def first_span(j):
        tail_copy(j).wait_recv()
        part_k, part_v = attend(rows, tail, grads, j, 0, block_at(me, j) == 0)
        lead_s[j, :, :HD] = part_k[:SPAN].astype(BF16)
        lead_s[j, :, HD:] = part_v[:SPAN].astype(BF16)
        lead_copy(j).start()
        grads[j, :SPAN, HD : 2 * HD] = (acc_k[j, :SPAN] + part_k[SPAN:]).astype(BF16)
        grads[j, :SPAN, 2 * HD :] = (acc_v[j, :SPAN] + part_v[SPAN:]).astype(BF16)

    def back_b(j):
        wait_bytes(cr_r.at[j, pl.ds(0, EXTRA - SIDE)], cr_rs.at[j])
        br_s[j] = mm(mct[...], cr_r[j]).astype(BF16)

        @pl.loop(1, NZ)
        def _(k):
            z = z_peer(k)
            remote(
                br_s.at[j, at_cross(z)], br_r.at[j, at_cross(zi)], br_ss.at[j], br_rs.at[j],
                z * NY + yi, head,
            ).start()

        br_r[j, at_cross(zi), :] = br_s[j, at_cross(zi), :]

    def close_chunk(j):
        lead_copy(j).wait_recv()
        grads[j, SPAN:, HD : 2 * HD] = (
            acc_k[j, SPAN:] + lead_r[j, :, :HD].astype(F32)
        ).astype(BF16)
        grads[j, SPAN:, 2 * HD :] = (
            acc_v[j, SPAN:] + lead_r[j, :, HD:].astype(F32)
        ).astype(BF16)

        def pack_back(r0):
            choose = column_hot(pos_col[j, pl.ds(r0, 256), :], ROWS // 128)
            send_r[j, pl.ds(r0, 256), :] = mm(choose, grads[j]).astype(BF16)

        pack_back(DIRECT)
        own_y = lax.rem(yi + NY - j, NY)

        @pl.loop(1, NY)
        def _(k):
            y = y_peer(k)
            remote(
                send_r.at[j, at_extra(y)], cr_r.at[j, at_side(own_y)], cr_ss.at[j],
                cr_rs.at[j], zi * NY + y, head,
            ).start()

        cr_r[j, at_side(own_y), :] = send_r[j, at_extra(yi), :]

        @pl.loop(0, DIRECT // 256)
        def _(t):
            pack_back(aligned(t * 256, 256))

        own = aligned(block_at(me, j) * CAP, CAP)

        def send_back(k):
            device = peer(k)
            remote(
                send_r.at[j, pl.ds(aligned(device * CAP, CAP), CAP)],
                recv_r.at[j, pl.ds(own, CAP)],
                ret_ss.at[j], ret_rs.at[j], device, head,
            ).start()

        @pl.loop(1, SEQ // 2)
        def _(k):
            send_back(k)

        @pl.when(j == HEADS - 1)
        def _():
            back_b(j)

        @pl.loop(SEQ // 2, SEQ)
        def _(k):
            send_back(k)

        recv_r[j, pl.ds(own, CAP), :] = send_r[j, pl.ds(aligned(me * CAP, CAP), CAP), :]

    def back_a(j):
        wait_bytes(br_r.at[j, pl.ds(0, EXTRA - CROSS)], br_rs.at[j])
        ar_s[j] = mm(mbt[...], br_r[j]).astype(BF16)

        @pl.loop(1, NY)
        def _(k):
            y = y_peer(k)
            remote(
                ar_s.at[j, at_side(y)], recv_r.at[j, at_extra(yi)], ar_ss.at[j], ar_rs.at[j],
                zi * NY + y, head,
            ).start()

        recv_r[j, at_extra(yi), :] = ar_s[j, at_side(yi), :]

    @pl.loop(0, HEADS + 4)
    def _(i):
        @pl.when(i < HEADS)
        def _():
            open_chunk(i)

        @pl.when(jnp.logical_and(i >= 1, i <= HEADS))
        def _():
            first_span(i - 1)

        @pl.when(i < 1)
        def _():
            stage_c(1)

        @pl.when(i < HEADS - 2)
        def _():
            pack_forward(i + 2)
            stage_c(i + 2)

        @pl.when(i < HEADS)
        def _():
            last_span(i)

        @pl.when(jnp.logical_and(i >= 3, i < HEADS + 2))
        def _():
            back_b(i - 3)

        @pl.when(jnp.logical_and(i >= 2, i < HEADS + 2))
        def _():
            close_chunk(i - 2)

        @pl.when(i >= 4)
        def _():
            back_a(i - 4)

    @pl.loop(0, HEADS)
    def _(j):
        wait_bytes(recv_r.at[j, pl.ds(0, DIRECT - CAP)], ret_rs.at[j])
        wait_bytes(recv_r.at[j, pl.ds(0, EXTRA - SIDE)], ar_rs.at[j])

        @pl.loop(0, ROWS // 256)
        def _(t):
            r0 = aligned(t * 256, 256)
            choose = column_hot(send_col[pl.ds(r0, 256), :], SLOTS // 128)
            xin[j, pl.ds(r0, 256), : 3 * HD] = mm(choose, recv_r[j]).astype(BF16)

        for t in range(3):
            out_copy(j, t).start()

    wait_bytes(flag_r.at[pl.ds(0, NZ - 1)], flag_rs)
    flag_ref[0, 0] = jnp.max(flag_r[...])
    wait_bytes(ids_buf.at[pl.ds(0, HEAD - 1)], ids_ss)
    wait_bytes(meta_r.at[:, pl.ds(0, SEQ - 1)], meta_ss)
    wait_bytes(cnt_r.at[pl.ds(0, NY - 1)], cnt_ss)
    wait_bytes(flag_r.at[pl.ds(0, NZ - 1)], flag_ss)

    @pl.loop(0, HEADS)
    def _(j):
        wait_bytes(send_f.at[j, pl.ds(0, DIRECT - CAP)], fwd_ss.at[j])
        wait_bytes(send_r.at[j, pl.ds(0, DIRECT - CAP)], ret_ss.at[j])
        wait_bytes(a_r.at[j, pl.ds(0, EXTRA - SIDE)], a_ss.at[j])
        wait_bytes(b_r.at[j, pl.ds(0, EXTRA - CROSS)], b_ss.at[j])
        wait_bytes(c_s.at[j, pl.ds(0, EXTRA - SIDE)], c_ss.at[j])
        wait_bytes(cr_r.at[j, pl.ds(0, EXTRA - SIDE)], cr_ss.at[j])
        wait_bytes(br_r.at[j, pl.ds(0, EXTRA - CROSS)], br_ss.at[j])
        wait_bytes(ar_s.at[j, pl.ds(0, EXTRA - SIDE)], ar_ss.at[j])
        wait_bytes(tail.at[j], tail_ss.at[j])
        wait_bytes(lead_s.at[j], lead_ss.at[j])
        for t in range(3):
            out_copy(j, t).wait()


def wide_kernel(
    ids_ref, q_ref, k_ref, v_ref, g_ref, dq_ref, dk_ref, dv_ref,
    ids_buf, xin, send_f, recv_f, meta_s, meta_r, rows, tail, lead_s, lead_r,
    grads, send_r, recv_r, outs, acc_k, acc_v, flat, send_row, send_col, pos_row, pos_col,
    in_sem, out_sem, ids_ss, ids_rs, meta_ss, meta_rs, fwd_ss, fwd_rs, ret_ss, ret_rs,
    tail_ss, tail_rs, lead_ss, lead_rs,
):
    me = lax.axis_index("seq")
    head = lax.axis_index("head")
    zi = me // NY
    yi = lax.rem(me, NY)

    def block_at(device, j):
        return (device // NY) * NY + lax.rem(lax.rem(device, NY) + NY - j, NY)

    def device_of(block, j):
        return (block // NY) * NY + lax.rem(lax.rem(block, NY) + j, NY)

    def peer(k):
        return lax.rem(me + k, SEQ)

    def remote(src, dst, ss, rs, seq, hd):
        return pltpu.make_async_remote_copy(
            src_ref=src, dst_ref=dst, send_sem=ss, recv_sem=rs,
            device_id=(seq, hd), device_id_type=MESH,
        )

    def wait_bytes(ref, sem):
        pltpu.make_async_copy(ref, ref, sem).wait()

    def in_copy(j, t):
        src = (q_ref, k_ref, v_ref, g_ref)[t]
        return pltpu.make_async_copy(
            src.at[:, pl.ds(aligned(j * HD, HD), HD)],
            xin.at[j, :, pl.ds(t * HD, HD)],
            in_sem.at[j, t],
        )

    def out_copy(j, t):
        dst = (dq_ref, dk_ref, dv_ref)[t]
        return pltpu.make_async_copy(
            outs.at[j, :, pl.ds(t * HD, HD)],
            dst.at[:, pl.ds(aligned(j * HD, HD), HD)],
            out_sem.at[j, t],
        )

    barrier = pltpu.get_barrier_semaphore()

    @pl.loop(1, SEQ)
    def _(k):
        pl.semaphore_signal(barrier, inc=1, device_id=(peer(k), head), device_id_type=MESH)

    @pl.loop(1, HEAD)
    def _(k):
        pl.semaphore_signal(
            barrier, inc=1, device_id=(me, lax.rem(head + k, HEAD)), device_id_type=MESH
        )

    @pl.loop(0, HEADS)
    def _(j):
        for t in range(4):
            in_copy(j, t).start()

    ids_buf[head] = ids_ref[...]
    pl.semaphore_wait(barrier, SEQ - 1 + HEAD - 1)

    @pl.loop(1, HEAD)
    def _(k):
        remote(
            ids_buf.at[head], ids_buf.at[head], ids_ss, ids_rs, me, lax.rem(head + k, HEAD)
        ).start()

    lane = iota((128, WIDE_SLOTS), 1)
    source_of = lax.shift_right_logical(lane * 1366, 16)
    flat[...] = onehot(lane - source_of * WIDE == iota((128, WIDE_SLOTS), 0))
    upper = onehot(iota((128, 128), 0) < iota((128, 128), 1))
    wait_bytes(ids_buf.at[pl.ds(0, HEAD - 1)], ids_rs)

    run = jnp.zeros((SEQ, 1), F32)
    meta = jnp.zeros((SEQ, 128), F32)
    for c in range(ROWS // 128):
        idc = ids_buf[c]
        owner = lax.shift_right_logical(idc, 3)
        cluster = (idc & 7).astype(F32) + 1.0
        mine = jnp.where(iota((SEQ, 128), 0) == owner, 1.0, 0.0)
        before = mm(mine.astype(BF16), upper) + run
        run = run + jnp.sum(mine, axis=1, keepdims=True)
        slot = jnp.sum(mine * before, axis=0, keepdims=True).astype(I32)
        index = owner * WIDE + slot
        send_row[:, c * 128 : (c + 1) * 128] = jnp.broadcast_to(index, (8, 128))
        send_col[c * 128 : (c + 1) * 128, :] = (
            jnp.broadcast_to(index, (128, 128)).astype(F32).T.astype(I32)
        )
        meta = meta + mm_nt((mine * cluster).astype(BF16), onehot(iota((128, 128), 0) == slot))
    for b in range(SEQ):
        meta_s[b % NY, b // NY] = meta[b : b + 1, :]

    @pl.loop(1, SEQ)
    def _(k):
        device = peer(k)
        remote(
            meta_s.at[:, device // NY], meta_r.at[:, me], meta_ss, meta_rs, device, head
        ).start()

    for b in range(NY):
        meta_r[b, me] = meta_s[b, zi]

    def pack_forward(j):
        for t in range(4):
            in_copy(j, t).wait()

        @pl.loop(0, WIDE_SLOTS // 256)
        def _(t):
            r0 = aligned(t * 256, 256)
            choose = onehot(send_row[0:1, :] == iota((256, ROWS), 0) + r0)
            send_f[j, pl.ds(r0, 256), :] = mm(choose, xin[j]).astype(BF16)

        @pl.loop(1, SEQ)
        def _(k):
            device = peer(k)
            start = aligned(block_at(device, j) * WIDE, WIDE)
            remote(
                send_f.at[j, pl.ds(start, WIDE)],
                recv_f.at[j, pl.ds(aligned(me * WIDE, WIDE), WIDE)],
                fwd_ss.at[j], fwd_rs.at[j], device, head,
            ).start()

        own = aligned(block_at(me, j) * WIDE, WIDE)
        recv_f[j, pl.ds(aligned(me * WIDE, WIDE), WIDE), :] = send_f[j, pl.ds(own, WIDE), :]

    @pl.loop(0, 2)
    def _(j):
        pack_forward(j)

    wait_bytes(meta_r.at[:, pl.ds(0, SEQ - 1)], meta_rs)

    def positions(j):
        m = meta_r[lax.rem(yi + NY - j, NY)].reshape(SEQ, 128)
        hot = jnp.concatenate([jnp.where(m == c + 1.0, 1.0, 0.0) for c in range(8)], axis=0)
        within = mm(hot.astype(BF16), upper)
        total = jnp.broadcast_to(jnp.sum(hot, axis=1, keepdims=True), (8 * SEQ, 128))
        lower = onehot(iota((8 * SEQ, 8 * SEQ), 1) < iota((8 * SEQ, 8 * SEQ), 0))
        placed = hot * (mm(lower, total.astype(BF16)) + within)
        pos = jnp.where(m > 0.5, 0.0, -1.0)
        for c in range(8):
            pos = pos + placed[c * SEQ : (c + 1) * SEQ, :]
        high = jnp.floor(pos * (1.0 / 32.0))
        low = pos - high * 32.0
        parts = mm(jnp.concatenate([high, low], axis=0).astype(BF16), flat[...])
        spread = parts[:SEQ] * 32.0 + parts[SEQ:]
        mine = iota((SEQ, WIDE_SLOTS), 0) == lax.shift_right_logical(iota((SEQ, WIDE_SLOTS), 1) * 1366, 16)
        row = jnp.sum(jnp.where(mine, spread, 0.0), axis=0, keepdims=True)
        pos_row[j] = jnp.broadcast_to(row, (8, WIDE_SLOTS)).astype(I32)
        for c in range(WIDE_SLOTS // 128):
            piece = row[:, c * 128 : (c + 1) * 128]
            pos_col[j, c * 128 : (c + 1) * 128, :] = (
                jnp.broadcast_to(piece, (128, 128)).T.astype(I32)
            )

    def tail_copy(j):
        after = device_of(lax.rem(block_at(me, j) + 1, SEQ), j)
        return remote(
            rows.at[j, pl.ds(SPAN, SPAN), pl.ds(HD, 2 * HD)], tail.at[j],
            tail_ss.at[j], tail_rs.at[j], after, head,
        )

    def lead_copy(j):
        prior = device_of(lax.rem(block_at(me, j) + SEQ - 1, SEQ), j)
        return remote(lead_s.at[j], lead_r.at[j], lead_ss.at[j], lead_rs.at[j], prior, head)

    def open_chunk(j):
        positions(j)
        wait_bytes(recv_f.at[j, pl.ds(0, WIDE_SLOTS - WIDE)], fwd_rs.at[j])

        @pl.loop(0, ROWS // 256)
        def _(t):
            r0 = aligned(t * 256, 256)
            choose = onehot(pos_row[j, 0:1, :] == iota((256, WIDE_SLOTS), 0) + r0)
            rows[j, pl.ds(r0, 256), :] = mm(choose, recv_f[j]).astype(BF16)

        tail_copy(j).start()

    def last_span(j):
        part_k, part_v = attend(rows, tail, grads, j, 1, block_at(me, j) == 0)
        acc_k[j] = part_k
        acc_v[j] = part_v

    def first_span(j):
        tail_copy(j).wait_recv()
        part_k, part_v = attend(rows, tail, grads, j, 0, block_at(me, j) == 0)
        lead_s[j, :, :HD] = part_k[:SPAN].astype(BF16)
        lead_s[j, :, HD:] = part_v[:SPAN].astype(BF16)
        lead_copy(j).start()
        grads[j, :SPAN, HD : 2 * HD] = (acc_k[j, :SPAN] + part_k[SPAN:]).astype(BF16)
        grads[j, :SPAN, 2 * HD :] = (acc_v[j, :SPAN] + part_v[SPAN:]).astype(BF16)

    def close_chunk(j):
        lead_copy(j).wait_recv()
        grads[j, SPAN:, HD : 2 * HD] = (
            acc_k[j, SPAN:] + lead_r[j, :, :HD].astype(F32)
        ).astype(BF16)
        grads[j, SPAN:, 2 * HD :] = (
            acc_v[j, SPAN:] + lead_r[j, :, HD:].astype(F32)
        ).astype(BF16)

        @pl.loop(0, WIDE_SLOTS // 256)
        def _(t):
            r0 = aligned(t * 256, 256)
            choose = column_hot(pos_col[j, pl.ds(r0, 256), :], ROWS // 128)
            send_r[j, pl.ds(r0, 256), :] = mm(choose, grads[j]).astype(BF16)

        own = aligned(block_at(me, j) * WIDE, WIDE)

        @pl.loop(1, SEQ)
        def _(k):
            device = peer(k)
            remote(
                send_r.at[j, pl.ds(aligned(device * WIDE, WIDE), WIDE)],
                recv_r.at[j, pl.ds(own, WIDE)],
                ret_ss.at[j], ret_rs.at[j], device, head,
            ).start()

        recv_r[j, pl.ds(own, WIDE), :] = send_r[j, pl.ds(aligned(me * WIDE, WIDE), WIDE), :]

    @pl.loop(0, HEADS + 2)
    def _(i):
        @pl.when(i < HEADS)
        def _():
            open_chunk(i)

        @pl.when(i < HEADS - 2)
        def _():
            pack_forward(i + 2)

        @pl.when(jnp.logical_and(i >= 1, i <= HEADS))
        def _():
            first_span(i - 1)

        @pl.when(i < HEADS)
        def _():
            last_span(i)

        @pl.when(i >= 2)
        def _():
            close_chunk(i - 2)

    @pl.loop(0, HEADS)
    def _(j):
        wait_bytes(recv_r.at[j, pl.ds(0, WIDE_SLOTS - WIDE)], ret_rs.at[j])

        @pl.loop(0, ROWS // 256)
        def _(t):
            r0 = aligned(t * 256, 256)
            choose = column_hot(send_col[pl.ds(r0, 256), :], WIDE_SLOTS // 128)
            outs[j, pl.ds(r0, 256), :] = mm(choose, recv_r[j]).astype(BF16)

        for t in range(3):
            out_copy(j, t).start()

    wait_bytes(ids_buf.at[pl.ds(0, HEAD - 1)], ids_ss)
    wait_bytes(meta_r.at[:, pl.ds(0, SEQ - 1)], meta_ss)

    @pl.loop(0, HEADS)
    def _(j):
        wait_bytes(send_f.at[j, pl.ds(0, WIDE_SLOTS - WIDE)], fwd_ss.at[j])
        wait_bytes(send_r.at[j, pl.ds(0, WIDE_SLOTS - WIDE)], ret_ss.at[j])
        wait_bytes(tail.at[j], tail_ss.at[j])
        wait_bytes(lead_s.at[j], lead_ss.at[j])
        for t in range(3):
            out_copy(j, t).wait()


def call_kernel(args):
    hbm = pl.BlockSpec(memory_space=pl.ANY)
    near = pl.BlockSpec(memory_space=pltpu.VMEM)
    dma = pltpu.SemaphoreType.DMA
    grad = jax.ShapeDtypeStruct((ROWS, HEADS * HD), BF16)
    step = pltpu.VMEM((HEADS, EXTRA, 4 * HD), BF16)
    back = pltpu.VMEM((HEADS, EXTRA, 3 * HD), BF16)
    square = pltpu.VMEM((EXTRA, EXTRA), BF16)
    return pl.pallas_call(
        kernel,
        out_shape=(grad, grad, grad, jax.ShapeDtypeStruct((1, 1), F32)),
        in_specs=[near, hbm, hbm, hbm, hbm],
        out_specs=(hbm, hbm, hbm, pl.BlockSpec(memory_space=pltpu.SMEM)),
        scratch_shapes=[
            pltpu.VMEM((HEAD, 1, 128), I32),
            pltpu.VMEM((HEADS, ROWS, 4 * HD), BF16),
            pltpu.VMEM((HEADS, SLOTS, 4 * HD), BF16),
            pltpu.VMEM((HEADS, SLOTS, 4 * HD), BF16),
            pltpu.VMEM((NY, NZ, 1, 128), F32),
            pltpu.VMEM((NY, SEQ, 1, 128), F32),
            pltpu.VMEM((NZ, 128), F32),
            pltpu.VMEM((NY, NZ, 128), F32),
            pltpu.VMEM((8, 128), F32),
            pltpu.VMEM((NZ, 8, 128), F32),
            pltpu.VMEM((HEADS, ROWS, 4 * HD), BF16),
            pltpu.VMEM((HEADS, SPAN, 2 * HD), BF16),
            pltpu.VMEM((HEADS, SPAN, 2 * HD), BF16),
            pltpu.VMEM((HEADS, SPAN, 2 * HD), BF16),
            pltpu.VMEM((HEADS, ROWS, 3 * HD), BF16),
            pltpu.VMEM((HEADS, SLOTS, 3 * HD), BF16),
            pltpu.VMEM((HEADS, SLOTS, 3 * HD), BF16),
            pltpu.VMEM((HEADS, ROWS, HD), F32),
            pltpu.VMEM((HEADS, ROWS, HD), F32),
            pltpu.VMEM((128, DIRECT + 512), BF16),
            pltpu.VMEM((8, ROWS), I32),
            pltpu.VMEM((ROWS, 128), I32),
            pltpu.VMEM((HEADS, 8, SLOTS), I32),
            pltpu.VMEM((HEADS, SLOTS, 128), I32),
            pltpu.VMEM((NY, SEQ, 128), F32),
            square, square, square, square,
            step, step, step, step, back, back, back, back,
            dma((HEADS, 4)),
            dma((HEADS, 3)),
        ]
        + [dma] * 8
        + [dma((HEADS,))] * 20,
        compiler_params=pltpu.CompilerParams(
            collective_id=0, has_side_effects=True, vmem_limit_bytes=60 * 1024 * 1024
        ),
    )(*args)


def call_wide(args):
    hbm = pl.BlockSpec(memory_space=pl.ANY)
    dma = pltpu.SemaphoreType.DMA
    grad = jax.ShapeDtypeStruct((ROWS, HEADS * HD), BF16)
    return pl.pallas_call(
        wide_kernel,
        out_shape=(grad, grad, grad),
        in_specs=[pl.BlockSpec(memory_space=pltpu.VMEM), hbm, hbm, hbm, hbm],
        out_specs=(hbm, hbm, hbm),
        scratch_shapes=[
            pltpu.VMEM((HEAD, 1, 128), I32),
            pltpu.VMEM((HEADS, ROWS, 4 * HD), BF16),
            pltpu.VMEM((HEADS, WIDE_SLOTS, 4 * HD), BF16),
            pltpu.VMEM((HEADS, WIDE_SLOTS, 4 * HD), BF16),
            pltpu.VMEM((NY, NZ, 1, 128), F32),
            pltpu.VMEM((NY, SEQ, 1, 128), F32),
            pltpu.VMEM((HEADS, ROWS, 4 * HD), BF16),
            pltpu.VMEM((HEADS, SPAN, 2 * HD), BF16),
            pltpu.VMEM((HEADS, SPAN, 2 * HD), BF16),
            pltpu.VMEM((HEADS, SPAN, 2 * HD), BF16),
            pltpu.VMEM((HEADS, ROWS, 3 * HD), BF16),
            pltpu.VMEM((HEADS, WIDE_SLOTS, 3 * HD), BF16),
            pltpu.VMEM((HEADS, WIDE_SLOTS, 3 * HD), BF16),
            pltpu.VMEM((HEADS, ROWS, 3 * HD), BF16),
            pltpu.VMEM((HEADS, ROWS, HD), F32),
            pltpu.VMEM((HEADS, ROWS, HD), F32),
            pltpu.VMEM((128, WIDE_SLOTS), BF16),
            pltpu.VMEM((8, ROWS), I32),
            pltpu.VMEM((ROWS, 128), I32),
            pltpu.VMEM((HEADS, 8, WIDE_SLOTS), I32),
            pltpu.VMEM((HEADS, WIDE_SLOTS, 128), I32),
            dma((HEADS, 4)),
            dma((HEADS, 3)),
            dma, dma, dma, dma,
            dma((HEADS,)), dma((HEADS,)), dma((HEADS,)), dma((HEADS,)),
            dma((HEADS,)), dma((HEADS,)), dma((HEADS,)), dma((HEADS,)),
        ],
        compiler_params=pltpu.CompilerParams(
            collective_id=1, has_side_effects=True, vmem_limit_bytes=60 * 1024 * 1024
        ),
    )(*args)


def hand_over(*refs):
    held, in_sem, out_sem = refs[6:]
    pieces = [(t, p) for p in range(4) for t in range(3)]

    def move(t, p, inward):
        part = pl.ds(p * (ROWS // 4), ROWS // 4)
        if inward:
            return pltpu.make_async_copy(refs[t].at[part], held.at[t, part], in_sem.at[t, p])
        return pltpu.make_async_copy(held.at[t, part], refs[t + 3].at[part], out_sem.at[t, p])

    for t, p in pieces:
        move(t, p, True).start()
    for t, p in pieces:
        move(t, p, True).wait()
        move(t, p, False).start()
    for t, p in pieces:
        move(t, p, False).wait()


def call_hand_over(grads):
    hbm = pl.BlockSpec(memory_space=pl.ANY)
    grad = jax.ShapeDtypeStruct((ROWS, HEADS * HD), BF16)
    return pl.pallas_call(
        hand_over, out_shape=(grad, grad, grad), in_specs=[hbm] * 3, out_specs=(hbm, hbm, hbm),
        scratch_shapes=[
            pltpu.VMEM((3, ROWS, HEADS * HD), BF16),
            pltpu.SemaphoreType.DMA((3, 4)),
            pltpu.SemaphoreType.DMA((3, 4)),
        ],
    )(*grads)


def local(cluster_id, queries, key_vectors, value_vectors, grad_output):
    args = (cluster_id.reshape(1, 128), queries, key_vectors, value_vectors, grad_output)
    dq, dk, dv, flag = call_kernel(args)
    grads = lax.cond(
        flag[0, 0] > 0.5, lambda given, done: call_wide(given), lambda given, done: done,
        args, (dq, dk, dv),
    )
    return call_hand_over(grads)


def solution(mesh):
    placed = (P(("seq", "head")),) + (P("seq", "head"),) * 4
    return jax.shard_map(
        local,
        mesh=mesh,
        in_specs=placed,
        out_specs=(P("seq", "head"),) * 3,
        check_vma=False,
    )
```

```python
import functools
import math

import jax
import jax.numpy as jnp
from jax import lax
from jax.experimental import pallas as pl
from jax.experimental.pallas import tpu as pltpu
from jax.sharding import PartitionSpec as P

MESH = pl.DeviceIdType.MESH
HD = 128
SPAN = 512
ROWS = 1024
SEQ = 32
HEAD = 8
NY = 4
NZ = 8
HEADS = 4
CAP = 32
DIRECT = SEQ * CAP
SIDE = 64
CROSS = 32
EXTRA = NY * SIDE
SLOTS = DIRECT + EXTRA
WIDE = 48
WIDE_SLOTS = SEQ * WIDE
QT = 256
FACTOR = 1.0 / math.sqrt(HD)
LOG2E = 1.4426950408889634
F32 = jnp.float32
BF16 = jnp.bfloat16
I32 = jnp.int32


def iota(shape, dim):
    return lax.broadcasted_iota(I32, shape, dim)


def onehot(mask):
    return jnp.where(mask, 1.0, 0.0).astype(BF16)


def mm(a, b):
    return jnp.dot(a, b, preferred_element_type=F32)


def mm_nt(a, b):
    return lax.dot_general(a, b, (((1,), (1,)), ((), ())), preferred_element_type=F32)


def aligned(value, size):
    return pl.multiple_of(value, size)


def column_hot(column, count):
    return jnp.concatenate(
        [onehot(column == iota((256, 128), 1) + 128 * c) for c in range(count)], axis=1
    )

def attend(rows, tail, grads, j, span, first):
    base = span * SPAN
    if span == 1:
        keys = rows[j, :, HD : 2 * HD]
        values = rows[j, :, 2 * HD : 3 * HD]
    else:
        keys = jnp.concatenate([tail[j, :, :HD], rows[j, :SPAN, HD : 2 * HD]], axis=0)
        values = jnp.concatenate([tail[j, :, HD:], rows[j, :SPAN, 2 * HD : 3 * HD]], axis=0)
    part_k = part_v = None
    for t in range(SPAN // QT):
        at = base + t * QT
        query = rows[j, at : at + QT, 0:HD]
        cot = rows[j, at : at + QT, 3 * HD : 4 * HD]
        scores = mm_nt(keys, query)
        if span == 0:
            gone = jnp.logical_and(iota((2 * SPAN, QT), 0) < SPAN, first)
            scores = jnp.where(gone, -jnp.inf, scores)
        top = jnp.max(scores, axis=0, keepdims=True)
        expo = jnp.exp2((scores - top) * (FACTOR * LOG2E))
        probs = expo * (1.0 / jnp.sum(expo, axis=0, keepdims=True))
        grad_probs = mm_nt(values, cot)
        delta = jnp.sum(probs * grad_probs, axis=0, keepdims=True)
        ds = (probs * (grad_probs - delta) * FACTOR).astype(BF16)
        pv = mm(probs.astype(BF16), cot)
        pk = mm(ds, query)
        part_k = pk if part_k is None else part_k + pk
        part_v = pv if part_v is None else part_v + pv
        dq = lax.dot_general(
            keys, ds, (((0,), (0,)), ((), ())), preferred_element_type=F32
        )
        grads[j, at : at + QT, 0:HD] = dq.T.astype(BF16)
    return part_k, part_v

def kernel(
    ids_ref, q_ref, k_ref, v_ref, g_ref, dq_ref, dk_ref, dv_ref, flag_ref,
    ids_buf, xin, send_f, recv_f, meta_s, meta_r, cnt_s, cnt_r, flag_s, flag_r, rows, tail,
    lead_s, lead_r, grads, send_r, recv_r, acc_k, acc_v, flat, send_row, send_col, pos_row,
    pos_col, spots, mb, mbt, mc, mct, a_r, b_s, b_r, c_s, cr_r, br_s, br_r, ar_s,
    in_sem, out_sem, ids_ss, ids_rs, meta_ss, meta_rs, cnt_ss, cnt_rs, flag_ss, flag_rs,
    fwd_ss, fwd_rs, ret_ss, ret_rs, tail_ss, tail_rs, lead_ss, lead_rs,
    a_ss, a_rs, b_ss, b_rs, c_ss, c_rs, cr_ss, cr_rs, br_ss, br_rs, ar_ss, ar_rs,
):
    me = lax.axis_index("seq")
    head = lax.axis_index("head")
    zi = me // NY
    yi = lax.rem(me, NY)

    def block_at(device, j):
        return (device // NY) * NY + lax.rem(lax.rem(device, NY) + NY - j, NY)

    def device_of(block, j):
        return (block // NY) * NY + lax.rem(lax.rem(block, NY) + j, NY)

    def peer(k):
        return lax.rem(me + k, SEQ)

    def remote(src, dst, ss, rs, seq, hd):
        return pltpu.make_async_remote_copy(
            src_ref=src, dst_ref=dst, send_sem=ss, recv_sem=rs,
            device_id=(seq, hd), device_id_type=MESH,
        )

    def wait_bytes(ref, sem):
        pltpu.make_async_copy(ref, ref, sem).wait()

    def in_copy(j, t):
        src = (q_ref, k_ref, v_ref, g_ref)[t]
        return pltpu.make_async_copy(
            src.at[:, pl.ds(aligned(j * HD, HD), HD)],
            xin.at[j, :, pl.ds(t * HD, HD)],
            in_sem.at[j, t],
        )

    def out_copy(j, t):
        dst = (dq_ref, dk_ref, dv_ref)[t]
        return pltpu.make_async_copy(
            xin.at[j, :, pl.ds(t * HD, HD)],
            dst.at[:, pl.ds(aligned(j * HD, HD), HD)],
            out_sem.at[j, t],
        )

    barrier = pltpu.get_barrier_semaphore()

    @pl.loop(1, SEQ)
    def _(k):
        pl.semaphore_signal(barrier, inc=1, device_id=(peer(k), head), device_id_type=MESH)

    @pl.loop(1, HEAD)
    def _(k):
        pl.semaphore_signal(
            barrier, inc=1, device_id=(me, lax.rem(head + k, HEAD)), device_id_type=MESH
        )

    @pl.loop(0, HEADS)
    def _(j):
        for t in range(4):
            in_copy(j, t).start()

    ids_buf[head] = ids_ref[...]
    pl.semaphore_wait(barrier, SEQ - 1 + HEAD - 1)

    @pl.loop(1, HEAD)
    def _(k):
        remote(
            ids_buf.at[head], ids_buf.at[head], ids_ss, ids_rs, me, lax.rem(head + k, HEAD)
        ).start()

    def slot_of(shape):
        col = iota(shape, 1)
        near = col < DIRECT
        past = col - DIRECT
        return (
            jnp.where(near, lax.shift_right_logical(col, 5), lax.shift_right_logical(past, 4)),
            jnp.where(near, col & 31, CAP + (past & 15)),
        )

    flat[...] = onehot(slot_of((128, DIRECT + 512))[1] == iota((128, DIRECT + 512), 0))
    upper = onehot(iota((128, 128), 0) < iota((128, 128), 1))
    sub = iota((SEQ, SEQ), 0)
    lan = iota((SEQ, SEQ), 1)
    below = onehot(lan < sub)
    below_z = onehot(
        jnp.logical_and(
            lan < sub, lax.shift_right_logical(lan, 2) == lax.shift_right_logical(sub, 2)
        )
    )
    row32 = iota((SEQ, 128), 0)
    row8 = iota((NZ, 128), 0)
    y_of = row32 & 3

    def quarter(value):
        return lax.shift_right_logical(value, 2)

    wait_bytes(ids_buf.at[pl.ds(0, HEAD - 1)], ids_rs)

    run = jnp.zeros((SEQ, 1), F32)
    owners, slots = [], []
    for c in range(ROWS // 128):
        owner = lax.shift_right_logical(ids_buf[c], 3)
        mine = jnp.where(row32 == owner, 1.0, 0.0)
        before = mm(mine.astype(BF16), upper) + run
        run = run + jnp.sum(mine, axis=1, keepdims=True)
        owners.append(owner)
        slots.append(jnp.sum(mine * before, axis=0, keepdims=True).astype(I32))

    past = jnp.maximum(jnp.broadcast_to(run, (SEQ, 128)) - float(CAP), 0.0)
    base_f = mm(below_z, past.astype(BF16))
    plane = onehot(quarter(iota((NZ, SEQ), 1)) == iota((NZ, SEQ), 0))
    cnt_s[...] = mm(plane, past.astype(BF16))
    cnt_r[yi] = cnt_s[...]

    @pl.loop(1, NY)
    def _(k):
        device = zi * NY + lax.rem(yi + k, NY)
        remote(cnt_s, cnt_r.at[yi], cnt_ss, cnt_rs, device, head).start()

    mine_e = cnt_s[...].astype(I32)
    offs = []
    for yy in range(NY):
        count = quarter(mine_e - ((yy - yi - row8 + 16) & 3) + 3).astype(F32)
        off = jnp.zeros((SEQ, 128), F32)
        for z in range(NZ - 1):
            off = off + jnp.where(quarter(row32) > z, count[z : z + 1, :], 0.0)
        offs.append(off)
    for c in range(ROWS // 128):
        owner, slot = owners[c], slots[c]
        mine = row32 == owner

        def pick(table):
            return jnp.sum(jnp.where(mine, table, 0.0), axis=0, keepdims=True).astype(I32)

        e = pick(base_f) + slot - CAP
        way = (e + yi + quarter(owner) + 64) & 3
        far = DIRECT + way * SIDE + quarter(e + 64) - 16
        for yy in range(NY):
            far = far + jnp.where(way == yy, pick(offs[yy]), 0)
        index = jnp.where(slot < CAP, owner * CAP + slot, far)
        send_row[:, c * 128 : (c + 1) * 128] = jnp.broadcast_to(index, (8, 128))

    def pack_tile(j, r0):
        choose = onehot(send_row[0:1, :] == iota((256, ROWS), 0) + r0)
        send_f[j, pl.ds(r0, 256), :] = mm(choose, xin[j]).astype(BF16)

    def y_peer(k):
        return lax.rem(yi + k, NY)

    def z_peer(k):
        return lax.rem(zi + k, NZ)

    def at_side(y):
        return pl.ds(aligned(y * SIDE, SIDE), SIDE)

    def at_cross(z):
        return pl.ds(aligned(z * CROSS, CROSS), CROSS)

    def at_extra(y):
        return pl.ds(aligned(DIRECT + y * SIDE, SIDE), SIDE)

    def stage_a(j):
        for t in range(4):
            in_copy(j, t).wait()
        pack_tile(j, DIRECT)

        @pl.loop(1, NY)
        def _(k):
            y = y_peer(k)
            remote(
                send_f.at[j, at_extra(y)], a_r.at[j, at_side(yi)], a_ss.at[j], a_rs.at[j],
                zi * NY + y, head,
            ).start()

        a_r[j, at_side(yi), :] = send_f[j, at_extra(yi), :]

    def stage_b(j):
        wait_bytes(a_r.at[j, pl.ds(0, EXTRA - SIDE)], a_rs.at[j])
        b_s[j] = mm(mb[...], a_r[j]).astype(BF16)

        @pl.loop(1, NZ)
        def _(k):
            z = z_peer(k)
            remote(
                b_s.at[j, at_cross(z)], b_r.at[j, at_cross(zi)], b_ss.at[j], b_rs.at[j],
                z * NY + yi, head,
            ).start()

        b_r[j, at_cross(zi), :] = b_s[j, at_cross(zi), :]

    def stage_c(j):
        wait_bytes(b_r.at[j, pl.ds(0, EXTRA - CROSS)], b_rs.at[j])
        c_s[j] = mm(mc[...], b_r[j]).astype(BF16)

        @pl.loop(1, NY)
        def _(k):
            y = y_peer(k)
            remote(
                c_s.at[j, at_side(lax.rem(y + NY - j, NY))], recv_f.at[j, at_extra(yi)],
                c_ss.at[j], c_rs.at[j], zi * NY + y, head,
            ).start()

        recv_f[j, at_extra(yi), :] = c_s[j, at_side(lax.rem(yi + NY - j, NY)), :]

    def pack_forward(j):
        @pl.loop(0, DIRECT // 256)
        def _(t):
            tile = lax.rem(zi // 2 + t, DIRECT // 256)
            pack_tile(j, aligned(tile * 256, 256))

            @pl.loop(0, 256 // CAP)
            def _(k):
                block = tile * (256 // CAP) + lax.rem(me + k, 256 // CAP)
                device = device_of(block, j)
                source = aligned(block * CAP, CAP)

                @pl.when(device != me)
                def _():
                    remote(
                        send_f.at[j, pl.ds(source, CAP)],
                        recv_f.at[j, pl.ds(aligned(me * CAP, CAP), CAP)],
                        fwd_ss.at[j], fwd_rs.at[j], device, head,
                    ).start()

        own = aligned(block_at(me, j) * CAP, CAP)
        recv_f[j, pl.ds(aligned(me * CAP, CAP), CAP), :] = send_f[j, pl.ds(own, CAP), :]

    stage_a(0)
    pack_forward(0)

    @pl.loop(1, HEADS)
    def _(j):
        stage_a(j)

    meta = jnp.zeros((SEQ, 128), F32)
    for c in range(ROWS // 128):
        cluster = (ids_buf[c] & 7).astype(F32) + 1.0
        mine = jnp.where(row32 == owners[c], cluster, 0.0)
        meta = meta + mm_nt(mine.astype(BF16), onehot(iota((128, 128), 0) == slots[c]))
    for b in range(SEQ):
        meta_s[b % NY, b // NY] = meta[b : b + 1, :]

    @pl.loop(1, SEQ)
    def _(k):
        device = peer(k)
        remote(
            meta_s.at[:, device // NY], meta_r.at[:, me], meta_ss, meta_rs, device, head
        ).start()

    for b in range(NY):
        meta_r[b, me] = meta_s[b, zi]
    wait_bytes(cnt_r.at[pl.ds(0, NY - 1)], cnt_rs)

    bad = jnp.zeros((1, 128), F32)
    starts_a, starts_b, counts = [], [], []
    filled = jnp.zeros((NZ, 128), I32)
    for y in range(NY):
        for yy in range(NY):
            share = quarter(cnt_r[y].astype(I32) - ((yy - y - row8 + 16) & 3) + 3)
            total = jnp.sum(share.astype(F32), axis=0, keepdims=True)
            bad = jnp.maximum(bad, total - float(SIDE))
        share = quarter(cnt_r[y].astype(I32) - ((yi - y - row8 + 16) & 3) + 3)
        start = jnp.zeros((NZ, 128), I32)
        for z in range(NZ - 1):
            start = start + jnp.where(row8 > z, share[z : z + 1, :], 0)
        starts_a.append(start)
        starts_b.append(filled)
        counts.append(share)
        filled = filled + share
    for yy in range(NY):
        total = jnp.zeros((NZ, 128), I32)
        for y in range(NY):
            total = total + quarter(cnt_r[y].astype(I32) - ((yy - y - row8 + 16) & 3) + 3)
        bad = jnp.maximum(
            bad, jnp.max(total.astype(F32), axis=0, keepdims=True) - float(CROSS)
        )

    def by_group(tables):
        group = lax.shift_right_logical(iota((NZ, EXTRA), 1), 6)
        result = jnp.zeros((NZ, EXTRA), I32)
        for y in range(NY):
            result = jnp.where(group == y, jnp.concatenate([tables[y]] * 2, axis=1), result)
        return result

    wide_a, wide_b, wide_c = by_group(starts_a), by_group(starts_b), by_group(counts)
    for z in range(NZ):
        step = iota((CROSS, EXTRA), 0) - wide_b[z : z + 1, :]
        place = (iota((CROSS, EXTRA), 1) & (SIDE - 1)) - wide_a[z : z + 1, :]
        hit = jnp.logical_and(
            jnp.logical_and(step >= 0, step < wide_c[z : z + 1, :]), step == place
        )
        mb[z * CROSS : (z + 1) * CROSS, :] = onehot(hit)
    mbt[...] = mb[...].astype(F32).T.astype(BF16)

    stage_b(0)
    pack_forward(1)

    @pl.loop(1, HEADS)
    def _(j):
        stage_b(j)

    for c in range(ROWS // 128):
        send_col[c * 128 : (c + 1) * 128, :] = (
            jnp.broadcast_to(send_row[0:1, c * 128 : (c + 1) * 128], (128, 128))
            .astype(F32).T.astype(I32)
        )
    wait_bytes(meta_r.at[:, pl.ds(0, SEQ - 1)], meta_rs)

    bases = [jnp.zeros((SEQ, 128), I32)]
    for b in range(NY):
        held = jnp.where(meta_r[b].reshape(SEQ, 128) > 0.5, 1.0, 0.0)
        held = jnp.maximum(jnp.sum(held, axis=1, keepdims=True) - float(CAP), 0.0)
        bases.append(bases[b] + jnp.broadcast_to(held, (SEQ, 128)).astype(I32))
    firsts = []
    for yy in range(NY):
        residue = (yy - y_of - zi + 16) & 3
        firsts.append([quarter(base - residue + 3) for base in bases])
    lengths = [[f[b + 1] - f[b] for b in range(NY)] for f in firsts]
    stacked = jnp.concatenate([v.astype(F32) for f in lengths for v in f], axis=1)
    before_c = mm(below, stacked.astype(BF16))
    landing = []
    for yy in range(NY):
        landing.append([])
        for b in range(NY):
            at = (yy * NY + b) * 128
            part = before_c[:, at : at + 128].astype(I32)
            landing[yy].append(part)
            total = (part + lengths[yy][b])[SEQ - 1 : SEQ, :].astype(F32)
            bad = jnp.maximum(bad, total - float(SIDE))
    lane = iota((SEQ, 128), 1)
    for b in range(NY):
        e = bases[b] + lane - CAP
        way = (e + y_of + zi + 64) & 3
        spot = jnp.zeros((SEQ, 128), I32)
        for yy in range(NY):
            here = yy * SIDE + landing[yy][b] + quarter(e + 64) - 16 - firsts[yy][b]
            spot = jnp.where(way == yy, here, spot)
        used = jnp.logical_and(meta_r[b].reshape(SEQ, 128) > 0.5, lane >= CAP)
        spots[b] = jnp.where(used, spot.astype(F32), -1.0)

    def chosen(tables):
        result = tables[0]
        for yy in range(1, NY):
            result = jnp.where(yi == yy, tables[yy], result)
        return result

    my_total = chosen([f[NY] for f in firsts])
    my_start = mm(below_z, my_total.astype(F32).astype(BF16))
    col = iota((SEQ, EXTRA), 1)
    for b in range(NY):
        landing_b = chosen([landing[yy][b] for yy in range(NY)]).astype(F32)
        length_b = chosen([lengths[yy][b] for yy in range(NY)]).astype(F32)
        source_b = my_start + chosen([firsts[yy][b] for yy in range(NY)]).astype(F32)
        found = jnp.zeros((SIDE, EXTRA), F32)
        for y in range(NY):
            match = iota((SEQ, EXTRA), 0) == lax.shift_right_logical(col, 5) * NY + y

            def across(table):
                twice = jnp.concatenate([table, table], axis=1)
                return jnp.sum(jnp.where(match, twice, 0.0), axis=0, keepdims=True).astype(I32)

            step = iota((SIDE, EXTRA), 0) - across(landing_b)
            place = (iota((SIDE, EXTRA), 1) & (CROSS - 1)) - across(source_b)
            hit = jnp.logical_and(
                jnp.logical_and(step >= 0, step < across(length_b)), step == place
            )
            found = found + jnp.where(hit, 1.0, 0.0)
        mc[b * SIDE : (b + 1) * SIDE, :] = found.astype(BF16)
    mct[...] = mc[...].astype(F32).T.astype(BF16)

    flag_s[...] = jnp.broadcast_to(jnp.where(bad > 0.5, 1.0, 0.0), (8, 128))
    flag_r[zi] = flag_s[...]

    @pl.loop(1, NZ)
    def _(k):
        remote(
            flag_s, flag_r.at[zi], flag_ss, flag_rs, z_peer(k) * NY + yi, head
        ).start()

    stage_c(0)

    def positions(j):
        block = lax.rem(yi + NY - j, NY)
        m = meta_r[block].reshape(SEQ, 128)
        hot = jnp.concatenate([jnp.where(m == c + 1.0, 1.0, 0.0) for c in range(8)], axis=0)
        within = mm(hot.astype(BF16), upper)
        total = jnp.broadcast_to(jnp.sum(hot, axis=1, keepdims=True), (8 * SEQ, 128))
        lower = onehot(iota((8 * SEQ, 8 * SEQ), 1) < iota((8 * SEQ, 8 * SEQ), 0))
        placed = hot * (mm(lower, total.astype(BF16)) + within)
        pos = jnp.where(m > 0.5, 0.0, -1.0)
        for c in range(8):
            pos = pos + placed[c * SEQ : (c + 1) * SEQ, :]

        def halves(value):
            high = jnp.floor(value * (1.0 / 32.0))
            return [high, value - high * 32.0]

        parts = mm(
            jnp.concatenate(halves(pos) + halves(spots[block]), axis=0).astype(BF16), flat[...]
        )
        mine = iota((SEQ, DIRECT + 512), 0) == slot_of((SEQ, DIRECT + 512))[0]
        spread = jnp.where(mine, parts[:SEQ] * 32.0 + parts[SEQ : 2 * SEQ], 0.0)
        line = jnp.sum(spread, axis=0, keepdims=True)
        spread = jnp.where(mine, parts[2 * SEQ : 3 * SEQ] * 32.0 + parts[3 * SEQ :], 0.0)
        target = jnp.sum(spread, axis=0, keepdims=True)[:, DIRECT:].astype(I32)
        high, low = halves(line[:, DIRECT:] + 1.0)
        pair = jnp.concatenate(
            [jnp.broadcast_to(high, (8, 512)), jnp.broadcast_to(low, (8, 512))], axis=0
        )
        found = mm_nt(pair.astype(BF16), onehot(iota((EXTRA, 512), 0) == target))
        extra = found[0:1, :] * 32.0 + found[8:9, :] - 1.0
        row = jnp.concatenate([line[:, :DIRECT], extra], axis=1)
        pos_row[j] = jnp.broadcast_to(row, (8, SLOTS)).astype(I32)
        for c in range(SLOTS // 128):
            piece = row[:, c * 128 : (c + 1) * 128]
            pos_col[j, c * 128 : (c + 1) * 128, :] = (
                jnp.broadcast_to(piece, (128, 128)).T.astype(I32)
            )

    def tail_copy(j):
        after = device_of(lax.rem(block_at(me, j) + 1, SEQ), j)
        return remote(
            rows.at[j, pl.ds(SPAN, SPAN), pl.ds(HD, 2 * HD)], tail.at[j],
            tail_ss.at[j], tail_rs.at[j], after, head,
        )

    def lead_copy(j):
        prior = device_of(lax.rem(block_at(me, j) + SEQ - 1, SEQ), j)
        return remote(lead_s.at[j], lead_r.at[j], lead_ss.at[j], lead_rs.at[j], prior, head)

    def open_chunk(j):
        positions(j)
        wait_bytes(recv_f.at[j, pl.ds(0, DIRECT - CAP)], fwd_rs.at[j])
        wait_bytes(recv_f.at[j, pl.ds(0, EXTRA - SIDE)], c_rs.at[j])

        @pl.loop(0, ROWS // 256)
        def _(t):
            r0 = aligned(t * 256, 256)
            choose = onehot(pos_row[j, 0:1, :] == iota((256, SLOTS), 0) + r0)
            rows[j, pl.ds(r0, 256), :] = mm(choose, recv_f[j]).astype(BF16)

        tail_copy(j).start()

    def last_span(j):
        part_k, part_v = attend(rows, tail, grads, j, 1, block_at(me, j) == 0)
        acc_k[j] = part_k
        acc_v[j] = part_v

    def first_span(j):
        tail_copy(j).wait_recv()
        part_k, part_v = attend(rows, tail, grads, j, 0, block_at(me, j) == 0)
        lead_s[j, :, :HD] = part_k[:SPAN].astype(BF16)
        lead_s[j, :, HD:] = part_v[:SPAN].astype(BF16)
        lead_copy(j).start()
        grads[j, :SPAN, HD : 2 * HD] = (acc_k[j, :SPAN] + part_k[SPAN:]).astype(BF16)
        grads[j, :SPAN, 2 * HD :] = (acc_v[j, :SPAN] + part_v[SPAN:]).astype(BF16)

    def back_b(j):
        wait_bytes(cr_r.at[j, pl.ds(0, EXTRA - SIDE)], cr_rs.at[j])
        br_s[j] = mm(mct[...], cr_r[j]).astype(BF16)

        @pl.loop(1, NZ)
        def _(k):
            z = z_peer(k)
            remote(
                br_s.at[j, at_cross(z)], br_r.at[j, at_cross(zi)], br_ss.at[j], br_rs.at[j],
                z * NY + yi, head,
            ).start()

        br_r[j, at_cross(zi), :] = br_s[j, at_cross(zi), :]

    def close_chunk(j):
        lead_copy(j).wait_recv()
        grads[j, SPAN:, HD : 2 * HD] = (
            acc_k[j, SPAN:] + lead_r[j, :, :HD].astype(F32)
        ).astype(BF16)
        grads[j, SPAN:, 2 * HD :] = (
            acc_v[j, SPAN:] + lead_r[j, :, HD:].astype(F32)
        ).astype(BF16)

        def pack_back(r0):
            choose = column_hot(pos_col[j, pl.ds(r0, 256), :], ROWS // 128)
            send_r[j, pl.ds(r0, 256), :] = mm(choose, grads[j]).astype(BF16)

        pack_back(DIRECT)
        own_y = lax.rem(yi + NY - j, NY)

        @pl.loop(1, NY)
        def _(k):
            y = y_peer(k)
            remote(
                send_r.at[j, at_extra(y)], cr_r.at[j, at_side(own_y)], cr_ss.at[j],
                cr_rs.at[j], zi * NY + y, head,
            ).start()

        cr_r[j, at_side(own_y), :] = send_r[j, at_extra(yi), :]

        @pl.loop(0, DIRECT // 256)
        def _(t):
            pack_back(aligned(t * 256, 256))

        own = aligned(block_at(me, j) * CAP, CAP)

        def send_back(k):
            device = peer(k)
            remote(
                send_r.at[j, pl.ds(aligned(device * CAP, CAP), CAP)],
                recv_r.at[j, pl.ds(own, CAP)],
                ret_ss.at[j], ret_rs.at[j], device, head,
            ).start()

        @pl.loop(1, SEQ // 2)
        def _(k):
            send_back(k)

        @pl.when(j == HEADS - 1)
        def _():
            back_b(j)

        @pl.loop(SEQ // 2, SEQ)
        def _(k):
            send_back(k)

        recv_r[j, pl.ds(own, CAP), :] = send_r[j, pl.ds(aligned(me * CAP, CAP), CAP), :]

    def back_a(j):
        wait_bytes(br_r.at[j, pl.ds(0, EXTRA - CROSS)], br_rs.at[j])
        ar_s[j] = mm(mbt[...], br_r[j]).astype(BF16)

        @pl.loop(1, NY)
        def _(k):
            y = y_peer(k)
            remote(
                ar_s.at[j, at_side(y)], recv_r.at[j, at_extra(yi)], ar_ss.at[j], ar_rs.at[j],
                zi * NY + y, head,
            ).start()

        recv_r[j, at_extra(yi), :] = ar_s[j, at_side(yi), :]

    @pl.loop(0, HEADS + 4)
    def _(i):
        @pl.when(i < HEADS)
        def _():
            open_chunk(i)

        @pl.when(jnp.logical_and(i >= 1, i <= HEADS))
        def _():
            first_span(i - 1)

        @pl.when(i < 1)
        def _():
            stage_c(1)

        @pl.when(i < HEADS - 2)
        def _():
            pack_forward(i + 2)
            stage_c(i + 2)

        @pl.when(jnp.logical_and(i >= 3, i < HEADS + 2))
        def _():
            back_b(i - 3)

        @pl.when(jnp.logical_and(i >= 2, i < HEADS + 2))
        def _():
            close_chunk(i - 2)

        @pl.when(i < HEADS)
        def _():
            last_span(i)

        @pl.when(i >= 4)
        def _():
            back_a(i - 4)

    @pl.loop(0, HEADS)
    def _(j):
        wait_bytes(recv_r.at[j, pl.ds(0, DIRECT - CAP)], ret_rs.at[j])
        wait_bytes(recv_r.at[j, pl.ds(0, EXTRA - SIDE)], ar_rs.at[j])

        @pl.loop(0, ROWS // 256)
        def _(t):
            r0 = aligned(t * 256, 256)
            choose = column_hot(send_col[pl.ds(r0, 256), :], SLOTS // 128)
            xin[j, pl.ds(r0, 256), : 3 * HD] = mm(choose, recv_r[j]).astype(BF16)

        for t in range(3):
            out_copy(j, t).start()

    wait_bytes(flag_r.at[pl.ds(0, NZ - 1)], flag_rs)
    flag_ref[0, 0] = jnp.max(flag_r[...])
    wait_bytes(ids_buf.at[pl.ds(0, HEAD - 1)], ids_ss)
    wait_bytes(meta_r.at[:, pl.ds(0, SEQ - 1)], meta_ss)
    wait_bytes(cnt_r.at[pl.ds(0, NY - 1)], cnt_ss)
    wait_bytes(flag_r.at[pl.ds(0, NZ - 1)], flag_ss)

    @pl.loop(0, HEADS)
    def _(j):
        wait_bytes(send_f.at[j, pl.ds(0, DIRECT - CAP)], fwd_ss.at[j])
        wait_bytes(send_r.at[j, pl.ds(0, DIRECT - CAP)], ret_ss.at[j])
        wait_bytes(a_r.at[j, pl.ds(0, EXTRA - SIDE)], a_ss.at[j])
        wait_bytes(b_r.at[j, pl.ds(0, EXTRA - CROSS)], b_ss.at[j])
        wait_bytes(c_s.at[j, pl.ds(0, EXTRA - SIDE)], c_ss.at[j])
        wait_bytes(cr_r.at[j, pl.ds(0, EXTRA - SIDE)], cr_ss.at[j])
        wait_bytes(br_r.at[j, pl.ds(0, EXTRA - CROSS)], br_ss.at[j])
        wait_bytes(ar_s.at[j, pl.ds(0, EXTRA - SIDE)], ar_ss.at[j])
        wait_bytes(tail.at[j], tail_ss.at[j])
        wait_bytes(lead_s.at[j], lead_ss.at[j])
        for t in range(3):
            out_copy(j, t).wait()


def wide_kernel(
    ids_ref, q_ref, k_ref, v_ref, g_ref, dq_ref, dk_ref, dv_ref,
    ids_buf, xin, send_f, recv_f, meta_s, meta_r, rows, tail, lead_s, lead_r,
    grads, send_r, recv_r, outs, acc_k, acc_v, flat, send_row, send_col, pos_row, pos_col,
    in_sem, out_sem, ids_ss, ids_rs, meta_ss, meta_rs, fwd_ss, fwd_rs, ret_ss, ret_rs,
    tail_ss, tail_rs, lead_ss, lead_rs,
):
    me = lax.axis_index("seq")
    head = lax.axis_index("head")
    zi = me // NY
    yi = lax.rem(me, NY)

    def block_at(device, j):
        return (device // NY) * NY + lax.rem(lax.rem(device, NY) + NY - j, NY)

    def device_of(block, j):
        return (block // NY) * NY + lax.rem(lax.rem(block, NY) + j, NY)

    def peer(k):
        return lax.rem(me + k, SEQ)

    def remote(src, dst, ss, rs, seq, hd):
        return pltpu.make_async_remote_copy(
            src_ref=src, dst_ref=dst, send_sem=ss, recv_sem=rs,
            device_id=(seq, hd), device_id_type=MESH,
        )

    def wait_bytes(ref, sem):
        pltpu.make_async_copy(ref, ref, sem).wait()

    def in_copy(j, t):
        src = (q_ref, k_ref, v_ref, g_ref)[t]
        return pltpu.make_async_copy(
            src.at[:, pl.ds(aligned(j * HD, HD), HD)],
            xin.at[j, :, pl.ds(t * HD, HD)],
            in_sem.at[j, t],
        )

    def out_copy(j, t):
        dst = (dq_ref, dk_ref, dv_ref)[t]
        return pltpu.make_async_copy(
            outs.at[j, :, pl.ds(t * HD, HD)],
            dst.at[:, pl.ds(aligned(j * HD, HD), HD)],
            out_sem.at[j, t],
        )

    barrier = pltpu.get_barrier_semaphore()

    @pl.loop(1, SEQ)
    def _(k):
        pl.semaphore_signal(barrier, inc=1, device_id=(peer(k), head), device_id_type=MESH)

    @pl.loop(1, HEAD)
    def _(k):
        pl.semaphore_signal(
            barrier, inc=1, device_id=(me, lax.rem(head + k, HEAD)), device_id_type=MESH
        )

    @pl.loop(0, HEADS)
    def _(j):
        for t in range(4):
            in_copy(j, t).start()

    ids_buf[head] = ids_ref[...]
    pl.semaphore_wait(barrier, SEQ - 1 + HEAD - 1)

    @pl.loop(1, HEAD)
    def _(k):
        remote(
            ids_buf.at[head], ids_buf.at[head], ids_ss, ids_rs, me, lax.rem(head + k, HEAD)
        ).start()

    lane = iota((128, WIDE_SLOTS), 1)
    source_of = lax.shift_right_logical(lane * 1366, 16)
    flat[...] = onehot(lane - source_of * WIDE == iota((128, WIDE_SLOTS), 0))
    upper = onehot(iota((128, 128), 0) < iota((128, 128), 1))
    wait_bytes(ids_buf.at[pl.ds(0, HEAD - 1)], ids_rs)

    run = jnp.zeros((SEQ, 1), F32)
    meta = jnp.zeros((SEQ, 128), F32)
    for c in range(ROWS // 128):
        idc = ids_buf[c]
        owner = lax.shift_right_logical(idc, 3)
        cluster = (idc & 7).astype(F32) + 1.0
        mine = jnp.where(iota((SEQ, 128), 0) == owner, 1.0, 0.0)
        before = mm(mine.astype(BF16), upper) + run
        run = run + jnp.sum(mine, axis=1, keepdims=True)
        slot = jnp.sum(mine * before, axis=0, keepdims=True).astype(I32)
        index = owner * WIDE + slot
        send_row[:, c * 128 : (c + 1) * 128] = jnp.broadcast_to(index, (8, 128))
        send_col[c * 128 : (c + 1) * 128, :] = (
            jnp.broadcast_to(index, (128, 128)).astype(F32).T.astype(I32)
        )
        meta = meta + mm_nt((mine * cluster).astype(BF16), onehot(iota((128, 128), 0) == slot))
    for b in range(SEQ):
        meta_s[b % NY, b // NY] = meta[b : b + 1, :]

    @pl.loop(1, SEQ)
    def _(k):
        device = peer(k)
        remote(
            meta_s.at[:, device // NY], meta_r.at[:, me], meta_ss, meta_rs, device, head
        ).start()

    for b in range(NY):
        meta_r[b, me] = meta_s[b, zi]

    def pack_forward(j):
        for t in range(4):
            in_copy(j, t).wait()

        @pl.loop(0, WIDE_SLOTS // 256)
        def _(t):
            r0 = aligned(t * 256, 256)
            choose = onehot(send_row[0:1, :] == iota((256, ROWS), 0) + r0)
            send_f[j, pl.ds(r0, 256), :] = mm(choose, xin[j]).astype(BF16)

        @pl.loop(1, SEQ)
        def _(k):
            device = peer(k)
            start = aligned(block_at(device, j) * WIDE, WIDE)
            remote(
                send_f.at[j, pl.ds(start, WIDE)],
                recv_f.at[j, pl.ds(aligned(me * WIDE, WIDE), WIDE)],
                fwd_ss.at[j], fwd_rs.at[j], device, head,
            ).start()

        own = aligned(block_at(me, j) * WIDE, WIDE)
        recv_f[j, pl.ds(aligned(me * WIDE, WIDE), WIDE), :] = send_f[j, pl.ds(own, WIDE), :]

    @pl.loop(0, 2)
    def _(j):
        pack_forward(j)

    wait_bytes(meta_r.at[:, pl.ds(0, SEQ - 1)], meta_rs)

    def positions(j):
        m = meta_r[lax.rem(yi + NY - j, NY)].reshape(SEQ, 128)
        hot = jnp.concatenate([jnp.where(m == c + 1.0, 1.0, 0.0) for c in range(8)], axis=0)
        within = mm(hot.astype(BF16), upper)
        total = jnp.broadcast_to(jnp.sum(hot, axis=1, keepdims=True), (8 * SEQ, 128))
        lower = onehot(iota((8 * SEQ, 8 * SEQ), 1) < iota((8 * SEQ, 8 * SEQ), 0))
        placed = hot * (mm(lower, total.astype(BF16)) + within)
        pos = jnp.where(m > 0.5, 0.0, -1.0)
        for c in range(8):
            pos = pos + placed[c * SEQ : (c + 1) * SEQ, :]
        high = jnp.floor(pos * (1.0 / 32.0))
        low = pos - high * 32.0
        parts = mm(jnp.concatenate([high, low], axis=0).astype(BF16), flat[...])
        spread = parts[:SEQ] * 32.0 + parts[SEQ:]
        mine = iota((SEQ, WIDE_SLOTS), 0) == lax.shift_right_logical(iota((SEQ, WIDE_SLOTS), 1) * 1366, 16)
        row = jnp.sum(jnp.where(mine, spread, 0.0), axis=0, keepdims=True)
        pos_row[j] = jnp.broadcast_to(row, (8, WIDE_SLOTS)).astype(I32)
        for c in range(WIDE_SLOTS // 128):
            piece = row[:, c * 128 : (c + 1) * 128]
            pos_col[j, c * 128 : (c + 1) * 128, :] = (
                jnp.broadcast_to(piece, (128, 128)).T.astype(I32)
            )

    def tail_copy(j):
        after = device_of(lax.rem(block_at(me, j) + 1, SEQ), j)
        return remote(
            rows.at[j, pl.ds(SPAN, SPAN), pl.ds(HD, 2 * HD)], tail.at[j],
            tail_ss.at[j], tail_rs.at[j], after, head,
        )

    def lead_copy(j):
        prior = device_of(lax.rem(block_at(me, j) + SEQ - 1, SEQ), j)
        return remote(lead_s.at[j], lead_r.at[j], lead_ss.at[j], lead_rs.at[j], prior, head)

    def open_chunk(j):
        positions(j)
        wait_bytes(recv_f.at[j, pl.ds(0, WIDE_SLOTS - WIDE)], fwd_rs.at[j])

        @pl.loop(0, ROWS // 256)
        def _(t):
            r0 = aligned(t * 256, 256)
            choose = onehot(pos_row[j, 0:1, :] == iota((256, WIDE_SLOTS), 0) + r0)
            rows[j, pl.ds(r0, 256), :] = mm(choose, recv_f[j]).astype(BF16)

        tail_copy(j).start()

    def last_span(j):
        part_k, part_v = attend(rows, tail, grads, j, 1, block_at(me, j) == 0)
        acc_k[j] = part_k
        acc_v[j] = part_v

    def first_span(j):
        tail_copy(j).wait_recv()
        part_k, part_v = attend(rows, tail, grads, j, 0, block_at(me, j) == 0)
        lead_s[j, :, :HD] = part_k[:SPAN].astype(BF16)
        lead_s[j, :, HD:] = part_v[:SPAN].astype(BF16)
        lead_copy(j).start()
        grads[j, :SPAN, HD : 2 * HD] = (acc_k[j, :SPAN] + part_k[SPAN:]).astype(BF16)
        grads[j, :SPAN, 2 * HD :] = (acc_v[j, :SPAN] + part_v[SPAN:]).astype(BF16)

    def close_chunk(j):
        lead_copy(j).wait_recv()
        grads[j, SPAN:, HD : 2 * HD] = (
            acc_k[j, SPAN:] + lead_r[j, :, :HD].astype(F32)
        ).astype(BF16)
        grads[j, SPAN:, 2 * HD :] = (
            acc_v[j, SPAN:] + lead_r[j, :, HD:].astype(F32)
        ).astype(BF16)

        @pl.loop(0, WIDE_SLOTS // 256)
        def _(t):
            r0 = aligned(t * 256, 256)
            choose = column_hot(pos_col[j, pl.ds(r0, 256), :], ROWS // 128)
            send_r[j, pl.ds(r0, 256), :] = mm(choose, grads[j]).astype(BF16)

        own = aligned(block_at(me, j) * WIDE, WIDE)

        @pl.loop(1, SEQ)
        def _(k):
            device = peer(k)
            remote(
                send_r.at[j, pl.ds(aligned(device * WIDE, WIDE), WIDE)],
                recv_r.at[j, pl.ds(own, WIDE)],
                ret_ss.at[j], ret_rs.at[j], device, head,
            ).start()

        recv_r[j, pl.ds(own, WIDE), :] = send_r[j, pl.ds(aligned(me * WIDE, WIDE), WIDE), :]

    @pl.loop(0, HEADS + 2)
    def _(i):
        @pl.when(i < HEADS)
        def _():
            open_chunk(i)

        @pl.when(i < HEADS - 2)
        def _():
            pack_forward(i + 2)

        @pl.when(jnp.logical_and(i >= 1, i <= HEADS))
        def _():
            first_span(i - 1)

        @pl.when(i < HEADS)
        def _():
            last_span(i)

        @pl.when(i >= 2)
        def _():
            close_chunk(i - 2)

    @pl.loop(0, HEADS)
    def _(j):
        wait_bytes(recv_r.at[j, pl.ds(0, WIDE_SLOTS - WIDE)], ret_rs.at[j])

        @pl.loop(0, ROWS // 256)
        def _(t):
            r0 = aligned(t * 256, 256)
            choose = column_hot(send_col[pl.ds(r0, 256), :], WIDE_SLOTS // 128)
            outs[j, pl.ds(r0, 256), :] = mm(choose, recv_r[j]).astype(BF16)

        for t in range(3):
            out_copy(j, t).start()

    wait_bytes(ids_buf.at[pl.ds(0, HEAD - 1)], ids_ss)
    wait_bytes(meta_r.at[:, pl.ds(0, SEQ - 1)], meta_ss)

    @pl.loop(0, HEADS)
    def _(j):
        wait_bytes(send_f.at[j, pl.ds(0, WIDE_SLOTS - WIDE)], fwd_ss.at[j])
        wait_bytes(send_r.at[j, pl.ds(0, WIDE_SLOTS - WIDE)], ret_ss.at[j])
        wait_bytes(tail.at[j], tail_ss.at[j])
        wait_bytes(lead_s.at[j], lead_ss.at[j])
        for t in range(3):
            out_copy(j, t).wait()


def call_kernel(args):
    hbm = pl.BlockSpec(memory_space=pl.ANY)
    near = pl.BlockSpec(memory_space=pltpu.VMEM)
    dma = pltpu.SemaphoreType.DMA
    grad = jax.ShapeDtypeStruct((ROWS, HEADS * HD), BF16)
    step = pltpu.VMEM((HEADS, EXTRA, 4 * HD), BF16)
    back = pltpu.VMEM((HEADS, EXTRA, 3 * HD), BF16)
    square = pltpu.VMEM((EXTRA, EXTRA), BF16)
    return pl.pallas_call(
        kernel,
        out_shape=(grad, grad, grad, jax.ShapeDtypeStruct((1, 1), F32)),
        in_specs=[near, hbm, hbm, hbm, hbm],
        out_specs=(hbm, hbm, hbm, pl.BlockSpec(memory_space=pltpu.SMEM)),
        scratch_shapes=[
            pltpu.VMEM((HEAD, 1, 128), I32),
            pltpu.VMEM((HEADS, ROWS, 4 * HD), BF16),
            pltpu.VMEM((HEADS, SLOTS, 4 * HD), BF16),
            pltpu.VMEM((HEADS, SLOTS, 4 * HD), BF16),
            pltpu.VMEM((NY, NZ, 1, 128), F32),
            pltpu.VMEM((NY, SEQ, 1, 128), F32),
            pltpu.VMEM((NZ, 128), F32),
            pltpu.VMEM((NY, NZ, 128), F32),
            pltpu.VMEM((8, 128), F32),
            pltpu.VMEM((NZ, 8, 128), F32),
            pltpu.VMEM((HEADS, ROWS, 4 * HD), BF16),
            pltpu.VMEM((HEADS, SPAN, 2 * HD), BF16),
            pltpu.VMEM((HEADS, SPAN, 2 * HD), BF16),
            pltpu.VMEM((HEADS, SPAN, 2 * HD), BF16),
            pltpu.VMEM((HEADS, ROWS, 3 * HD), BF16),
            pltpu.VMEM((HEADS, SLOTS, 3 * HD), BF16),
            pltpu.VMEM((HEADS, SLOTS, 3 * HD), BF16),
            pltpu.VMEM((HEADS, ROWS, HD), F32),
            pltpu.VMEM((HEADS, ROWS, HD), F32),
            pltpu.VMEM((128, DIRECT + 512), BF16),
            pltpu.VMEM((8, ROWS), I32),
            pltpu.VMEM((ROWS, 128), I32),
            pltpu.VMEM((HEADS, 8, SLOTS), I32),
            pltpu.VMEM((HEADS, SLOTS, 128), I32),
            pltpu.VMEM((NY, SEQ, 128), F32),
            square, square, square, square,
            step, step, step, step, back, back, back, back,
            dma((HEADS, 4)),
            dma((HEADS, 3)),
        ]
        + [dma] * 8
        + [dma((HEADS,))] * 20,
        compiler_params=pltpu.CompilerParams(
            collective_id=0, has_side_effects=True, vmem_limit_bytes=60 * 1024 * 1024
        ),
    )(*args)


def call_wide(args):
    hbm = pl.BlockSpec(memory_space=pl.ANY)
    dma = pltpu.SemaphoreType.DMA
    grad = jax.ShapeDtypeStruct((ROWS, HEADS * HD), BF16)
    return pl.pallas_call(
        wide_kernel,
        out_shape=(grad, grad, grad),
        in_specs=[pl.BlockSpec(memory_space=pltpu.VMEM), hbm, hbm, hbm, hbm],
        out_specs=(hbm, hbm, hbm),
        scratch_shapes=[
            pltpu.VMEM((HEAD, 1, 128), I32),
            pltpu.VMEM((HEADS, ROWS, 4 * HD), BF16),
            pltpu.VMEM((HEADS, WIDE_SLOTS, 4 * HD), BF16),
            pltpu.VMEM((HEADS, WIDE_SLOTS, 4 * HD), BF16),
            pltpu.VMEM((NY, NZ, 1, 128), F32),
            pltpu.VMEM((NY, SEQ, 1, 128), F32),
            pltpu.VMEM((HEADS, ROWS, 4 * HD), BF16),
            pltpu.VMEM((HEADS, SPAN, 2 * HD), BF16),
            pltpu.VMEM((HEADS, SPAN, 2 * HD), BF16),
            pltpu.VMEM((HEADS, SPAN, 2 * HD), BF16),
            pltpu.VMEM((HEADS, ROWS, 3 * HD), BF16),
            pltpu.VMEM((HEADS, WIDE_SLOTS, 3 * HD), BF16),
            pltpu.VMEM((HEADS, WIDE_SLOTS, 3 * HD), BF16),
            pltpu.VMEM((HEADS, ROWS, 3 * HD), BF16),
            pltpu.VMEM((HEADS, ROWS, HD), F32),
            pltpu.VMEM((HEADS, ROWS, HD), F32),
            pltpu.VMEM((128, WIDE_SLOTS), BF16),
            pltpu.VMEM((8, ROWS), I32),
            pltpu.VMEM((ROWS, 128), I32),
            pltpu.VMEM((HEADS, 8, WIDE_SLOTS), I32),
            pltpu.VMEM((HEADS, WIDE_SLOTS, 128), I32),
            dma((HEADS, 4)),
            dma((HEADS, 3)),
            dma, dma, dma, dma,
            dma((HEADS,)), dma((HEADS,)), dma((HEADS,)), dma((HEADS,)),
            dma((HEADS,)), dma((HEADS,)), dma((HEADS,)), dma((HEADS,)),
        ],
        compiler_params=pltpu.CompilerParams(
            collective_id=1, has_side_effects=True, vmem_limit_bytes=60 * 1024 * 1024
        ),
    )(*args)


def hand_over(*refs):
    held, in_sem, out_sem = refs[6:]
    pieces = [(t, p) for p in range(4) for t in range(3)]

    def move(t, p, inward):
        part = pl.ds(p * (ROWS // 4), ROWS // 4)
        if inward:
            return pltpu.make_async_copy(refs[t].at[part], held.at[t, part], in_sem.at[t, p])
        return pltpu.make_async_copy(held.at[t, part], refs[t + 3].at[part], out_sem.at[t, p])

    for t, p in pieces:
        move(t, p, True).start()
    for t, p in pieces:
        move(t, p, True).wait()
        move(t, p, False).start()
    for t, p in pieces:
        move(t, p, False).wait()


def call_hand_over(grads):
    hbm = pl.BlockSpec(memory_space=pl.ANY)
    grad = jax.ShapeDtypeStruct((ROWS, HEADS * HD), BF16)
    return pl.pallas_call(
        hand_over, out_shape=(grad, grad, grad), in_specs=[hbm] * 3, out_specs=(hbm, hbm, hbm),
        scratch_shapes=[
            pltpu.VMEM((3, ROWS, HEADS * HD), BF16),
            pltpu.SemaphoreType.DMA((3, 4)),
            pltpu.SemaphoreType.DMA((3, 4)),
        ],
    )(*grads)


def local(cluster_id, queries, key_vectors, value_vectors, grad_output):
    args = (cluster_id.reshape(1, 128), queries, key_vectors, value_vectors, grad_output)
    dq, dk, dv, flag = call_kernel(args)
    grads = lax.cond(
        flag[0, 0] > 0.5, lambda given, done: call_wide(given), lambda given, done: done,
        args, (dq, dk, dv),
    )
    return call_hand_over(grads)


def solution(mesh):
    placed = (P(("seq", "head")),) + (P("seq", "head"),) * 4
    return jax.shard_map(
        local,
        mesh=mesh,
        in_specs=placed,
        out_specs=(P("seq", "head"),) * 3,
        check_vma=False,
    )
```
